32 devices in a mesh: section: 2 (over x), dp: 4 (over y, core), tensor: 4 (over z).
Axes of the slice: x: 2, y: 2, z: 4, core: 2. Of those that a mesh axis runs over, the one named last changes fastest.
Arguments:
- inputs: bfloat16 [2, 8, 1024, 512], P('section', 'dp', 'tensor'), may hold values from -6 to 6
- cotangent: bfloat16 [2, 8, 1024, 512], P('section', 'dp', 'tensor'), may hold values from -6 to 6
- lengths: int32 [2, 8, 8], P(None, 'dp'), may hold values from 0 to 1024, as said below
- row_flags: int32 [8], P('dp'), may hold values from 0 to 1, as said below
- qkv_w: bfloat16 [2, 3, 512, 512], P('section', None, None, 'tensor'), may hold values from -0.25 to 0.25
- out_w: bfloat16 [2, 512, 512], P('section', 'tensor'), may hold values from -0.75 to 0.75
- cross_w: bfloat16 [2, 2, 512, 512], P('section', None, None, 'tensor'), may hold values from -0.375 to 0.375
- up_w: bfloat16 [2, 512, 2048], P('section', None, 'tensor'), may hold values from -0.25 to 0.25
- down_w: bfloat16 [2, 2048, 512], P('section', 'tensor'), may hold values from -0.125 to 0.125
- norm_gain: float32 [2, 2, 512], replicated, may hold values from 0.5 to 1.5
- norm_bias: float32 [2, 2, 512], replicated, may hold values from -1.5 to 1.5
- cross_gain: float32 [512], replicated, may hold values from 0.5 to 1.5
- cross_bias: float32 [512], replicated, may hold values from -1.5 to 1.5
Outputs:
- outputs: bfloat16 [2, 8, 1024, 512], P('section', 'dp', 'tensor')
- input_grad: float32 [2, 8, 1024, 512], P('section', 'dp', 'tensor')
- qkv_grad: float32 [2, 3, 512, 512], P('section', None, None, 'tensor')
- out_grad: float32 [2, 512, 512], P('section', 'tensor')
- cross_grad: float32 [2, 2, 512, 512], P('section', None, None, 'tensor')
- up_grad: float32 [2, 512, 2048], P('section', None, 'tensor')
- down_grad: float32 [2, 2048, 512], P('section', 'tensor')
- norm_gain_grad: float32 [2, 2, 512], replicated
- norm_bias_grad: float32 [2, 2, 512], replicated
- cross_gain_grad: float32 [512], replicated
- cross_bias_grad: float32 [512], replicated
The draws below stay inside these ranges and needn't reach their ends.
Inputs may be any that keep to these rules, and one draw needn't show every extreme that they name: `lengths`: for a row with flag 1, entry 0 of each side is the length of its one pair and later entries are 0; for a row with flag 0, entry j is the length of the pair in slot j of 128 positions, 1 to 128. In each aligned block of 2 rows, one row has flag 1 and length 1024 on both sides. `row_flags`: in each aligned block of 2 rows, one or more rows have flag 1.
All inputs are finite; a program needn't handle non-finite values.
Results may differ from the reference program's by a relative error of at most 0.04.
Values may be sent and summed in bfloat16 or wider, within the bound.
No kernel may reach another device: no remote copies, remote signals or barrier semaphores. Data moves between devices by JAX's collectives and lax.ppermute only.
A program may use at most 192 MiB of HBM per device.

```python
import jax
import jax.numpy as jnp
from jax import lax

D = 512
HEADS = 8
HD = 64
FF = 2048
LEN = 1024
SYNTH_SLOT_LEN = 128
MB = 2
SEQ_MB = 1
SYNTH_SLOTS = 8
TOTAL_ROWS = 8


def pair_flags(key):
    flag_key = jax.random.fold_in(key, 11)
    drawn_key, leader_key = jax.random.split(flag_key)
    group_size = MB * SEQ_MB
    drawn = jax.random.randint(drawn_key, (TOTAL_ROWS,), 0, 2)
    leader = jax.random.randint(leader_key, (TOTAL_ROWS // group_size,), 0, group_size)
    row_ids = jnp.arange(TOTAL_ROWS, dtype=jnp.int32)
    leading = row_ids % group_size == jnp.repeat(leader, group_size)
    return (jnp.where(leading, 1, drawn).astype(jnp.int32), leading)


def draw_row_flags(key, part):
    flags_now, leading = pair_flags(key)
    return flags_now


def draw_lengths(key, part):
    flags_now, leading = pair_flags(key)
    key = jax.random.fold_in(key, 5)
    real_key, synthetic_random_key = jax.random.split(key)
    real_len = jax.random.randint(real_key, (2, TOTAL_ROWS), LEN // 4, LEN + 1)
    real_len = jnp.where(leading[None, :], LEN, real_len)
    synthetic_length = jax.random.randint(synthetic_random_key, (2, TOTAL_ROWS, SYNTH_SLOTS), 1, SYNTH_SLOT_LEN + 1)
    first_slot = jnp.where(flags_now[None, :] == 1, real_len, synthetic_length[:, :, 0])
    later_slots = jnp.where(flags_now[None, :, None] == 1, 0, synthetic_length[:, :, 1:])
    return jnp.concatenate([first_slot[:, :, None], later_slots], axis=2).astype(jnp.int32)


def level_of(key, shape, pieces, least, largest):
    loudness = 1.0
    for axis_at, shards_of in pieces:
        heights = jax.random.uniform(jax.random.fold_in(jax.random.fold_in(key, 6), axis_at), (shards_of,), jnp.float32, least / len(pieces), largest / len(pieces))
        loudness = loudness * jnp.repeat(jnp.exp(heights), shape[axis_at] // shards_of).reshape((-1,) + (1,) * (len(shape) - 1 - axis_at))
    return loudness


def noise(own_key, shape, width, bound, pieces=(), held_as=jnp.bfloat16):
    values = jax.random.normal(own_key, shape, jnp.float32) * width
    if len(pieces) > 0:
        values = level_of(own_key, shape, pieces, -0.22, 0.18) * values
    return jnp.clip(values, min=-bound, max=bound).astype(held_as)


def setup_inputs(seed: int = 0) -> dict:
    keys = jax.random.split(jax.random.key(seed), 14)
    inputs = noise(keys[0], (2, TOTAL_ROWS, LEN, D), 1.0, 6.0, ((0, 2), (1, 4), (2, 4)))
    cotangent = noise(keys[1], (2, TOTAL_ROWS, LEN, D), 1.0, 6.0, ((0, 2), (1, 4), (2, 4)))
    lengths = draw_lengths(jax.random.fold_in(keys[13], 71), 0)
    row_flags = draw_row_flags(jax.random.fold_in(keys[13], 71), 0)
    qkv_w = noise(keys[4], (2, 3, D, D), D ** -0.5, 0.25, ((0, 2), (3, 4)))
    out_w = noise(keys[5], (2, D, D), HD ** -0.5, 0.75, ((0, 2), (1, 4)))
    cross_w = noise(keys[6], (2, 2, D, D), (D // 2) ** -0.5, 0.375, ((0, 2), (3, 4)))
    up_w = noise(keys[7], (2, D, FF), D ** -0.5, 0.25, ((0, 2), (2, 4)))
    down_w = noise(keys[8], (2, FF, D), FF ** -0.5, 0.125, ((0, 2), (1, 4)))
    norm_gain = jnp.clip(1.0 + 0.1 * jax.random.normal(keys[9], (2, 2, D), jnp.float32), 0.5, 1.5)
    norm_bias = noise(keys[10], (2, 2, D), 0.3, 1.5, (), jnp.float32)
    cross_gain = jnp.clip(1.0 + 0.1 * jax.random.normal(keys[11], (D,), jnp.float32), 0.5, 1.5)
    cross_bias = noise(keys[12], (D,), 0.3, 1.5, (), jnp.float32)
    return dict(inputs=inputs, cotangent=cotangent, lengths=lengths, row_flags=row_flags, qkv_w=qkv_w, out_w=out_w, cross_w=cross_w, up_w=up_w, down_w=down_w, norm_gain=norm_gain, norm_bias=norm_bias, cross_gain=cross_gain, cross_bias=cross_bias)


NEG = -1e+30
EPS = 1e-05

@jax.custom_vjp
def low(v):
    return lax.optimization_barrier(v.astype(jnp.bfloat16)).astype(jnp.float32)

@jax.custom_vjp
def low_back(v):
    return v

def low_keep(v):
    return (low(v), None)

def low_pass(kept, grad):
    return (grad,)

def back_keep(v):
    return (v, None)

def back_low(kept, grad):
    return (low(grad),)
low.defvjp(low_keep, low_pass)
low_back.defvjp(back_keep, back_low)

def matmul(left, right):
    return jnp.dot(left, right, precision=lax.Precision.HIGHEST)

def layer_norm(resid, gain, bias_vec):
    mean_removed = resid - lax.optimization_barrier(jnp.mean(resid, axis=-1, keepdims=True))
    inverse = lax.rsqrt(lax.optimization_barrier(jnp.mean(mean_removed * mean_removed, axis=-1, keepdims=True)) + EPS)
    return mean_removed * inverse * gain + bias_vec

def row_info(lens, row_flag):
    positions = jnp.arange(LEN, dtype=jnp.int32)
    slot_size = jnp.where(row_flag == 1, LEN, SYNTH_SLOT_LEN).astype(jnp.int32)
    segment = positions // slot_size
    offset = positions - segment * slot_size
    slot_index_list = jnp.arange(SYNTH_SLOTS, dtype=jnp.int32)
    seg_len = lax.optimization_barrier(jnp.sum(jnp.where(segment[:, None] == slot_index_list[None, :], lens[None, :], 0), axis=1))
    return (segment, offset < seg_len)

def attend(q_rows, k_rows, v_rows, key_mask):
    q_heads = q_rows.reshape(LEN, HEADS, HD)
    k_heads = k_rows.reshape(LEN, HEADS, HD)
    v_heads = v_rows.reshape(LEN, HEADS, HD)
    scores = jnp.einsum('qhd,khd->hqk', q_heads, k_heads, precision=lax.Precision.HIGHEST) * HD ** (-0.5)
    scores = low_back(scores)
    scores = jnp.where(key_mask[None], scores, NEG)
    top_score = lax.optimization_barrier(jnp.max(scores, axis=-1, keepdims=True))
    expo = jnp.exp(scores - top_score)
    attn_prob = expo / lax.optimization_barrier(jnp.sum(expo, axis=-1, keepdims=True))
    result = jnp.einsum('hqk,khd->qhd', low(attn_prob), v_heads, precision=lax.Precision.HIGHEST)
    return result.reshape(LEN, HEADS * HD)

def self_layer(rows_in, w_qkv, w_out, gain, bias_vec, key_mask):
    rows_low = low(rows_in)
    q_rows = low(low_back(matmul(rows_low, w_qkv[0])))
    k_rows = low(low_back(matmul(rows_low, w_qkv[1])))
    v_rows = low(low_back(matmul(rows_low, w_qkv[2])))
    attended = low(low_back(attend(q_rows, k_rows, v_rows, key_mask)))
    branch = low_back(matmul(attended, w_out))
    return layer_norm(rows_in + branch, gain, bias_vec)

def ffn_layer(rows_in, w_up, w_down, gain, bias_vec):
    rows_low = low(rows_in)
    hidden = low_back(matmul(rows_low, w_up))
    activ = low(jax.nn.silu(hidden))
    branch = low_back(matmul(activ, w_down))
    return layer_norm(rows_in + branch, gain, bias_vec)

def one_row(params, src_rows, tgt_rows, src_len, tgt_len, row_flag):
    qkv_w, out_w, cross_w, up_w, down_w, norm_gain, norm_bias, cross_gain, cross_bias = params
    src_seg, src_valid = row_info(src_len, row_flag)
    tgt_seg, tgt_valid = row_info(tgt_len, row_flag)
    positions = jnp.arange(LEN, dtype=jnp.int32)
    enc_mask = (src_seg[:, None] == src_seg[None, :]) & src_valid[None, :]
    dec_mask = (tgt_seg[:, None] == tgt_seg[None, :]) & tgt_valid[None, :] & (positions[None, :] <= positions[:, None])
    cross_mask = (tgt_seg[:, None] == src_seg[None, :]) & src_valid[None, :]
    enc_mid = self_layer(src_rows, qkv_w[0], out_w[0], norm_gain[0, 0], norm_bias[0, 0], enc_mask)
    memory = ffn_layer(enc_mid, up_w[0], down_w[0], norm_gain[0, 1], norm_bias[0, 1])
    dec_mid = self_layer(tgt_rows, qkv_w[1], out_w[1], norm_gain[1, 0], norm_bias[1, 0], dec_mask)
    mem_low = low(memory)
    cross_k = low(low_back(matmul(mem_low, cross_w[0, 0])))
    cross_v = low(low_back(matmul(mem_low, cross_w[0, 1])))
    cross_q = low(low_back(matmul(low(dec_mid), cross_w[1, 0])))
    cross_att = low(low_back(attend(cross_q, cross_k, cross_v, cross_mask)))
    cross_branch = low_back(matmul(cross_att, cross_w[1, 1].T))
    dec_cross = layer_norm(dec_mid + cross_branch, cross_gain, cross_bias)
    final = ffn_layer(dec_cross, up_w[1], down_w[1], norm_gain[1, 1], norm_bias[1, 1])
    return (memory, final)

def reference(inputs, cotangent, lengths, row_flags, qkv_w, out_w, cross_w, up_w, down_w, norm_gain, norm_bias, cross_gain, cross_bias):
    floats = tuple((arr.astype(jnp.float32) for arr in (qkv_w, out_w, cross_w, up_w, down_w, norm_gain, norm_bias, cross_gain, cross_bias)))
    source = inputs.astype(jnp.float32)

    def forward(params, rows_all):

        def scan_step(carry, item):
            mem_row, fin_row = jax.checkpoint(one_row)(params, *item)
            return (carry, (mem_row, fin_row))
        _, (memory, final) = lax.scan(scan_step, jnp.zeros((), jnp.float32), (rows_all[0], rows_all[1], lengths[0], lengths[1], row_flags))
        return jnp.stack([memory, final])
    results, pullback = jax.vjp(forward, floats, source)
    gradients, input_grad = pullback(cotangent.astype(jnp.float32))
    return (results.astype(jnp.bfloat16), input_grad, gradients[0], gradients[1], gradients[2], gradients[3], gradients[4], gradients[5], gradients[6], gradients[7], gradients[8])
```

```python
import functools

import jax
import jax.numpy as jnp
from jax import lax
from jax.experimental import pallas as pl
from jax.experimental.pallas import tpu as pltpu
from jax.sharding import PartitionSpec as P

HEADS = 8
HD = 64
PAIR = 2 * HD
SLOT_BITS = 7
SLOTS = 8
NEG = -1e30
EPS = 1e-05
SCALE = HD ** -0.5
BF = jnp.bfloat16
F32 = jnp.float32
MIB = 1024 * 1024


def swap_dp(x, bit):
    n = lax.axis_size("dp")
    return lax.ppermute(x, "dp", [(i, i ^ bit) for i in range(n)])


def shift_tensor(x, step):
    n = lax.axis_size("tensor")
    return lax.ppermute(x, "tensor", [(i, (i + step) % n) for i in range(n)])


def swap_tensor(x, bit):
    n = lax.axis_size("tensor")
    return lax.ppermute(x, "tensor", [(i, i ^ bit) for i in range(n)])


def to_decoder(x):
    return lax.ppermute(x, "section", [(0, 1)])


def to_encoder(x):
    return lax.ppermute(x, "section", [(1, 0)])


def deal_route(k):
    n_t = lax.axis_size("tensor")
    route = []
    for d in range(lax.axis_size("dp")):
        group, core = divmod(d, 2)
        for t in range(n_t):
            plane = 2 * core + (t + k) % 2
            route.append((d * n_t + t, (2 * group + t // 2) * n_t + plane))
    return route


def deal(x, k):
    return lax.ppermute(x, ("dp", "tensor"), deal_route(k))


def deal_back(x, k):
    return lax.ppermute(x, ("dp", "tensor"), [(b, a) for a, b in deal_route(k)])


def gather_pieces(piece):
    along_z = jnp.stack([piece] + [shift_tensor(piece, r) for r in range(1, 4)])
    along_y = swap_dp(along_z, 2)
    return (along_z, swap_dp(along_z, 1), along_y, swap_dp(along_y, 1))


def reduce_pieces(keep, send):
    halves = (keep.astype(F32) + swap_dp(send, 1).astype(F32)).astype(BF)
    quarter = (halves[0].astype(F32) + swap_dp(halves[1], 2).astype(F32)).astype(BF)
    total = quarter[0].astype(F32)
    for r in range(1, 4):
        total = total + shift_tensor(quarter[r], -r).astype(F32)
    bit = 4
    while bit < lax.axis_size("dp"):
        total = total + swap_dp(total.astype(BF), bit).astype(F32)
        bit *= 2
    return total.astype(BF)


def spread_pieces(piece):
    along_y = jnp.stack([piece, swap_dp(piece, 2)])
    mate = swap_dp(along_y, 1)
    return jnp.stack([along_y[0], mate[0], along_y[1], mate[1]])


def dg(a, b, ca, cb):
    return lax.dot_general(a, b, (((ca,), (cb,)), ((), ())), preferred_element_type=F32)


def norm_fwd(r):
    off = r - jnp.mean(r, axis=-1, keepdims=True)
    inv = lax.rsqrt(jnp.mean(off * off, axis=-1, keepdims=True) + EPS)
    return off * inv, inv


def norm_bwd(dy, n, inv, gain):
    sc = dy * gain
    dr = inv * (
        sc
        - jnp.mean(sc, axis=-1, keepdims=True)
        - n * jnp.mean(sc * n, axis=-1, keepdims=True)
    )
    return dr, jnp.sum(dy * n, axis=0, keepdims=True), jnp.sum(dy, axis=0, keepdims=True)


def head_lanes(h):
    return (lax.broadcasted_iota(jnp.int32, (1, PAIR), 1) // HD) == h


def mask_bias(info, n_q, n_k, q_axis):
    flip = info[9]
    q_shape = (n_q, 1) if q_axis == 0 else (1, n_q)
    full = (n_q, n_k) if q_axis == 0 else (n_k, n_q)
    q_pos = lax.broadcasted_iota(jnp.int32, q_shape, q_axis) ^ flip
    seg = jnp.where(info[8] == 1, 0, q_pos >> SLOT_BITS)
    size = jnp.zeros(q_shape, jnp.int32)
    for j in range(SLOTS):
        size = size + jnp.where(seg == j, info[j], 0)
    first = seg << SLOT_BITS
    end = first + size
    end = jnp.where(info[10] == 1, jnp.minimum(end, q_pos + 1), end)
    k_pos = lax.broadcasted_iota(jnp.int32, full, 1 - q_axis) ^ flip
    return jnp.where((k_pos >= first) & (k_pos < end), 0.0, NEG)


def weights_in_order(refs, wall):
    for rel, ref in enumerate(refs):
        for z in range(ref.shape[0]):
            wall[rel, :, z * PAIR : (z + 1) * PAIR] = ref[z]


def attend_forward(q_ref, k_ref, v_ref, bias_ref, att_ref, lse_ref):
    n_q = q_ref.shape[0]

    def pair(hp, _):
        sl = pl.ds(pl.multiple_of(hp * PAIR, PAIR), PAIR)
        kp = k_ref[:, sl]
        vp = v_ref[:, sl]
        qp = q_ref[:, sl]
        out = None
        for h in range(2):
            lanes = head_lanes(h)
            s = dg(jnp.where(lanes, qp, jnp.zeros_like(qp)), kp, 1, 1) + bias_ref[...]
            top = jnp.max(s, axis=1, keepdims=True)
            e = jnp.exp(s - top)
            total = jnp.sum(e, axis=1, keepdims=True)
            o = dg(e.astype(BF), vp, 1, 0) * (1.0 / total)
            lse = jnp.broadcast_to(top + jnp.log(total), (n_q, 8))
            lse_ref[hp * 2 + h] = jnp.transpose(lse)[0:1, :]
            o = jnp.where(lanes, o, 0.0)
            out = o if out is None else out + o
        att_ref[:, sl] = out.astype(BF)
        return 0

    lax.fori_loop(0, HEADS // 2, pair, 0)


def attend_backward(info, q_ref, k_ref, v_ref, do_ref, att_ref, lse_ref, bias_ref, rd_ref, dq_ref, dk_ref, dv_ref):
    n_q = q_ref.shape[0]
    width = q_ref.shape[1]
    block = 256
    empty = info[0]
    for j in range(1, SLOTS):
        empty = empty + info[j]
    empty = empty == 0
    p_fix = jnp.where(empty, 1.0 / k_ref.shape[0], 1.0)
    s_fix = jnp.where(empty, 0.0, 1.0)
    prod = do_ref[...].astype(F32) * att_ref[...].astype(F32)
    high = prod.astype(BF)
    low = (prod - high.astype(F32)).astype(BF)
    heads = lax.broadcasted_iota(jnp.int32, (HEADS, width), 0)
    lanes_of = lax.broadcasted_iota(jnp.int32, (HEADS, width), 1) // HD
    ones = jnp.where(heads == lanes_of, 1.0, 0.0).astype(BF)
    rd = dg(ones, high, 1, 1) + dg(ones, low, 1, 1)
    for h in range(HEADS):
        rd_ref[h] = rd[h : h + 1]

    def pair(hp, _):
        sl = pl.ds(pl.multiple_of(hp * PAIR, PAIR), PAIR)
        kp = k_ref[:, sl]
        vp = v_ref[:, sl]
        k_t = jnp.transpose(kp)
        dk = dv = None
        for qi in range(n_q // block):
            qs = slice(qi * block, (qi + 1) * block)
            qp = q_ref[qs, sl]
            dop = do_ref[qs, sl]
            dqs = []
            for h in range(2):
                lanes = head_lanes(h)
                qm = jnp.where(lanes, qp, jnp.zeros_like(qp))
                dom = jnp.where(lanes, dop, jnp.zeros_like(dop))
                s = dg(kp, qm, 1, 1) + bias_ref[:, qs]
                p = jnp.exp(s - lse_ref[hp * 2 + h, :, qs])
                dp = dg(vp, dom, 1, 1)
                ds = (p * (dp - rd_ref[hp * 2 + h, :, qs])).astype(BF)
                a = dg(p.astype(BF), dom, 1, 0)
                dv = a if dv is None else dv + a
                a = dg(ds, qm, 1, 0)
                dk = a if dk is None else dk + a
                dqs.append(dg(k_t[h * HD : (h + 1) * HD], ds, 1, 0))
            dq = jnp.transpose(jnp.concatenate(dqs, axis=0))
            dq_ref[qs, sl] = (dq * (SCALE * s_fix)).astype(BF)
        dk_ref[:, sl] = (dk * s_fix).astype(BF)
        dv_ref[:, sl] = (dv * p_fix).astype(BF)
        return 0

    lax.fori_loop(0, HEADS // 2, pair, 0)


def attention_kernel(n_src, info, *refs):
    xq = refs[:n_src[0]]
    xk = refs[n_src[0] : n_src[0] + n_src[1]]
    refs = refs[n_src[0] + n_src[1] :]
    w_refs = refs[:4]
    gain, shift = refs[4:6]
    y_ref, n_ref, inv_ref, q_ref, k_ref, v_ref, att_ref, lse_ref = refs[6:14]
    wall, bias_ref = refs[14:16]
    weights_in_order(w_refs, wall)
    me = info[11]
    bias_ref[...] = mask_bias(info, q_ref.shape[0], k_ref.shape[0], 0)
    rows = xq[0][...] if len(xq) == 1 else jnp.concatenate([r[...] for r in xq], axis=0)
    rows_low = rows.astype(BF)
    q = dg(rows_low, wall[me], 1, 0).astype(BF)
    q_ref[...] = q * jnp.asarray(SCALE, BF)
    wk = wall[me ^ 1]
    wv = wall[me ^ 2]
    at = 0
    for ref in xk:
        part = ref[...]
        k_ref[at : at + ref.shape[0]] = dg(part, wk, 1, 0).astype(BF)
        v_ref[at : at + ref.shape[0]] = dg(part, wv, 1, 0).astype(BF)
        at += ref.shape[0]
    attend_forward(q_ref, k_ref, v_ref, bias_ref, att_ref, lse_ref)
    branch = dg(att_ref[...], wall[me ^ 3], 1, 1)
    n, inv = norm_fwd(rows.astype(F32) + branch)
    n_ref[...] = n
    inv_ref[...] = inv
    y_ref[...] = n * gain[...] + shift[...]


def silu_parts(u):
    sg = jax.nn.sigmoid(u)
    return u * sg, sg


def ffn_forward_kernel(x_ref, *refs):
    ups = refs[:4]
    downs = refs[4:8]
    gain, shift, y_ref, low_ref, n_ref, inv_ref = refs[8:]
    x = x_ref[...]
    low = x.astype(BF)
    acc = x
    for up, down in zip(ups, downs):
        n_z, width, feat = up.shape
        for z in range(0, n_z, 2):
            u = dg(low, up[z : z + 2].reshape(2 * width, feat), 1, 1)
            act = silu_parts(u)[0].astype(BF)
            acc = acc + dg(act, down[z : z + 2].reshape(2 * width, feat), 1, 0)
    n, inv = norm_fwd(acc)
    y = n * gain[...] + shift[...]
    y_ref[...] = y
    low_ref[...] = y.astype(BF)
    n_ref[...] = n
    inv_ref[...] = inv


def ffn_both_kernel(x_ref, cot_ref, *refs):
    ups = refs[:4]
    downs = refs[4:8]
    gain, shift, final_ref, n_ref, inv_ref, dx_ref, u_ref = refs[8:]
    x = x_ref[...]
    low = x.astype(BF)
    acc = x
    at = 0
    for up, down in zip(ups, downs):
        n_z, width, feat = up.shape
        for z in range(0, n_z, 2):
            u = dg(low, up[z : z + 2].reshape(2 * width, feat), 1, 1)
            u_ref[:, at : at + 2 * width] = u
            at += 2 * width
            act = silu_parts(u)[0].astype(BF)
            acc = acc + dg(act, down[z : z + 2].reshape(2 * width, feat), 1, 0)
    n, inv = norm_fwd(acc)
    final_ref[...] = (n * gain[...] + shift[...]).astype(BF)
    n_ref[...] = n
    inv_ref[...] = inv
    dr, _, _ = norm_bwd(cot_ref[...].astype(F32), n, inv, gain[...])
    dbr = dr.astype(BF)
    acc = dr
    at = 0
    for up, down in zip(ups, downs):
        n_z, width, feat = up.shape
        for z in range(0, n_z, 2):
            u = u_ref[:, at : at + 2 * width]
            at += 2 * width
            sg = jax.nn.sigmoid(u)
            dact = dg(dbr, down[z : z + 2].reshape(2 * width, feat), 1, 1)
            du = (dact * sg * (1.0 + u * (1.0 - sg))).astype(BF)
            acc = acc + dg(du, up[z : z + 2].reshape(2 * width, feat), 1, 0)
    dx_ref[...] = acc


def cross_backward_kernel(info, dy_ref, n_ref, inv_ref, gain, q_ref, k_ref, v_ref, att_ref, lse_ref, w0, w1, w2, w3,
                          dh_ref, dmem_own_ref, dmem_mate_ref, dbr_ref, dq_ref, dk_ref, dv_ref, dnorm_ref,
                          wall, bias_ref, rd_ref, do_ref):
    weights_in_order((w0, w1, w2, w3), wall)
    me = info[11]
    bias_ref[...] = mask_bias(info, q_ref.shape[0], k_ref.shape[0], 1)
    dr, dg_sum, db_sum = norm_bwd(dy_ref[...], n_ref[...], inv_ref[...], gain[...])
    dnorm_ref[0:1] = dg_sum
    dnorm_ref[1:2] = db_sum
    dbr = dr.astype(BF)
    dbr_ref[...] = dbr
    do_ref[...] = dg(dbr, wall[me ^ 3], 1, 0).astype(BF)
    attend_backward(info, q_ref, k_ref, v_ref, do_ref, att_ref, lse_ref, bias_ref, rd_ref, dq_ref, dk_ref, dv_ref)
    dh_ref[...] = dr + dg(dq_ref[...], wall[me], 1, 1)
    half = dmem_own_ref.shape[0]
    wk = wall[me ^ 1]
    wv = wall[me ^ 2]
    for ref, at in ((dmem_own_ref, 0), (dmem_mate_ref, half)):
        part = dg(dk_ref[at : at + half], wk, 1, 1) + dg(dv_ref[at : at + half], wv, 1, 1)
        ref[...] = part.astype(BF)


def put_matrix(keep_ref, send_ref, me, which, value):
    slot = me ^ which
    y = slot >> 1

    @pl.when(slot % 2 == 0)
    def _():
        for z in range(4):
            keep_ref[y, z] = value[:, z * PAIR : (z + 1) * PAIR]

    @pl.when(slot % 2 == 1)
    def _():
        for z in range(4):
            send_ref[y, z] = value[:, z * PAIR : (z + 1) * PAIR]


def cross_weights_kernel(info, h_ref, mem_own, mem_mate, att_ref, dbr_ref, dq_ref, dk_ref, dv_ref, keep_ref, send_ref):
    me = info[11]
    half = mem_own.shape[0]
    put_matrix(keep_ref, send_ref, me, 0, dg(h_ref[...].astype(BF), dq_ref[...], 0, 0).astype(BF))
    for which, ref in ((1, dk_ref), (2, dv_ref)):
        value = dg(mem_own[...], ref[:half], 0, 0) + dg(mem_mate[...], ref[half:], 0, 0)
        put_matrix(keep_ref, send_ref, me, which, value.astype(BF))
    put_matrix(keep_ref, send_ref, me, 3, dg(dbr_ref[...], att_ref[...], 0, 0).astype(BF))


def ffn_backward_kernel(info, x_ref, n3_ref, inv3_ref, dy_ref, gain3, dmid_ref, n1_ref, inv1_ref, gain1, *refs):
    ups = refs[:4]
    downs = refs[4:8]
    outs = refs[8:12]
    att_g = refs[12]
    keep_ref, send_ref, dr1_ref, dbr1_ref, dnorm_ref = refs[13:18]
    wall = refs[18]
    do_ref = att_g
    weights_in_order(outs, wall)
    me = info[11]
    low = x_ref[...].astype(BF)
    dr3, dg3, db3 = norm_bwd(dy_ref[...], n3_ref[...], inv3_ref[...], gain3[...])
    dbr = dr3.astype(BF)
    acc = dr3
    for rel in range(4):
        up = ups[rel]
        down = downs[rel]
        target = (keep_ref, send_ref)[rel % 2]
        n_z, width, feat = up.shape
        for z in range(0, n_z, 2):
            wu = up[z : z + 2].reshape(2 * width, feat)
            wd = down[z : z + 2].reshape(2 * width, feat)
            u_t = dg(wu, low, 1, 1)
            act_t, sg = silu_parts(u_t)
            act_t = act_t.astype(BF)
            dact_t = dg(wd, dbr, 1, 1)
            du_t = (dact_t * sg * (1.0 + u_t * (1.0 - sg))).astype(BF)
            acc = acc + dg(du_t, wu, 0, 0)
            dup = dg(du_t, low, 1, 0).astype(BF)
            ddown = dg(act_t, dbr, 1, 0).astype(BF)
            for i in range(2):
                target[rel // 2, z + i, 0] = dup[i * width : (i + 1) * width]
                target[rel // 2, z + i, 1] = ddown[i * width : (i + 1) * width]
    dmid = jnp.where(info[12] == 1, dmid_ref[...], acc)
    dr1, dg1, db1 = norm_bwd(dmid, n1_ref[...], inv1_ref[...], gain1[...])
    dr1_ref[...] = dr1
    dbr1 = dr1.astype(BF)
    dbr1_ref[...] = dbr1
    do_ref[...] = dg(dbr1, wall[me ^ 3], 1, 0).astype(BF)
    for i, row in enumerate((dg1, dg3, db1, db3)):
        dnorm_ref[i : i + 1] = row


def self_backward_kernel(info, q_ref, k_ref, v_ref, do_ref, att_ref, lse_ref, dq_ref, dk_own, dk_mate, bias_ref, rd_ref, dk_ref, dv_ref):
    bias_ref[...] = mask_bias(info, q_ref.shape[0], k_ref.shape[0], 1)
    attend_backward(info, q_ref, k_ref, v_ref, do_ref, att_ref, lse_ref, bias_ref, rd_ref, dq_ref, dk_ref, dv_ref)
    half = q_ref.shape[0]
    dk_own[0] = dk_ref[:half]
    dk_own[1] = dv_ref[:half]
    dk_mate[0] = dk_ref[half:]
    dk_mate[1] = dv_ref[half:]


def input_backward_kernel(info, x0, x1, dr_ref, dq_ref, own_ref, got_ref, att_ref, dbr_ref, w0, w1, w2, w3,
                          dx_ref, keep_ref, send_ref, wall):
    weights_in_order((w0, w1, w2, w3), wall)
    me = info[11]
    dq = dq_ref[...]
    dk = (own_ref[0].astype(F32) + got_ref[0].astype(F32)).astype(BF)
    dv = (own_ref[1].astype(F32) + got_ref[1].astype(F32)).astype(BF)
    dx = dr_ref[...] + dg(dq, wall[me], 1, 1) + dg(dk, wall[me ^ 1], 1, 1) + dg(dv, wall[me ^ 2], 1, 1)
    dx_ref[...] = dx.astype(BF)
    x = jnp.concatenate([x0[...], x1[...]], axis=0)
    for which, value in ((0, dq), (1, dk), (2, dv)):
        put_matrix(keep_ref, send_ref, me, which, dg(x, value, 0, 0).astype(BF))
    put_matrix(keep_ref, send_ref, me, 3, dg(dbr_ref[...], att_ref[...], 0, 0).astype(BF))


def call(kernel, outs, args, scratch=(), flops=0, vmem=44):
    specs = [
        pl.BlockSpec(memory_space=pltpu.SMEM if a.dtype == jnp.int32 else pltpu.VMEM) for a in args
    ]
    size = sum(a.size * a.dtype.itemsize for a in args)
    size += sum(int(jnp.dtype(dt).itemsize) * functools.reduce(lambda p, q: p * q, shape, 1) for shape, dt in outs)
    return pl.pallas_call(
        kernel,
        out_shape=tuple(jax.ShapeDtypeStruct(shape, dt) for shape, dt in outs),
        in_specs=specs,
        out_specs=tuple(pl.BlockSpec(memory_space=pltpu.VMEM) for _ in outs),
        scratch_shapes=list(scratch),
        compiler_params=pltpu.CompilerParams(vmem_limit_bytes=vmem * MIB),
        cost_estimate=pl.CostEstimate(flops=int(flops), bytes_accessed=int(size), transcendentals=0),
    )(*args)


def body(
    inputs,
    cotangent,
    lengths,
    row_flags,
    qkv_w,
    out_w,
    cross_w,
    up_w,
    down_w,
    norm_gain,
    norm_bias,
    cross_gain,
    cross_bias,
):
    section = lax.axis_index("section")
    is_dec = section == 1
    d = lax.axis_index("dp")
    t = lax.axis_index("tensor")
    core = d % 2
    me = d % 4
    feat = inputs.shape[3]
    chunk = inputs.shape[2]
    half = 2 * chunk
    row_len = 2 * half
    quarter = qkv_w.shape[3]
    n_t = 4

    got = [deal(lax.dynamic_index_in_dim(inputs[0], (t + k) % 2, 0, False), k) for k in range(2)]
    mate = [swap_dp(g, 1) for g in got]

    stack = jnp.concatenate([qkv_w[0], out_w[0].T[None]], axis=0)
    attn_ws = gather_pieces(lax.dynamic_index_in_dim(stack, me, 0, False))
    unit_quarter = up_w.shape[2] // 4
    up_piece = lax.dynamic_slice_in_dim(up_w[0], me * unit_quarter, unit_quarter, 1).T
    down_piece = lax.dynamic_slice_in_dim(down_w[0], me * unit_quarter, unit_quarter, 0)
    up_ws = gather_pieces(up_piece)
    down_ws = gather_pieces(down_piece)
    from_enc = to_decoder(jnp.where(me == 1, cross_w[0, 0], cross_w[0, 1]))
    cross_piece = jnp.where(me == 0, cross_w[0, 0], jnp.where(me == 3, cross_w[0, 1], from_enc))
    cross_ws = gather_pieces(cross_piece)

    own_info = jnp.concatenate(
        [lengths[0], lengths[1], row_flags[:, None], jnp.zeros((2, 7), jnp.int32)], axis=1
    ).astype(F32)
    mate_info = swap_dp(own_info, 1)
    row_info = jnp.where(t // 2 == core, own_info, mate_info)
    row_info = lax.dynamic_index_in_dim(row_info, t % 2, 0, False).astype(jnp.int32)
    flip = core * half + (t % 2) * chunk

    def info_of(lens, causal):
        tail = jnp.stack([row_info[16], flip, causal, me, is_dec.astype(jnp.int32), 0, 0, 0]).astype(jnp.int32)
        return jnp.concatenate([lens, tail])

    src_lens = row_info[0:8]
    tgt_lens = row_info[8:16]
    self_info = info_of(jnp.where(is_dec, tgt_lens, src_lens), is_dec.astype(jnp.int32))
    cross_info = info_of(src_lens, jnp.zeros((), jnp.int32))

    gains = jnp.where(is_dec, norm_gain[1], norm_gain[0])
    shifts = jnp.where(is_dec, norm_bias[1], norm_bias[0])
    gain1, gain3 = gains[0:1], gains[1:2]
    shift1, shift3 = shifts[0:1], shifts[1:2]
    cgain, cshift = cross_gain[None], cross_bias[None]

    f_proj = 2 * half * feat * feat
    f_att = 2 * half * row_len * feat
    f_ffn = 2 * half * feat * up_w.shape[2] * n_t

    rows = (half, feat)
    att_outs = [
        (rows, F32), (rows, F32), ((half, 1), F32), (rows, BF), ((row_len, feat), BF), ((row_len, feat), BF),
        (rows, BF), ((HEADS, 1, half), F32),
    ]
    wall = pltpu.VMEM((4, feat, feat), BF)
    bias_n = pltpu.VMEM((half, row_len), F32)
    bias_t = pltpu.VMEM((row_len, half), F32)
    rd_s = pltpu.VMEM((HEADS, 1, half), F32)

    def attention(info, xq, xk, ws, gain, shift):
        return call(
            functools.partial(attention_kernel, (len(xq), len(xk))), att_outs,
            [info, *xq, *xk, *ws, gain, shift], [wall, bias_n], flops=6 * f_proj + 4 * f_att,
        )

    mid, n1, inv1, q1, k1, v1, att1, lse1 = attention(self_info, got, got + mate, attn_ws, gain1, shift1)
    mem, mem_low, n3e, inv3e = call(
        ffn_forward_kernel, [(rows, F32), (rows, BF), (rows, F32), ((half, 1), F32)],
        [mid, *up_ws, *down_ws, gain3, shift3], flops=2 * f_ffn,
    )

    mem_own = to_decoder(mem_low)
    mem_mate = swap_dp(mem_own, 1)

    cot = jnp.concatenate(
        [deal(lax.dynamic_index_in_dim(cotangent[0], (t + k) % 2, 0, False), k) for k in range(2)], axis=0
    )

    h2, n2, inv2, q2, k2, v2, att2, lse2 = attention(cross_info, [mid], [mem_own, mem_mate], cross_ws, cgain, cshift)
    final, n3d, inv3d, dh2 = call(
        ffn_both_kernel, [(rows, BF), (rows, F32), ((half, 1), F32), (rows, F32)],
        [h2, cot, *up_ws, *down_ws, gain3, shift3],
        [pltpu.VMEM((half, up_w.shape[2] * n_t), F32)], flops=4 * f_ffn,
    )
    dh1, dmem_own, dmem_mate, dbr2, dq2, dk2, dv2, dnorm2 = call(
        cross_backward_kernel,
        [(rows, F32), (rows, BF), (rows, BF), (rows, BF), (rows, BF), ((row_len, feat), BF), ((row_len, feat), BF), ((8, feat), F32)],
        [cross_info, dh2, n2, inv2, cgain, q2, k2, v2, att2, lse2, *cross_ws],
        [wall, bias_t, rd_s, pltpu.VMEM(rows, BF)], flops=6 * f_proj + 8 * f_att,
    )
    dmem = (dmem_own.astype(F32) + swap_dp(dmem_mate, 1).astype(F32)).astype(BF)
    dmem_enc = to_encoder(dmem)
    pieces = [((2, n_t, feat, quarter), BF)] * 2
    cross_keep, cross_send = call(
        cross_weights_kernel, pieces, [cross_info, mid, mem_own, mem_mate, att2, dbr2, dq2, dk2, dv2], flops=6 * f_proj,
    )

    ffn_x = jnp.where(is_dec, h2, mid)
    n3 = jnp.where(is_dec, n3d, n3e)
    inv3 = jnp.where(is_dec, inv3d, inv3e)
    dy3 = cot.astype(F32) + dmem_enc.astype(F32)
    ffn_pieces = [((2, n_t, 2, unit_quarter, feat), BF)] * 2
    do1, ffn_keep, ffn_send, dr1, dbr1, dnorm1 = call(
        ffn_backward_kernel,
        [(rows, BF), *ffn_pieces, (rows, F32), (rows, BF), ((8, feat), F32)],
        [self_info, ffn_x, n3, inv3, dy3, gain3, dh1, n1, inv1, gain1, *up_ws, *down_ws, *attn_ws],
        [wall], flops=5 * f_ffn,
    )
    dq1, dkv_own, dkv_mate = call(
        self_backward_kernel, [(rows, BF), ((2, half, feat), BF), ((2, half, feat), BF)],
        [self_info, q1, k1, v1, do1, att1, lse1],
        [bias_t, rd_s, pltpu.VMEM((row_len, feat), BF), pltpu.VMEM((row_len, feat), BF)], flops=8 * f_att,
    )
    dkv_got = swap_dp(dkv_mate, 1)
    dx, self_keep, self_send = call(
        input_backward_kernel, [(rows, BF), *pieces],
        [self_info, *got, dr1, dq1, dkv_own, dkv_got, att1, dbr1, *attn_ws], [wall], flops=7 * f_proj,
    )

    ffn_sum = spread_pieces(reduce_pieces(ffn_keep, ffn_send))
    self_sum = spread_pieces(reduce_pieces(self_keep, self_send))
    cross_sum = reduce_pieces(cross_keep, cross_send)
    cross_sum = jnp.where(is_dec, cross_sum, to_encoder(cross_sum))
    cross_sum = spread_pieces(cross_sum)

    def matrix(stacked, which):
        return lax.dynamic_index_in_dim(stacked, me ^ which, 0, False).astype(F32)

    qkv_grad = jnp.stack([matrix(self_sum, m) for m in range(3)])
    out_grad = matrix(self_sum, 3).T
    cross_grad = jnp.stack([
        matrix(cross_sum, jnp.where(is_dec, 0, 1)), matrix(cross_sum, jnp.where(is_dec, 3, 2))
    ])
    ffn_true = [matrix(ffn_sum, m) for m in range(4)]
    up_grad = jnp.concatenate([f[0].T for f in ffn_true], axis=1)
    down_grad = jnp.concatenate([f[1] for f in ffn_true], axis=0)

    norms = jnp.concatenate([dnorm1[0:4], dnorm2[0:2], jnp.zeros((2, feat), F32)], axis=0)
    bit = 1
    while bit < lax.axis_size("dp"):
        norms = norms + swap_dp(norms, bit)
        bit *= 2
    norms = norms + swap_tensor(norms, 1)
    norms = norms + swap_tensor(norms, 2)
    other = lax.ppermute(norms, "section", [(0, 1), (1, 0)])
    enc = jnp.where(is_dec, other, norms)
    dec = jnp.where(is_dec, norms, other)
    full_gain = jnp.stack([enc[0:2], dec[0:2]])
    full_bias = jnp.stack([enc[2:4], dec[2:4]])

    def rows_back(value):
        back = [deal_back(value[k * chunk : (k + 1) * chunk], k) for k in range(2)]
        even = t % 2 == 0
        return jnp.stack([jnp.where(even, back[0], back[1]), jnp.where(even, back[1], back[0])])

    out_rows = rows_back(jnp.where(is_dec, final, mem_low))
    grad_rows = rows_back(dx).astype(F32)
    return (
        out_rows[None],
        grad_rows[None],
        qkv_grad[None],
        out_grad[None],
        cross_grad[None],
        up_grad[None],
        down_grad[None],
        full_gain,
        full_bias,
        dec[4],
        dec[5],
    )


def solution(mesh):
    return jax.shard_map(
        body,
        mesh=mesh,
        in_specs=(
            P("section", "dp", "tensor", None),
            P("section", "dp", "tensor", None),
            P(None, "dp", None),
            P("dp"),
            P("section", None, None, "tensor"),
            P("section", "tensor", None),
            P("section", None, None, "tensor"),
            P("section", None, "tensor"),
            P("section", "tensor", None),
            P(),
            P(),
            P(),
            P(),
        ),
        out_specs=(
            P("section", "dp", "tensor", None),
            P("section", "dp", "tensor", None),
            P("section", None, None, "tensor"),
            P("section", "tensor", None),
            P("section", None, None, "tensor"),
            P("section", None, "tensor"),
            P("section", "tensor", None),
            P(),
            P(),
            P(),
            P(),
        ),
        check_vma=False,
    )
```

```python
import functools

import jax
import jax.numpy as jnp
from jax import lax
from jax.experimental import pallas as pl
from jax.experimental.pallas import tpu as pltpu
from jax.sharding import PartitionSpec as P

HEADS = 8
HD = 64
PAIR = 2 * HD
SLOT_BITS = 7
SLOTS = 8
NEG = -1e30
EPS = 1e-05
SCALE = HD ** -0.5
BF = jnp.bfloat16
F32 = jnp.float32
MIB = 1024 * 1024


def swap_dp(x, bit):
    n = lax.axis_size("dp")
    return lax.ppermute(x, "dp", [(i, i ^ bit) for i in range(n)])


def shift_tensor(x, step):
    n = lax.axis_size("tensor")
    return lax.ppermute(x, "tensor", [(i, (i + step) % n) for i in range(n)])


def swap_tensor(x, bit):
    n = lax.axis_size("tensor")
    return lax.ppermute(x, "tensor", [(i, i ^ bit) for i in range(n)])


def to_decoder(x):
    return lax.ppermute(x, "section", [(0, 1)])


def to_encoder(x):
    return lax.ppermute(x, "section", [(1, 0)])


def deal_route(k):
    n_t = lax.axis_size("tensor")
    route = []
    for d in range(lax.axis_size("dp")):
        group, core = divmod(d, 2)
        for t in range(n_t):
            plane = 2 * core + (t + k) % 2
            route.append((d * n_t + t, (2 * group + t // 2) * n_t + plane))
    return route


def deal(x, k):
    return lax.ppermute(x, ("dp", "tensor"), deal_route(k))


def deal_back(x, k):
    return lax.ppermute(x, ("dp", "tensor"), [(b, a) for a, b in deal_route(k)])


def after(x, *events):
    return lax.optimization_barrier((x, *events))[0]


def z_pieces(piece):
    return [shift_tensor(piece, r) for r in range(1, 4)]


def y_pieces(along_z):
    zs = jnp.stack(along_z)
    return zs, swap_dp(zs, 2)


def core_pieces(zs, ys):
    return (zs, swap_dp(zs, 1), ys, swap_dp(ys, 1))


def add_low(*parts):
    return sum(p.astype(F32) for p in parts).astype(BF)


def other_groups(total):
    bit = 4
    while bit < lax.axis_size("dp"):
        total = add_low(total, swap_dp(total, bit))
        bit *= 2
    return total


def z_parts(quarter):
    return [quarter[0]] + [shift_tensor(quarter[r], -r) for r in range(1, 4)]


def z_sum(parts):
    return other_groups(add_low(*parts))


def spread_pieces(piece):
    along_y = jnp.stack([piece, swap_dp(piece, 2)])
    mate = swap_dp(along_y, 1)
    return jnp.stack([along_y[0], mate[0], along_y[1], mate[1]])


def dg(a, b, ca, cb):
    return lax.dot_general(a, b, (((ca,), (cb,)), ((), ())), preferred_element_type=F32)


def norm_fwd(r):
    off = r - jnp.mean(r, axis=-1, keepdims=True)
    inv = lax.rsqrt(jnp.mean(off * off, axis=-1, keepdims=True) + EPS)
    return off * inv, inv


def norm_bwd(dy, n, inv, gain):
    sc = dy * gain
    dr = inv * (
        sc
        - jnp.mean(sc, axis=-1, keepdims=True)
        - n * jnp.mean(sc * n, axis=-1, keepdims=True)
    )
    return dr, jnp.sum(dy * n, axis=0, keepdims=True), jnp.sum(dy, axis=0, keepdims=True)


def head_lanes(h):
    return (lax.broadcasted_iota(jnp.int32, (1, PAIR), 1) // HD) == h


def mask_bias(info, row, n_q, n_k, q_axis):
    flip = info[row, 9]
    q_shape = (n_q, 1) if q_axis == 0 else (1, n_q)
    full = (n_q, n_k) if q_axis == 0 else (n_k, n_q)
    q_pos = lax.broadcasted_iota(jnp.int32, q_shape, q_axis) ^ flip
    seg = jnp.where(info[row, 8] == 1, 0, q_pos >> SLOT_BITS)
    size = jnp.zeros(q_shape, jnp.int32)
    for j in range(SLOTS):
        size = size + jnp.where(seg == j, info[row, j], 0)
    first = seg << SLOT_BITS
    end = first + size
    end = jnp.where(info[row, 10] == 1, jnp.minimum(end, q_pos + 1), end)
    k_pos = lax.broadcasted_iota(jnp.int32, full, 1 - q_axis) ^ flip
    return jnp.where((k_pos >= first) & (k_pos < end), 0.0, NEG)


class Copies:
    def __init__(self, sems):
        self.sems = sems
        self.count = 0

    def start(self, src, dst):
        copy = pltpu.make_async_copy(src, dst, self.sems.at[self.count])
        self.count += 1
        copy.start()
        return copy


class Raw:
    def __init__(self, value):
        self.value = value


class Fetch(Raw):
    pass


class Late(Raw):
    pass


class Fetched:
    def __init__(self, copy, ref):
        self.copy = copy
        self.ref = ref
        self.shape = ref.shape

    def ready(self):
        if self.copy is not None:
            self.copy.wait()
            self.copy = None
        return self.ref

    def __getitem__(self, at):
        return self.ready()[at]


class Result:
    def __init__(self, copies, ref, dst):
        self.copies = copies
        self.ref = ref
        self.dst = dst
        self.shape = ref.shape
        self.copy = None

    def __setitem__(self, at, value):
        self.ref[at] = value

    def __getitem__(self, at):
        return self.ref[at]

    def flush(self):
        if self.copy is None:
            self.copy = self.copies.start(self.ref, self.dst)


def load_wall(copies, me, refs, wall):
    local, *pieces = refs
    started = []
    for rel, ref in enumerate(pieces):
        started.append(copies.start(local.at[me ^ rel], wall.at[rel, :, pl.ds(0, PAIR)]))
        for z in range(1, 4):
            started.append(copies.start(ref.at[z - 1], wall.at[rel, :, pl.ds(z * PAIR, PAIR)]))
    return started


def load_units(copies, me, refs, units):
    local, *pieces = refs
    started = []
    for rel, ref in enumerate(pieces):
        started.append(copies.start(local.at[me ^ rel], units.at[rel * 4]))
        started.append(copies.start(ref, units.at[pl.ds(rel * 4 + 1, 3)]))
    return started


def wait_all(started):
    for copy in started:
        copy.wait()


def unit_block(units, which, i):
    return jnp.concatenate([units[2 * i, which], units[2 * i + 1, which]], axis=0)


def attend_forward(q_ref, k_ref, v_ref, bias_ref, att_ref, lse_ref):
    n_q = q_ref.shape[0]

    def pair(hp, _):
        sl = pl.ds(pl.multiple_of(hp * PAIR, PAIR), PAIR)
        kp = k_ref[:, sl]
        vp = v_ref[:, sl]
        qp = q_ref[:, sl]
        out = None
        for h in range(2):
            lanes = head_lanes(h)
            s = dg(jnp.where(lanes, qp, jnp.zeros_like(qp)), kp, 1, 1) + bias_ref[...]
            top = jnp.max(s, axis=1, keepdims=True)
            e = jnp.exp(s - top)
            total = jnp.sum(e, axis=1, keepdims=True)
            o = dg(e.astype(BF), vp, 1, 0) * (1.0 / total)
            lse = jnp.broadcast_to(top + jnp.log(total), (n_q, 8))
            lse_ref[hp * 2 + h] = jnp.transpose(lse)[0:1, :]
            o = jnp.where(lanes, o, 0.0)
            out = o if out is None else out + o
        att_ref[:, sl] = out.astype(BF)
        return 0

    lax.fori_loop(0, HEADS // 2, pair, 0)


def attend_backward(info, row, n_pairs, q_ref, k_ref, v_ref, do_ref, att_ref, lse_ref, bias_ref, rd_ref, dq_ref, dk_ref, dv_ref):
    n_q = q_ref.shape[0]
    block = 256
    empty = info[row, 0]
    for j in range(1, SLOTS):
        empty = empty + info[row, j]
    empty = empty == 0
    p_fix = jnp.where(empty, 1.0 / k_ref.shape[0], 1.0)
    s_fix = jnp.where(empty, 0.0, 1.0)
    width = n_pairs * PAIR
    prod = do_ref[...].astype(F32) * att_ref[...].astype(F32)
    high = prod.astype(BF)
    low = (prod - high.astype(F32)).astype(BF)
    heads = lax.broadcasted_iota(jnp.int32, (HEADS, width), 0)
    lanes_of = lax.broadcasted_iota(jnp.int32, (HEADS, width), 1) // HD
    ones = jnp.where(heads == lanes_of, 1.0, 0.0).astype(BF)
    rd = dg(ones, high, 1, 1) + dg(ones, low, 1, 1)
    for h in range(2 * n_pairs):
        rd_ref[h] = rd[h : h + 1]

    def pair(hp, _):
        sl = pl.ds(pl.multiple_of(hp * PAIR, PAIR), PAIR)
        kp = k_ref[:, sl]
        vp = v_ref[:, sl]
        k_t = jnp.transpose(kp)
        dk = dv = None
        for qi in range(n_q // block):
            qs = slice(qi * block, (qi + 1) * block)
            qp = q_ref[qs, sl]
            dop = do_ref[qs, sl]
            dqs = []
            for h in range(2):
                lanes = head_lanes(h)
                qm = jnp.where(lanes, qp, jnp.zeros_like(qp))
                dom = jnp.where(lanes, dop, jnp.zeros_like(dop))
                s = dg(kp, qm, 1, 1) + bias_ref[:, qs]
                p = jnp.exp(s - lse_ref[hp * 2 + h, :, qs])
                dp = dg(vp, dom, 1, 1)
                ds = (p * (dp - rd_ref[hp * 2 + h, :, qs])).astype(BF)
                a = dg(p.astype(BF), dom, 1, 0)
                dv = a if dv is None else dv + a
                a = dg(ds, qm, 1, 0)
                dk = a if dk is None else dk + a
                dqs.append(dg(k_t[h * HD : (h + 1) * HD], ds, 1, 0))
            dq = jnp.transpose(jnp.concatenate(dqs, axis=0))
            dq_ref[qs, sl] = (dq * (SCALE * s_fix)).astype(BF)
        dk_ref[:, sl] = (dk * s_fix).astype(BF)
        dv_ref[:, sl] = (dv * p_fix).astype(BF)
        return 0

    lax.fori_loop(0, n_pairs, pair, 0)


def self_forward_kernel(copies, info, x0, x1, x2, x3, gain, shift, *refs):
    w_refs = refs[:5]
    y_out, low_out, n_out, inv_out, q_out, k_out, v_out, att_out, lse_out, wall, bias_ref = refs[5:]
    me = info[0, 11]
    started = load_wall(copies, me, w_refs, wall)
    bias_ref[...] = mask_bias(info, 0, q_out.shape[0], k_out.shape[0], 0)
    wait_all(started)
    rows_low = jnp.concatenate([x0[...], x1[...]], axis=0)
    q_out[...] = dg(rows_low, wall[me], 1, 0).astype(BF) * jnp.asarray(SCALE, BF)
    wk = wall[me ^ 1]
    wv = wall[me ^ 2]
    at = 0
    for ref in (x0, x1, x2, x3):
        part = ref[...]
        k_out[at : at + ref.shape[0]] = dg(part, wk, 1, 0).astype(BF)
        v_out[at : at + ref.shape[0]] = dg(part, wv, 1, 0).astype(BF)
        at += ref.shape[0]
    for out in (q_out, k_out, v_out):
        out.flush()
    attend_forward(q_out.ref, k_out.ref, v_out.ref, bias_ref, att_out.ref, lse_out)
    att_out.flush()
    branch = dg(att_out[...], wall[me ^ 3], 1, 1)
    n, inv = norm_fwd(rows_low.astype(F32) + branch)
    n_out[...] = n
    inv_out[...] = inv
    y = n * gain[...] + shift[...]
    y_out[...] = y
    low_out[...] = y.astype(BF)


def silu_parts(u):
    sg = jax.nn.sigmoid(u)
    return u * sg, sg


def ffn_forward_kernel(copies, info, x_ref, gain, shift, *refs):
    low_out, n_out, inv_out, units = refs[5:]
    started = load_units(copies, info[0, 11], refs[:5], units)
    x = x_ref[...]
    low = x.astype(BF)
    acc = x
    wait_all(started)
    for i in range(units.shape[0] // 2):
        u = dg(low, unit_block(units, 0, i), 1, 1)
        act = silu_parts(u)[0].astype(BF)
        acc = acc + dg(act, unit_block(units, 1, i), 1, 0)
    n, inv = norm_fwd(acc)
    low_out[...] = (n * gain[...] + shift[...]).astype(BF)
    n_out[...] = n
    inv_out[...] = inv


def decoder_kernel(copies, info, mem_own, mem_mate, h_low, h_ref, cot0, cot1, cgain, cshift, gain3, shift3, mem_low, n3e, inv3e, *refs):
    w_refs, unit_refs = refs[:5], refs[5:10]
    out0, out1, x_ref, n3_ref, inv3_ref = refs[10:15]
    dh_out, dmem_own_out, dmem_mate_out, dbr_out, att_out, dq_out, dk_out, dv_out, dnorm_out = refs[15:24]
    (wall, units, bias_n, bias_t, q_ref, k_ref, v_ref, lse_ref, rd_ref, do_ref, u_ref, n2_ref, dh2_ref) = refs[24:]
    me = info[1, 11]
    dec = info[1, 12] == 1
    n_q, n_k = q_ref.shape[0], k_ref.shape[0]
    wall_started = load_wall(copies, me, w_refs, wall)
    unit_started = load_units(copies, me, unit_refs, units)
    bias_n[...] = mask_bias(info, 1, n_q, n_k, 0)
    bias_t[...] = mask_bias(info, 1, n_q, n_k, 1)
    wait_all(wall_started)
    q_ref[...] = dg(h_low[...], wall[me], 1, 0).astype(BF) * jnp.asarray(SCALE, BF)
    half = mem_own.shape[0]
    for ref, at in ((mem_own, 0), (mem_mate, half)):
        k_ref[at : at + half] = dg(ref[...], wall[me ^ 1], 1, 0).astype(BF)
        v_ref[at : at + half] = dg(ref[...], wall[me ^ 2], 1, 0).astype(BF)
    attend_forward(q_ref, k_ref, v_ref, bias_n, att_out, lse_ref)
    n2, inv2 = norm_fwd(h_ref[...] + dg(att_out[...], wall[me ^ 3], 1, 1))
    n2_ref[...] = n2
    acc = n2 * cgain[...] + cshift[...]
    low = acc.astype(BF)
    x_ref[...] = low
    wait_all(unit_started)
    width = 2 * PAIR
    blocks = units.shape[0] // 2
    for i in range(blocks):
        u = dg(low, unit_block(units, 0, i), 1, 1)
        u_ref[:, i * width : (i + 1) * width] = u
        act = silu_parts(u)[0].astype(BF)
        acc = acc + dg(act, unit_block(units, 1, i), 1, 0)
    n, inv = norm_fwd(acc)
    y = (n * gain3[...] + shift3[...]).astype(BF)
    out0[...] = y[: out0.shape[0]]
    out1[...] = y[out0.shape[0] :]
    n3_ref[...] = n
    inv3_ref[...] = inv
    cot = jnp.concatenate([cot0[...], cot1[...]], axis=0).astype(F32)
    for ref, src in ((out0, mem_low[: out0.shape[0]]), (out1, mem_low[out0.shape[0] :]), (x_ref, h_low[...]), (n3_ref, n3e[...]), (inv3_ref, inv3e[...])):
        ref[...] = jnp.where(dec, ref[...], src)
    dr, _, _ = norm_bwd(cot, n, inv, gain3[...])
    dbr = dr.astype(BF)
    acc = dr
    for i in range(blocks):
        u = u_ref[:, i * width : (i + 1) * width]
        sg = jax.nn.sigmoid(u)
        dact = dg(dbr, unit_block(units, 1, i), 1, 1)
        du = (dact * sg * (1.0 + u * (1.0 - sg))).astype(BF)
        acc = acc + dg(du, unit_block(units, 0, i), 1, 0)
    dr, dg_sum, db_sum = norm_bwd(acc, n2_ref[...], inv2, cgain[...])
    dnorm_out[0:1] = dg_sum
    dnorm_out[1:2] = db_sum
    dh2_ref[...] = dr
    dbr = dr.astype(BF)
    dbr_out[...] = dbr
    do_ref[...] = dg(dbr, wall[me ^ 3], 1, 0).astype(BF)
    attend_backward(
        info, 1, HEADS // 2, q_ref, k_ref, v_ref, do_ref, att_out, lse_ref, bias_t, rd_ref, dq_out, dk_out, dv_out
    )
    wk = wall[me ^ 1]
    wv = wall[me ^ 2]
    for out, at in ((dmem_mate_out, half), (dmem_own_out, 0)):
        part = dg(dk_out[at : at + half], wk, 1, 1) + dg(dv_out[at : at + half], wv, 1, 1)
        out[...] = part.astype(BF)
    dh_out[...] = dh2_ref[...] + dg(dq_out[...], wall[me], 1, 1)


def put_matrix(keep_ref, send_ref, me, which, value):
    slot = me ^ which
    y = slot >> 1

    @pl.when(slot % 2 == 0)
    def _():
        for z in range(4):
            keep_ref[y, z, : value.shape[0]] = value[:, z * PAIR : (z + 1) * PAIR]

    @pl.when(slot % 2 == 1)
    def _():
        for z in range(4):
            send_ref[y, z, : value.shape[0]] = value[:, z * PAIR : (z + 1) * PAIR]


def cross_weights_kernel(copies, info, h_low, dq_ref, mem_own, mem_mate, dk_ref, dv_ref, dbr_ref, att_ref, keep, send):
    me = info[1, 11]
    half = mem_own.shape[0]

    put_matrix(keep, send, me, 0, dg(h_low[...], dq_ref[...], 0, 0).astype(BF))
    for which, ref in ((1, dk_ref), (2, dv_ref)):
        value = dg(mem_own[...], ref[:half], 0, 0) + dg(mem_mate[...], ref[half:], 0, 0)
        put_matrix(keep, send, me, which, value.astype(BF))
    put_matrix(keep, send, me, 3, dg(dbr_ref[...], att_ref[...], 0, 0).astype(BF))


def ffn_backward_part(info, low, dbr, acc, units, half_units, target):
    for i in range(half_units):
        y, z = i // 2, i % 2
        wu = unit_block(units, 0, i)
        wd = unit_block(units, 1, i)
        u_t = dg(wu, low, 1, 1)
        act_t, sg = silu_parts(u_t)
        act_t = act_t.astype(BF)
        dact_t = dg(wd, dbr, 1, 1)
        du_t = (dact_t * sg * (1.0 + u_t * (1.0 - sg))).astype(BF)
        acc = acc + dg(du_t, wu, 0, 0)
        dup = dg(du_t, low, 1, 0).astype(BF)
        ddown = dg(act_t, dbr, 1, 0).astype(BF)
        for j in range(2):
            target[y, 0, 2 * z + j] = dup[j * PAIR : (j + 1) * PAIR]
            target[y, 1, 2 * z + j] = ddown[j * PAIR : (j + 1) * PAIR]
    return acc


def load_half_units(copies, me, local, first, refs, units):
    started = []
    for y, ref in enumerate(refs):
        started.append(copies.start(local.at[me ^ (first + 2 * y)], units.at[y * 4]))
        started.append(copies.start(ref, units.at[pl.ds(y * 4 + 1, 3)]))
    return started


def ffn_backward_mate_kernel(copies, info, x_ref, n3_ref, inv3_ref, cot0, cot1, dmem_ref, gain3, local, piece0, piece1,
                             send, acc_out, dbr_out, dnorm_out, units):
    started = load_half_units(copies, info[0, 11], local, 1, (piece0, piece1), units)
    dy = jnp.concatenate([cot0[...], cot1[...]], axis=0).astype(F32) + dmem_ref[...].astype(F32)
    dr3, dg3, db3 = norm_bwd(dy, n3_ref[...], inv3_ref[...], gain3[...])
    dnorm_out[0:1] = dg3
    dnorm_out[1:2] = db3
    dbr = dr3.astype(BF)
    dbr_out[...] = dbr
    wait_all(started)
    acc_out[...] = ffn_backward_part(info, x_ref[...], dbr, dr3, units, 4, send)


def ffn_backward_own_kernel(copies, info, x_ref, dbr_ref, acc_ref, n1_ref, inv1_ref, gain1, dmid_ref, local, piece0, piece1,
                            w0, w1, w2, w3, w4, do_out, keep, dr1_out, dbr1_out, dnorm_out, units, wall):
    me = info[0, 11]
    started = load_half_units(copies, me, local, 0, (piece0, piece1), units)
    wall_started = load_wall(copies, me, (w0, w1, w2, w3, w4), wall)
    wait_all(started)
    acc = ffn_backward_part(info, x_ref[...], dbr_ref[...], acc_ref[...], units, 4, keep)
    dmid = jnp.where(info[0, 12] == 1, dmid_ref[...], acc)
    dr1, dg1, db1 = norm_bwd(dmid, n1_ref[...], inv1_ref[...], gain1[...])
    dr1_out[...] = dr1
    dbr1 = dr1.astype(BF)
    dbr1_out[...] = dbr1
    dnorm_out[0:1] = dg1
    dnorm_out[1:2] = db1
    wait_all(wall_started)
    do_out[...] = dg(dbr1, wall[me ^ 3], 1, 0).astype(BF)


def self_backward_kernel(first, copies, info, q, k, v, att, do, lse, dq_out, own, mate, bias_ref, q_ref, k_ref, v_ref, do_ref, att_ref, rd_ref, dk_ref, dv_ref):
    width = q_ref.shape[1]
    columns = pl.ds(first * PAIR, width)
    started = [copies.start(src.at[:, columns], dst) for src, dst in ((q, q_ref), (k, k_ref), (v, v_ref), (att, att_ref))]
    bias_ref[...] = mask_bias(info, 0, q_ref.shape[0], k_ref.shape[0], 1)
    do_ref[...] = do[:, columns]
    wait_all(started)
    lse_ref = lse.at[pl.ds(2 * first, 2 * width // PAIR)]
    attend_backward(info, 0, width // PAIR, q_ref, k_ref, v_ref, do_ref, att_ref, lse_ref, bias_ref, rd_ref, dq_out, dk_ref, dv_ref)
    half = q_ref.shape[0]
    for dst, at in ((mate, half), (own, 0)):
        dst[0] = dk_ref[at : at + half]
        dst[1] = dv_ref[at : at + half]


def input_backward_kernel(copies, info, x0, x1, dq_a, dq_b, own_a, own_b, got_a, got_b, att_ref, dbr_ref, dr_ref, dnorm1, dnorm2, dnorm3, *refs):
    w_refs = refs[:5]
    dx0, dx1, keep, send, wall = refs[5:]
    me = info[0, 11]
    started = load_wall(copies, me, w_refs, wall)
    dq = jnp.concatenate([dq_a[...], dq_b[...]], axis=1)

    def total(i):
        parts = [(own[i].astype(F32) + got[i].astype(F32)).astype(BF) for own, got in ((own_a, got_a), (own_b, got_b))]
        return jnp.concatenate(parts, axis=1)

    dk = total(0)
    dv = total(1)
    x = jnp.concatenate([x0[...], x1[...]], axis=0)
    for which, value in ((0, dq), (1, dk), (2, dv)):
        put_matrix(keep, send, me, which, dg(x, value, 0, 0).astype(BF))
    put_matrix(keep, send, me, 3, dg(dbr_ref[...], att_ref[...], 0, 0).astype(BF))
    feat = dq.shape[1]
    norms = jnp.concatenate([dnorm1[0:1], dnorm3[0:1], dnorm1[1:2], dnorm3[1:2], dnorm2[0:2], jnp.zeros((2, feat), F32)], axis=0)
    rows = jnp.concatenate([norms[:, i * PAIR : (i + 1) * PAIR] for i in range(feat // PAIR)], axis=0).astype(BF)
    for out in (keep, send):
        for y in range(2):
            for z in range(4):
                out[y, z, feat:] = rows
    wait_all(started)
    dx = dr_ref[...] + dg(dq, wall[me], 1, 1) + dg(dk, wall[me ^ 1], 1, 1) + dg(dv, wall[me ^ 2], 1, 1)
    half = dx0.shape[0]
    dx0[...] = dx[:half].astype(BF)
    dx1[...] = dx[half:].astype(BF)


def call(kernel, outs, args, scratch=(), vmem=60, us=1.0):
    in_hbm = pl.BlockSpec(memory_space=pltpu.HBM)
    in_vmem = pl.BlockSpec(memory_space=pltpu.VMEM)
    in_smem = pl.BlockSpec(memory_space=pltpu.SMEM)
    arrays = [a.value if isinstance(a, Raw) else a for a in args]
    shapes = [o.value if isinstance(o, Raw) else o for o in outs]
    moved = [pltpu.VMEM(a.value.shape, a.value.dtype) for a in args if isinstance(a, Fetch)]
    moved += [pltpu.VMEM(*o.value) for o in outs if isinstance(o, Late)]

    def wrapped(*refs):
        ins, refs = refs[: len(arrays)], refs[len(arrays) :]
        results, refs = refs[: len(shapes)], refs[len(shapes) :]
        buffers, rest, sems = list(refs[: len(moved)]), refs[len(moved) : -1], refs[-1]
        copies = Copies(sems)
        given = []
        for ref, arg in zip(ins, args):
            if isinstance(arg, Fetch):
                buffer = buffers.pop(0)
                ref = Fetched(copies.start(ref, buffer), buffer)
            given.append(ref)
        produced = []
        for ref, out in zip(results, outs):
            produced.append(Result(copies, buffers.pop(0), ref) if isinstance(out, Late) else ref)
        kernel(copies, *given, *produced, *rest)
        for ref in given:
            if isinstance(ref, Fetched):
                ref.ready()
        for out in produced:
            if isinstance(out, Result):
                out.flush()
        for out in produced:
            if isinstance(out, Result):
                out.copy.wait()

    return pl.pallas_call(
        wrapped,
        out_shape=tuple(jax.ShapeDtypeStruct(*o) for o in shapes),
        in_specs=[
            in_hbm if isinstance(a, Raw) else in_smem if a.dtype == jnp.int32 else in_vmem for a in args
        ],
        out_specs=tuple(in_hbm if isinstance(o, Raw) else in_vmem for o in outs),
        scratch_shapes=[*moved, *scratch, pltpu.SemaphoreType.DMA((64,))],
        compiler_params=pltpu.CompilerParams(vmem_limit_bytes=vmem * MIB),
        cost_estimate=pl.CostEstimate(flops=int(us * 1e9), bytes_accessed=int(us * 2e6), transcendentals=0),
    )(*arrays)


def body(
    inputs,
    cotangent,
    lengths,
    row_flags,
    qkv_w,
    out_w,
    cross_w,
    up_w,
    down_w,
    norm_gain,
    norm_bias,
    cross_gain,
    cross_bias,
):
    section = lax.axis_index("section")
    is_dec = section == 1
    d = lax.axis_index("dp")
    t = lax.axis_index("tensor")
    core = d % 2
    me = d % 4
    feat = inputs.shape[3]
    chunk = inputs.shape[2]
    half = 2 * chunk
    row_len = 2 * half
    quarter = qkv_w.shape[3]
    n_t = 4

    attn_local = jnp.concatenate([qkv_w[0], out_w[0].T[None]], axis=0)
    piece = jnp.where(me == 3, out_w[0].T, lax.dynamic_index_in_dim(qkv_w[0], jnp.minimum(me, 2), 0, False))
    attn_z = z_pieces(piece)
    got = [deal(lax.dynamic_index_in_dim(inputs[0], (t + k) % 2, 0, False), k) for k in range(2)]
    unit_quarter = up_w.shape[2] // 4
    ffn_local = jnp.stack([up_w[0].T.reshape(4, unit_quarter, feat), down_w[0].reshape(4, unit_quarter, feat)], axis=1)
    cross_other = to_decoder(after(cross_w[0], attn_z))
    cross_local = jnp.stack([cross_w[0, 0], cross_other[0], cross_other[1], cross_w[0, 1]])
    cross_piece = lax.dynamic_index_in_dim(cross_local, me, 0, False)

    own_info = jnp.concatenate(
        [lengths[0], lengths[1], row_flags[:, None], jnp.zeros((2, 7), jnp.int32)], axis=1
    ).astype(F32)
    mate_info = swap_dp(own_info, 1)
    row_info = jnp.where(t // 2 == core, own_info, mate_info)
    row_info = lax.dynamic_index_in_dim(row_info, t % 2, 0, False).astype(jnp.int32)
    flip = core * half + (t % 2) * chunk
    src_lens = row_info[0:8]
    dec_int = is_dec.astype(jnp.int32)

    def tail(causal):
        return jnp.stack([row_info[16], flip, causal, me, dec_int, t, 0, 0]).astype(jnp.int32)

    info = jnp.stack([
        jnp.concatenate([jnp.where(is_dec, row_info[8:16], src_lens), tail(dec_int)]),
        jnp.concatenate([src_lens, tail(0)]),
    ])

    gains = jnp.where(is_dec, norm_gain[1], norm_gain[0])
    shifts = jnp.where(is_dec, norm_bias[1], norm_bias[0])
    gain1, gain3 = gains[0:1], gains[1:2]
    shift1, shift3 = shifts[0:1], shifts[1:2]
    cgain, cshift = cross_gain[None], cross_bias[None]

    rows = (half, feat)
    full = (row_len, feat)
    column = (half, 1)
    wall = pltpu.VMEM((4, feat, feat), BF)
    units = pltpu.VMEM((4 * n_t, 2, unit_quarter, feat), BF)
    bias_n = pltpu.VMEM((half, row_len), F32)
    bias_t = pltpu.VMEM((row_len, half), F32)
    rd_s = pltpu.VMEM((HEADS, 1, half), F32)

    def raw(*arrays):
        return [Raw(a) for a in arrays]

    def fetch(*arrays):
        return [Fetch(a) for a in arrays]

    def late(*shapes):
        return [Late(a) for a in shapes]

    attn_zs, attn_ys = y_pieces(attn_z)
    attn_ws = raw(attn_local, *core_pieces(attn_zs, attn_ys))
    mate = [swap_dp(g, 1) for g in got]
    ffn_z = z_pieces(after(lax.dynamic_index_in_dim(ffn_local, me, 0, False), attn_zs))
    mid, mid_low, n1, inv1, q1, k1, v1, att1, lse1 = call(
        self_forward_kernel,
        [(rows, F32), (rows, BF), *late((rows, F32)), (column, F32), *late((rows, BF), (full, BF), (full, BF), (rows, BF)),
         ((HEADS, 1, half), F32)],
        [info, *fetch(after(got[0], cross_piece), got[1], *mate), gain1, shift1, *attn_ws], [wall, bias_n], 17, 13.0,
    )
    ffn_zs, ffn_ys = y_pieces(after(ffn_z, mid))
    cross_z = z_pieces(after(cross_piece, mid))
    ffn_ws = raw(ffn_local, *core_pieces(ffn_zs, after(ffn_ys, *cross_z)))
    mem_low, n3e, inv3e = call(
        ffn_forward_kernel, [(rows, BF), (rows, F32), (column, F32)], [info, mid, gain3, shift3, *ffn_ws], [units], 8, 4.5,
    )
    mem_own = to_decoder(mem_low)
    cross_zs, cross_ys = y_pieces(after(cross_z, mem_low))
    cot = [deal(after(lax.dynamic_index_in_dim(cotangent[0], (t + k) % 2, 0, False), mem_low), k) for k in range(2)]
    mem_own, cross_ys, *cot = lax.optimization_barrier((mem_own, cross_ys, *cot))
    cross_ws = raw(cross_local, *core_pieces(cross_zs, cross_ys))
    mem_mate = swap_dp(mem_own, 1)

    out0, out1, ffn_x, n3, inv3, dh1, dmem_own, dmem_mate, dbr2, att2, dq2, dk2, dv2, dnorm2 = call(
        decoder_kernel,
        [((chunk, feat), BF), ((chunk, feat), BF), (rows, BF), (rows, F32), (column, F32), (rows, F32), (rows, BF), (rows, BF),
         (rows, BF), (rows, BF), (rows, BF), (full, BF), (full, BF), ((8, feat), F32)],
        [info, *fetch(mem_own, mem_mate), mid_low, mid, *fetch(*cot), cgain, cshift, gain3, shift3, mem_low, n3e, inv3e, *cross_ws, *ffn_ws],
        [wall, units, bias_n, bias_t, pltpu.VMEM(rows, BF), pltpu.VMEM(full, BF), pltpu.VMEM(full, BF),
         rd_s, rd_s, pltpu.VMEM(rows, BF), pltpu.VMEM((half, 4 * n_t * unit_quarter), F32),
         pltpu.VMEM(rows, F32), pltpu.VMEM(rows, F32)], 33, 35.0,
    )
    dmem_got = swap_dp(dmem_mate, 1)
    pieces = [((2, n_t, feat, quarter), BF)] * 2
    cross_keep, cross_send = call(
        cross_weights_kernel, pieces, [info, mid_low, dq2, mem_own, mem_mate, dk2, dv2, dbr2, att2], vmem=8, us=3.5,
    )
    dmem = add_low(dmem_own, after(dmem_got, cross_keep))
    dmem_enc = to_encoder(dmem)
    out_back = [deal_back(after(out, dmem), k) for k, out in enumerate((out0, out1))]
    cross_mate = swap_dp(after(cross_send, dmem), 1)
    cross_got = swap_dp(add_low(cross_keep[1], cross_mate[1]), 2)
    dmem_enc, cross_got, *out_back = lax.optimization_barrier((dmem_enc, cross_got, *out_back))
    cross_quarter = add_low(cross_keep[0], cross_mate[0], cross_got)

    ffn_pieces = (2, 2, n_t, unit_quarter, feat)
    half_units = pltpu.VMEM((2 * n_t, 2, unit_quarter, feat), BF)
    ffn_local_w, ffn_own0, ffn_mate0, ffn_own1, ffn_mate1 = ffn_ws
    ffn_send, acc, dbr3, dnorm3 = call(
        ffn_backward_mate_kernel, [(ffn_pieces, BF), (rows, F32), (rows, BF), ((8, feat), F32)],
        [info, ffn_x, n3, inv3, *fetch(*cot, after(dmem_enc, cross_quarter)), gain3, ffn_local_w, ffn_mate0, ffn_mate1],
        [half_units], 10, 6.0,
    )
    cross_parts = z_parts(cross_quarter)
    ffn_got = swap_dp(ffn_send, 1)
    do1, ffn_keep, dr1, dbr1, dnorm1 = call(
        ffn_backward_own_kernel, [(rows, BF), (ffn_pieces, BF), (rows, F32), (rows, BF), ((8, feat), F32)],
        [info, ffn_x, dbr3, acc, *fetch(n1), inv1, gain1, dh1, ffn_local_w, ffn_own0, ffn_own1, *attn_ws],
        [half_units, wall], 11, 7.0,
    )
    ffn_got = after(ffn_got, do1)
    cross_parts = after(cross_parts, do1)
    up_got = swap_dp(add_low(ffn_keep[1, 0], ffn_got[1, 0]), 2)

    def self_backward(first, n_pairs, do):
        width = n_pairs * PAIR
        half_grad = ((2, half, width), BF)
        return call(
            functools.partial(self_backward_kernel, first), [((half, width), BF), half_grad, half_grad],
            [info, *raw(q1, k1, v1, att1), do, lse1],
            [bias_t, pltpu.VMEM((half, width), BF), pltpu.VMEM((row_len, width), BF), pltpu.VMEM((row_len, width), BF),
             pltpu.VMEM((half, width), BF), pltpu.VMEM((half, width), BF), rd_s,
             pltpu.VMEM((row_len, width), BF), pltpu.VMEM((row_len, width), BF)], 11, 7.0,
        )

    dq_a, own_a, mate_a = self_backward(0, 2, do1)
    got_a = swap_dp(mate_a, 1)
    down_got = swap_dp(after(add_low(ffn_keep[1, 1], ffn_got[1, 1]), dq_a), 2)
    dq_b, own_b, mate_b = self_backward(2, 2, after(do1, dq_a))
    got_b = swap_dp(mate_b, 1)
    up_quarter = add_low(ffn_keep[0, 0], ffn_got[0, 0], after(up_got, dq_b))
    up_parts = z_parts(up_quarter)
    self_pieces = [((2, n_t, feat + 32, quarter), BF)] * 2
    dx0, dx1, self_keep, self_send = call(
        input_backward_kernel, [((chunk, feat), BF), ((chunk, feat), BF), *self_pieces],
        [info, *fetch(*got), dq_a, dq_b, own_a, own_b, *fetch(after(got_a, up_quarter), got_b, att1), dbr1, dr1, dnorm1, dnorm2, dnorm3,
         *attn_ws],
        [wall], 10, 4.5,
    )

    self_mate = swap_dp(self_send, 1)
    self_got = swap_dp(add_low(self_keep[1], self_mate[1]), 2)
    down_quarter = add_low(ffn_keep[0, 1], ffn_got[0, 1], after(down_got, self_mate))
    down_parts = z_parts(down_quarter)
    up_sum = z_sum(after(up_parts, self_mate))
    cross_sum = z_sum(after(cross_parts, self_mate))
    cross_sum = jnp.where(is_dec, cross_sum, to_encoder(cross_sum))
    cross_sum = spread_pieces(cross_sum)
    self_quarter = add_low(self_keep[0], self_mate[0], after(self_got, down_quarter))
    self_parts = z_parts(self_quarter)
    down_sum = z_sum(after(down_parts, self_quarter))
    self_piece = z_sum(self_parts)
    self_sum = spread_pieces(self_piece[:feat])
    ffn_sum = spread_pieces(after(jnp.stack([up_sum, down_sum]), self_quarter))

    def matrix(stacked, which):
        return lax.dynamic_index_in_dim(stacked, me ^ which, 0, False).astype(F32)

    qkv_grad = jnp.stack([matrix(self_sum, m) for m in range(3)])
    out_grad = matrix(self_sum, 3).T
    cross_grad = jnp.stack([
        matrix(cross_sum, jnp.where(is_dec, 0, 1)), matrix(cross_sum, jnp.where(is_dec, 3, 2))
    ])
    ffn_true = [matrix(ffn_sum, m) for m in range(4)]
    up_grad = jnp.concatenate([f[0].T for f in ffn_true], axis=1)
    down_grad = jnp.concatenate([f[1] for f in ffn_true], axis=0)

    norms = self_piece[feat:].astype(F32).reshape(n_t, 8, PAIR).transpose(1, 0, 2).reshape(8, feat)
    other = lax.ppermute(norms, "section", [(0, 1), (1, 0)])
    enc = jnp.where(is_dec, other, norms)
    dec = jnp.where(is_dec, norms, other)
    full_gain = jnp.stack([enc[0:2], dec[0:2]])
    full_bias = jnp.stack([enc[2:4], dec[2:4]])

    def in_order(back):
        even = t % 2 == 0
        return jnp.stack([jnp.where(even, back[0], back[1]), jnp.where(even, back[1], back[0])])

    out_rows = in_order(out_back)
    grad_rows = in_order([deal_back(after(dx, self_quarter), k) for k, dx in enumerate((dx0, dx1))]).astype(F32)
    return (
        out_rows[None],
        grad_rows[None],
        qkv_grad[None],
        out_grad[None],
        cross_grad[None],
        up_grad[None],
        down_grad[None],
        full_gain,
        full_bias,
        dec[4],
        dec[5],
    )


def solution(mesh):
    return jax.shard_map(
        body,
        mesh=mesh,
        in_specs=(
            P("section", "dp", "tensor", None),
            P("section", "dp", "tensor", None),
            P(None, "dp", None),
            P("dp"),
            P("section", None, None, "tensor"),
            P("section", "tensor", None),
            P("section", None, None, "tensor"),
            P("section", None, "tensor"),
            P("section", "tensor", None),
            P(),
            P(),
            P(),
            P(),
        ),
        out_specs=(
            P("section", "dp", "tensor", None),
            P("section", "dp", "tensor", None),
            P("section", None, None, "tensor"),
            P("section", "tensor", None),
            P("section", None, None, "tensor"),
            P("section", None, "tensor"),
            P("section", "tensor", None),
            P(),
            P(),
            P(),
            P(),
        ),
        check_vma=False,
    )
```

```python
import functools

import jax
import jax.numpy as jnp
from jax import lax
from jax.experimental import pallas as pl
from jax.experimental.pallas import tpu as pltpu
from jax.sharding import PartitionSpec as P

HEADS = 8
HD = 64
PAIR = 2 * HD
SLOT_BITS = 7
SLOTS = 8
NEG = -1e30
EPS = 1e-05
SCALE = HD ** -0.5
BF = jnp.bfloat16
F32 = jnp.float32
MIB = 1024 * 1024


def swap_dp(x, bit):
    n = lax.axis_size("dp")
    return lax.ppermute(x, "dp", [(i, i ^ bit) for i in range(n)])


def shift_tensor(x, step):
    n = lax.axis_size("tensor")
    return lax.ppermute(x, "tensor", [(i, (i + step) % n) for i in range(n)])


def swap_tensor(x, bit):
    n = lax.axis_size("tensor")
    return lax.ppermute(x, "tensor", [(i, i ^ bit) for i in range(n)])


def to_decoder(x):
    return lax.ppermute(x, "section", [(0, 1)])


def to_encoder(x):
    return lax.ppermute(x, "section", [(1, 0)])


def deal_route(k):
    n_t = lax.axis_size("tensor")
    route = []
    for d in range(lax.axis_size("dp")):
        group, core = divmod(d, 2)
        for t in range(n_t):
            plane = 2 * core + (t + k) % 2
            route.append((d * n_t + t, (2 * group + t // 2) * n_t + plane))
    return route


def deal(x, k):
    return lax.ppermute(x, ("dp", "tensor"), deal_route(k))


def deal_back(x, k):
    return lax.ppermute(x, ("dp", "tensor"), [(b, a) for a, b in deal_route(k)])


def together(*xs):
    return lax.optimization_barrier(xs)


def after(x, *events):
    return lax.optimization_barrier((x, *events))[0]


def z_pieces(piece):
    return [shift_tensor(piece, r) for r in range(1, 4)]


def add_low(*parts):
    return sum(p.astype(F32) for p in parts).astype(BF)


def other_groups(total):
    bit = 4
    while bit < lax.axis_size("dp"):
        total = add_low(total, swap_dp(total, bit))
        bit *= 2
    return total


def z_parts(quarter):
    return [quarter[0]] + [shift_tensor(quarter[r], -r) for r in range(1, 4)]


def cross_owner(section, d):
    return (d % 4 in (1, 2)) == (section == 0)


def cross_to_owner(quarter):
    n = lax.axis_size("dp")
    return lax.ppermute(quarter, ("section", "dp"), [(n + d, d) for d in range(n) if cross_owner(0, d)])


def cross_z_parts(quarter):
    n_d, n_t = lax.axis_size("dp"), lax.axis_size("tensor")
    parts = [quarter[0]]
    for r in range(1, 4):
        route = [
            ((s * n_d + d) * n_t + t, (s * n_d + d) * n_t + (t - r) % n_t)
            for s in range(2) for d in range(n_d) if cross_owner(s, d) for t in range(n_t)
        ]
        parts.append(lax.ppermute(quarter[r], ("section", "dp", "tensor"), route))
    return parts


def z_sum(parts):
    return other_groups(add_low(*parts))


def dg(a, b, ca, cb):
    return lax.dot_general(a, b, (((ca,), (cb,)), ((), ())), preferred_element_type=F32)


def norm_fwd(r):
    off = r - jnp.mean(r, axis=-1, keepdims=True)
    inv = lax.rsqrt(jnp.mean(off * off, axis=-1, keepdims=True) + EPS)
    return off * inv, inv


def norm_bwd(dy, n, inv, gain):
    sc = dy * gain
    dr = inv * (
        sc
        - jnp.mean(sc, axis=-1, keepdims=True)
        - n * jnp.mean(sc * n, axis=-1, keepdims=True)
    )
    return dr, jnp.sum(dy * n, axis=0, keepdims=True), jnp.sum(dy, axis=0, keepdims=True)


def head_lanes(h):
    return (lax.broadcasted_iota(jnp.int32, (1, PAIR), 1) // HD) == h


def mask_bias(info, row, n_q, n_k, q_axis):
    flip = info[row, 9]
    q_shape = (n_q, 1) if q_axis == 0 else (1, n_q)
    full = (n_q, n_k) if q_axis == 0 else (n_k, n_q)
    q_pos = lax.broadcasted_iota(jnp.int32, q_shape, q_axis) ^ flip
    seg = jnp.where(info[row, 8] == 1, 0, q_pos >> SLOT_BITS)
    size = jnp.zeros(q_shape, jnp.int32)
    for j in range(SLOTS):
        size = size + jnp.where(seg == j, info[row, j], 0)
    first = seg << SLOT_BITS
    end = first + size
    end = jnp.where(info[row, 10] == 1, jnp.minimum(end, q_pos + 1), end)
    k_pos = lax.broadcasted_iota(jnp.int32, full, 1 - q_axis) ^ flip
    return jnp.where((k_pos >= first) & (k_pos < end), 0.0, NEG)


class Copies:
    def __init__(self, sems):
        self.sems = sems
        self.count = 0

    def start(self, src, dst):
        copy = pltpu.make_async_copy(src, dst, self.sems.at[self.count])
        self.count += 1
        copy.start()
        return copy


class Raw:
    def __init__(self, value):
        self.value = value


class Fetch(Raw):
    pass


class Late(Raw):
    pass


class Fetched:
    def __init__(self, copy, ref):
        self.copy = copy
        self.ref = ref
        self.shape = ref.shape

    def ready(self):
        if self.copy is not None:
            self.copy.wait()
            self.copy = None
        return self.ref

    def __getitem__(self, at):
        return self.ready()[at]


class Result:
    def __init__(self, copies, ref, dst):
        self.copies = copies
        self.ref = ref
        self.dst = dst
        self.shape = ref.shape
        self.copy = None

    def __setitem__(self, at, value):
        self.ref[at] = value

    def __getitem__(self, at):
        return self.ref[at]

    def flush(self):
        if self.copy is None:
            self.copy = self.copies.start(self.ref, self.dst)


def load_wall(copies, me, refs, wall):
    local, *pieces = refs
    started = []
    for rel, ref in enumerate(pieces):
        started.append(copies.start(local.at[me ^ rel], wall.at[rel, :, pl.ds(0, PAIR)]))
        for z in range(1, 4):
            started.append(copies.start(ref.at[z - 1], wall.at[rel, :, pl.ds(z * PAIR, PAIR)]))
    return started


def load_units(copies, me, refs, units, rels=range(4)):
    local, *pieces = refs
    started = []
    for i, rel in enumerate(rels):
        started.append(copies.start(local.at[me ^ rel], units.at[4 * i]))
        started.append(copies.start(pieces[rel], units.at[pl.ds(4 * i + 1, 3)]))
    return started


def wait_all(started):
    for copy in started:
        copy.wait()


def unit_block(units, which, i):
    return jnp.concatenate([units[2 * i, which], units[2 * i + 1, which]], axis=0)


def attend_forward(first, n_pairs, q_ref, k_ref, v_ref, bias_ref, att_ref, lse_ref):
    n_q = q_ref.shape[0]

    def pair(hp, _):
        sl = pl.ds(pl.multiple_of((hp + first) * PAIR, PAIR), PAIR)
        kp = k_ref[:, sl]
        vp = v_ref[:, sl]
        qp = q_ref[:, sl]
        out = None
        for h in range(2):
            lanes = head_lanes(h)
            s = dg(jnp.where(lanes, qp, jnp.zeros_like(qp)), kp, 1, 1) + bias_ref[...]
            top = jnp.max(s, axis=1, keepdims=True)
            e = jnp.exp(s - top)
            total = jnp.sum(e, axis=1, keepdims=True)
            o = dg(e.astype(BF), vp, 1, 0) * (1.0 / total)
            lse = jnp.broadcast_to(top + jnp.log(total), (n_q, 8))
            lse_ref[hp * 2 + h] = jnp.transpose(lse)[0:1, :]
            o = jnp.where(lanes, o, 0.0)
            out = o if out is None else out + o
        att_ref[:, pl.ds(pl.multiple_of(hp * PAIR, PAIR), PAIR)] = out.astype(BF)
        return 0

    lax.fori_loop(0, n_pairs, pair, 0)


def attend_backward(info, row, n_pairs, q_ref, k_ref, v_ref, do_ref, att_ref, lse_ref, bias_ref, rd_ref, dq_ref, dk_ref, dv_ref):
    n_q = q_ref.shape[0]
    block = 256
    empty = info[row, 0]
    for j in range(1, SLOTS):
        empty = empty + info[row, j]
    empty = empty == 0
    p_fix = jnp.where(empty, 1.0 / k_ref.shape[0], 1.0)
    s_fix = jnp.where(empty, 0.0, 1.0)
    width = n_pairs * PAIR
    prod = do_ref[...].astype(F32) * att_ref[...].astype(F32)
    high = prod.astype(BF)
    low = (prod - high.astype(F32)).astype(BF)
    heads = lax.broadcasted_iota(jnp.int32, (HEADS, width), 0)
    lanes_of = lax.broadcasted_iota(jnp.int32, (HEADS, width), 1) // HD
    ones = jnp.where(heads == lanes_of, 1.0, 0.0).astype(BF)
    rd = dg(ones, high, 1, 1) + dg(ones, low, 1, 1)
    for h in range(2 * n_pairs):
        rd_ref[h] = rd[h : h + 1]

    def pair(hp, _):
        sl = pl.ds(pl.multiple_of(hp * PAIR, PAIR), PAIR)
        kp = k_ref[:, sl]
        vp = v_ref[:, sl]
        k_t = jnp.transpose(kp)
        dk = dv = None
        for qi in range(n_q // block):
            qs = slice(qi * block, (qi + 1) * block)
            qp = q_ref[qs, sl]
            dop = do_ref[qs, sl]
            dqs = []
            for h in range(2):
                lanes = head_lanes(h)
                qm = jnp.where(lanes, qp, jnp.zeros_like(qp))
                dom = jnp.where(lanes, dop, jnp.zeros_like(dop))
                s = dg(kp, qm, 1, 1) + bias_ref[:, qs]
                p = jnp.exp(s - lse_ref[hp * 2 + h, :, qs])
                dp = dg(vp, dom, 1, 1)
                ds = (p * (dp - rd_ref[hp * 2 + h, :, qs])).astype(BF)
                a = dg(p.astype(BF), dom, 1, 0)
                dv = a if dv is None else dv + a
                a = dg(ds, qm, 1, 0)
                dk = a if dk is None else dk + a
                dqs.append(dg(k_t[h * HD : (h + 1) * HD], ds, 1, 0))
            dq = jnp.transpose(jnp.concatenate(dqs, axis=0))
            dq_ref[qs, sl] = (dq * (SCALE * s_fix)).astype(BF)
        dk_ref[:, sl] = (dk * s_fix).astype(BF)
        dv_ref[:, sl] = (dv * p_fix).astype(BF)
        return 0

    lax.fori_loop(0, n_pairs, pair, 0)


def self_forward_kernel(copies, info, x0, x1, x2, x3, gain, shift, *refs):
    w_refs = refs[:5]
    y_out, low_out, n_out, inv_out, q_out, k_out, v_out, att_out, lse_out, wall, bias_ref = refs[5:]
    me = info[0, 11]
    started = load_wall(copies, me, w_refs, wall)
    bias_ref[...] = mask_bias(info, 0, q_out.shape[0], k_out.shape[0], 0)
    wait_all(started)
    rows_low = jnp.concatenate([x0[...], x1[...]], axis=0)
    q_out[...] = dg(rows_low, wall[me], 1, 0).astype(BF) * jnp.asarray(SCALE, BF)
    wk = wall[me ^ 1]
    wv = wall[me ^ 2]
    at = 0
    for ref in (x0, x1, x2, x3):
        part = ref[...]
        k_out[at : at + ref.shape[0]] = dg(part, wk, 1, 0).astype(BF)
        v_out[at : at + ref.shape[0]] = dg(part, wv, 1, 0).astype(BF)
        at += ref.shape[0]
    attend_forward(0, HEADS // 2, q_out, k_out, v_out, bias_ref, att_out, lse_out)
    n, inv = norm_fwd(rows_low.astype(F32) + dg(att_out[...], wall[me ^ 3], 1, 1))
    n_out[...] = n
    inv_out[...] = jnp.broadcast_to(inv, inv_out.shape)
    y = n * gain[...] + shift[...]
    y_out[...] = y
    low_out[...] = y.astype(BF)


def silu_parts(u):
    sg = jax.nn.sigmoid(u)
    return u * sg, sg


def ffn_forward_kernel(copies, info, x_ref, gain, shift, *refs):
    low_out, n_out, inv_out, units = refs[5:]
    started = load_units(copies, info[0, 11], refs[:5], units)
    x = x_ref[...]
    low = x.astype(BF)
    acc = x
    wait_all(started)
    for i in range(units.shape[0] // 2):
        u = dg(low, unit_block(units, 0, i), 1, 1)
        act = silu_parts(u)[0].astype(BF)
        acc = acc + dg(act, unit_block(units, 1, i), 1, 0)
    n, inv = norm_fwd(acc)
    low_out[...] = (n * gain[...] + shift[...]).astype(BF)
    n_out[...] = n
    inv_out[...] = jnp.broadcast_to(inv, inv_out.shape)


def cross_forward_kernel(copies, info, mem_own, mem_mate, h_low, h_ref, cgain, cshift, *refs):
    y_out, n_out, inv_out, q_out, k_out, v_out, att_out, lse_out, wall, bias_ref = refs[5:]
    me = info[1, 11]
    started = load_wall(copies, me, refs[:5], wall)
    bias_ref[...] = mask_bias(info, 1, q_out.shape[0], k_out.shape[0], 0)
    wait_all(started)
    q_out[...] = dg(h_low[...], wall[me], 1, 0).astype(BF) * jnp.asarray(SCALE, BF)
    half = mem_own.shape[0]
    for ref, at in ((mem_own, 0), (mem_mate, half)):
        k_out[at : at + half] = dg(ref[...], wall[me ^ 1], 1, 0).astype(BF)
        v_out[at : at + half] = dg(ref[...], wall[me ^ 2], 1, 0).astype(BF)
    attend_forward(0, HEADS // 2, q_out, k_out, v_out, bias_ref, att_out, lse_out)
    n, inv = norm_fwd(h_ref[...] + dg(att_out[...], wall[me ^ 3], 1, 1))
    n_out[...] = n
    inv_out[...] = jnp.broadcast_to(inv, inv_out.shape)
    y_out[...] = n * cgain[...] + cshift[...]


def decoder_kernel(copies, info, h_ref, cot0, cot1, n2_ref, inv2_ref, cgain, gain3, shift3, q_ref, k_ref, v_ref, att_ref, lse_ref,
                   h_low, mem_low, n3e, inv3e, *refs):
    w_refs, unit_refs = refs[:5], refs[5:10]
    (out0, out1, x_ref, n3_ref, inv3_ref, dh_out, dmem_own_out, dmem_mate_out, dbr_out, dq_out, dk_out, dv_out, dnorm_out,
     wall, units, bias_ref, rd_ref, do_ref, u_ref) = refs[10:]
    me = info[1, 11]
    dec = info[1, 12] == 1
    started = load_units(copies, me, unit_refs, units)
    wall_started = load_wall(copies, me, w_refs, wall)
    bias_ref[...] = mask_bias(info, 1, q_ref.shape[0], k_ref.shape[0], 1)
    acc = h_ref[...]
    low = acc.astype(BF)
    x_ref[...] = low
    wait_all(started)
    width = 2 * PAIR
    blocks = units.shape[0] // 2
    for i in range(blocks):
        u = dg(low, unit_block(units, 0, i), 1, 1)
        u_ref[:, i * width : (i + 1) * width] = u
        act = silu_parts(u)[0].astype(BF)
        acc = acc + dg(act, unit_block(units, 1, i), 1, 0)
    n, inv = norm_fwd(acc)
    y = (n * gain3[...] + shift3[...]).astype(BF)
    half = out0.shape[0]
    out0[...] = y[:half]
    out1[...] = y[half:]
    n3_ref[...] = n
    inv3_ref[...] = jnp.broadcast_to(inv, inv3_ref.shape)
    passed = ((out0, mem_low[:half]), (out1, mem_low[half:]), (x_ref, h_low[...]), (n3_ref, n3e[...]), (inv3_ref, inv3e[...]))
    for ref, src in passed:
        ref[...] = jnp.where(dec, ref[...], src)
    cot = jnp.concatenate([cot0[...], cot1[...]], axis=0).astype(F32)
    dr, _, _ = norm_bwd(cot, n, inv, gain3[...])
    dbr = dr.astype(BF)
    acc = dr
    for i in range(blocks):
        u = u_ref[:, i * width : (i + 1) * width]
        sg = jax.nn.sigmoid(u)
        dact = dg(dbr, unit_block(units, 1, i), 1, 1)
        du = (dact * sg * (1.0 + u * (1.0 - sg))).astype(BF)
        acc = acc + dg(du, unit_block(units, 0, i), 1, 0)
    dr, dg_sum, db_sum = norm_bwd(acc, n2_ref[...], inv2_ref[:, 0:1], cgain[...])
    dnorm_out[0:1] = dg_sum
    dnorm_out[1:2] = db_sum
    dh_out[...] = dr
    dbr = dr.astype(BF)
    dbr_out[...] = dbr
    wait_all(wall_started)
    do_ref[...] = dg(dbr, wall[me ^ 3], 1, 0).astype(BF)
    attend_backward(info, 1, HEADS // 2, q_ref, k_ref, v_ref, do_ref, att_ref, lse_ref, bias_ref, rd_ref, dq_out, dk_out, dv_out)
    half = dmem_own_out.shape[0]
    wk = wall[me ^ 1]
    wv = wall[me ^ 2]
    for out, at in ((dmem_mate_out, half), (dmem_own_out, 0)):
        part = dg(dk_out[at : at + half], wk, 1, 1) + dg(dv_out[at : at + half], wv, 1, 1)
        out[...] = part.astype(BF)
    dh_out[...] = dh_out[...] + dg(dq_out[...], wall[me], 1, 1)


def put_matrix(keep_ref, send_ref, me, which, value):
    slot = me ^ which
    y = slot >> 1

    def put(ref):
        for z in range(4):
            ref[y, z, : value.shape[0]] = value[:, z * PAIR : (z + 1) * PAIR]

    @pl.when(slot % 2 == 0)
    def _():
        put(keep_ref)

    @pl.when(slot % 2 == 1)
    def _():
        put(send_ref)


def cross_weights_kernel(copies, info, h_low, dq_ref, mem_own, mem_mate, dk_ref, dv_ref, dbr_ref, att_ref, keep, send):
    me = info[1, 11]
    half = mem_own.shape[0]


    put_matrix(keep, send, me, 0, dg(h_low[...], dq_ref[...], 0, 0).astype(BF))
    for which, ref in ((1, dk_ref), (2, dv_ref)):
        value = dg(mem_own[...], ref[:half], 0, 0) + dg(mem_mate[...], ref[half:], 0, 0)
        put_matrix(keep, send, me, which, value.astype(BF))
    put_matrix(keep, send, me, 3, dg(dbr_ref[...], att_ref[...], 0, 0).astype(BF))


def ffn_backward_part(low, dbr, acc, units, target):
    for i in range(units.shape[0] // 2):
        y, z = i // 2, i % 2
        wu = unit_block(units, 0, i)
        wd = unit_block(units, 1, i)
        u_t = dg(wu, low, 1, 1)
        act_t, sg = silu_parts(u_t)
        act_t = act_t.astype(BF)
        dact_t = dg(wd, dbr, 1, 1)
        du_t = (dact_t * sg * (1.0 + u_t * (1.0 - sg))).astype(BF)
        acc = acc + dg(du_t, wu, 0, 0)
        dup = dg(du_t, low, 1, 0).astype(BF)
        ddown = dg(act_t, dbr, 1, 0).astype(BF)
        for j in range(2):
            target[y, 2 * z + j, 0] = dup[j * PAIR : (j + 1) * PAIR]
            target[y, 2 * z + j, 1] = ddown[j * PAIR : (j + 1) * PAIR]
    return acc


def ffn_backward_mate_kernel(copies, info, x_ref, n3_ref, inv3_ref, cot0, cot1, dmem_ref, gain3, *refs):
    send, acc_out, dbr_out, dnorm_out, units = refs[5:]
    started = load_units(copies, info[0, 11], refs[:5], units, (1, 3))
    dy = jnp.concatenate([cot0[...], cot1[...]], axis=0).astype(F32) + dmem_ref[...].astype(F32)
    dr3, dg3, db3 = norm_bwd(dy, n3_ref[...], inv3_ref[:, 0:1], gain3[...])
    dnorm_out[0:1] = dg3
    dnorm_out[1:2] = db3
    dbr = dr3.astype(BF)
    dbr_out[...] = dbr
    wait_all(started)
    acc_out[...] = ffn_backward_part(x_ref[...], dbr, dr3, units, send)


def ffn_backward_own_kernel(copies, info, x_ref, dbr_ref, acc_ref, n1_ref, inv1_ref, gain1, dmid_ref, *refs):
    do_out, keep, dr1_out, dbr1_out, dnorm_out, units, wall = refs[10:]
    me = info[0, 11]
    started = load_units(copies, me, refs[:5], units, (0, 2))
    wall_started = load_wall(copies, me, refs[5:10], wall)
    wait_all(started)
    acc = ffn_backward_part(x_ref[...], dbr_ref[...], acc_ref[...], units, keep)
    dmid = jnp.where(info[0, 12] == 1, dmid_ref[...], acc)
    dr1, dg1, db1 = norm_bwd(dmid, n1_ref[...], inv1_ref[:, 0:1], gain1[...])
    dr1_out[...] = dr1
    dbr1 = dr1.astype(BF)
    dbr1_out[...] = dbr1
    dnorm_out[0:1] = dg1
    dnorm_out[1:2] = db1
    wait_all(wall_started)
    do_out[...] = dg(dbr1, wall[me ^ 3], 1, 0).astype(BF)


def self_backward_kernel(first, copies, info, q, k, v, att, do, lse, dq_out, own, mate, bias_ref, q_ref, k_ref, v_ref, do_ref, att_ref, rd_ref, dk_ref, dv_ref):
    width = q_ref.shape[1]
    columns = pl.ds(first * PAIR, width)
    started = [copies.start(src.at[:, columns], dst) for src, dst in ((q, q_ref), (k, k_ref), (v, v_ref), (att, att_ref))]
    bias_ref[...] = mask_bias(info, 0, q_ref.shape[0], k_ref.shape[0], 1)
    do_ref[...] = do[:, columns]
    wait_all(started)
    lse_ref = lse.at[pl.ds(2 * first, 2 * width // PAIR)]
    attend_backward(info, 0, width // PAIR, q_ref, k_ref, v_ref, do_ref, att_ref, lse_ref, bias_ref, rd_ref, dq_out, dk_ref, dv_ref)
    half = q_ref.shape[0]
    for dst, at in ((mate, half), (own, 0)):
        dst[0] = dk_ref[at : at + half]
        dst[1] = dv_ref[at : at + half]


def head_sums(own_a, own_b, got_a, got_b, i):
    parts = [(own[i].astype(F32) + got[i].astype(F32)).astype(BF) for own, got in ((own_a, got_a), (own_b, got_b))]
    return jnp.concatenate(parts, axis=1)


def self_weights_kernel(copies, info, x0, x1, dq_a, dq_b, own_a, own_b, got_a, got_b, att_ref, dbr_ref, dnorm1, dnorm2, dnorm3, keep, send, dk_out, dv_out):
    me = info[0, 11]
    dq = jnp.concatenate([dq_a[...], dq_b[...]], axis=1)
    dk = head_sums(own_a, own_b, got_a, got_b, 0)
    dv = head_sums(own_a, own_b, got_a, got_b, 1)
    dk_out[...] = dk
    dv_out[...] = dv
    x = jnp.concatenate([x0[...], x1[...]], axis=0)
    for which, value in ((0, dq), (1, dk), (2, dv)):
        put_matrix(keep, send, me, which, dg(x, value, 0, 0).astype(BF))
    put_matrix(keep, send, me, 3, dg(dbr_ref[...], att_ref[...], 0, 0).astype(BF))
    feat = dq.shape[1]
    norms = jnp.concatenate([dnorm1[0:1], dnorm3[0:1], dnorm1[1:2], dnorm3[1:2], dnorm2[0:2], jnp.zeros((2, feat), F32)], axis=0)
    rows = jnp.concatenate([norms[:, i * PAIR : (i + 1) * PAIR] for i in range(feat // PAIR)], axis=0).astype(BF)
    for out in (keep, send):
        for y in range(2):
            for z in range(4):
                out[y, z, feat:] = rows


def input_backward_kernel(copies, info, dq_a, dq_b, dk_ref, dv_ref, dr_ref, *refs):
    dx0, dx1, wall = refs[5:]
    me = info[0, 11]
    started = load_wall(copies, me, refs[:5], wall)
    dq = jnp.concatenate([dq_a[...], dq_b[...]], axis=1)
    wait_all(started)
    dx = dr_ref[...] + dg(dq, wall[me], 1, 1) + dg(dk_ref[...], wall[me ^ 1], 1, 1) + dg(dv_ref[...], wall[me ^ 2], 1, 1)
    half = dx0.shape[0]
    dx0[...] = dx[:half].astype(BF)
    dx1[...] = dx[half:].astype(BF)


US = {
    "self_forward_kernel": 13.5, "ffn_forward_kernel": 4.5, "cross_forward_kernel": 13.5, "decoder_kernel": 23.0,
    "cross_weights_kernel": 3.7, "ffn_backward_mate_kernel": 6.0, "ffn_backward_own_kernel": 6.7,
    "self_backward_kernel": 7.5, "self_weights_kernel": 3.5, "input_backward_kernel": 2.0,
}


def call(kernel, outs, args, scratch=(), vmem=60):
    in_hbm = pl.BlockSpec(memory_space=pltpu.HBM)
    in_vmem = pl.BlockSpec(memory_space=pltpu.VMEM)
    in_smem = pl.BlockSpec(memory_space=pltpu.SMEM)
    us = 0.01 * US[getattr(kernel, "func", kernel).__name__]
    arrays = [a.value if isinstance(a, Raw) else a for a in args]
    shapes = [o.value if isinstance(o, Raw) else o for o in outs]
    moved = [pltpu.VMEM(a.value.shape, a.value.dtype) for a in args if isinstance(a, Fetch)]
    moved += [pltpu.VMEM(*o.value) for o in outs if isinstance(o, Late)]

    def wrapped(*refs):
        ins, refs = refs[: len(arrays)], refs[len(arrays) :]
        results, refs = refs[: len(shapes)], refs[len(shapes) :]
        buffers, rest, sems = list(refs[: len(moved)]), refs[len(moved) : -1], refs[-1]
        copies = Copies(sems)
        given = []
        for ref, arg in zip(ins, args):
            if isinstance(arg, Fetch):
                buffer = buffers.pop(0)
                ref = Fetched(copies.start(ref, buffer), buffer)
            given.append(ref)
        produced = []
        for ref, out in zip(results, outs):
            produced.append(Result(copies, buffers.pop(0), ref) if isinstance(out, Late) else ref)
        kernel(copies, *given, *produced, *rest)
        for ref in given:
            if isinstance(ref, Fetched):
                ref.ready()
        for out in produced:
            if isinstance(out, Result):
                out.flush()
        for out in produced:
            if isinstance(out, Result):
                out.copy.wait()

    return pl.pallas_call(
        wrapped,
        out_shape=tuple(jax.ShapeDtypeStruct(*o) for o in shapes),
        in_specs=[
            in_hbm if isinstance(a, Raw) else in_smem if a.dtype == jnp.int32 else in_vmem for a in args
        ],
        out_specs=tuple(in_hbm if isinstance(o, Raw) else in_vmem for o in outs),
        scratch_shapes=[*moved, *scratch, pltpu.SemaphoreType.DMA((64,))],
        compiler_params=pltpu.CompilerParams(vmem_limit_bytes=vmem * MIB),
        cost_estimate=pl.CostEstimate(flops=int(us * 1e9), bytes_accessed=int(us * 2e6), transcendentals=0),
    )(*arrays)


def body(
    inputs,
    cotangent,
    lengths,
    row_flags,
    qkv_w,
    out_w,
    cross_w,
    up_w,
    down_w,
    norm_gain,
    norm_bias,
    cross_gain,
    cross_bias,
):
    section = lax.axis_index("section")
    is_dec = section == 1
    d = lax.axis_index("dp")
    t = lax.axis_index("tensor")
    core = d % 2
    me = d % 4
    feat = inputs.shape[3]
    chunk = inputs.shape[2]
    half = 2 * chunk
    row_len = 2 * half
    quarter = qkv_w.shape[3]
    n_t = 4

    attn_local = jnp.concatenate([qkv_w[0], out_w[0].T[None]], axis=0)
    piece = jnp.where(me == 3, out_w[0].T, lax.dynamic_index_in_dim(qkv_w[0], jnp.minimum(me, 2), 0, False))
    attn_z = z_pieces(piece)
    got = [deal(lax.dynamic_index_in_dim(inputs[0], (t + k) % 2, 0, False), k) for k in range(2)]
    unit_quarter = up_w.shape[2] // 4
    ffn_local = jnp.stack([up_w[0].T.reshape(4, unit_quarter, feat), down_w[0].reshape(4, unit_quarter, feat)], axis=1)
    cross_other = to_decoder(after(cross_w[0], attn_z))
    cross_local = jnp.stack([cross_w[0, 0], cross_other[0], cross_other[1], cross_w[0, 1]])
    cross_piece = lax.dynamic_index_in_dim(cross_local, me, 0, False)

    own_info = jnp.concatenate(
        [lengths[0], lengths[1], row_flags[:, None], jnp.zeros((2, 7), jnp.int32)], axis=1
    ).astype(F32)
    mate_info = swap_dp(own_info, 1)
    row_info = jnp.where(t // 2 == core, own_info, mate_info)
    row_info = lax.dynamic_index_in_dim(row_info, t % 2, 0, False).astype(jnp.int32)
    flip = core * half + (t % 2) * chunk
    src_lens = row_info[0:8]
    dec_int = is_dec.astype(jnp.int32)

    def tail(causal):
        return jnp.stack([row_info[16], flip, causal, me, dec_int, t, 0, 0]).astype(jnp.int32)

    info = jnp.stack([
        jnp.concatenate([jnp.where(is_dec, row_info[8:16], src_lens), tail(dec_int)]),
        jnp.concatenate([src_lens, tail(0)]),
    ])

    gains = jnp.where(is_dec, norm_gain[1], norm_gain[0])
    shifts = jnp.where(is_dec, norm_bias[1], norm_bias[0])
    cgain, cshift = cross_gain[None], cross_bias[None]

    rows = (half, feat)
    full = (row_len, feat)
    column = (half, PAIR)
    wall = pltpu.VMEM((4, feat, feat), BF)
    units = pltpu.VMEM((4 * n_t, 2, unit_quarter, feat), BF)
    bias_n = pltpu.VMEM((half, row_len), F32)
    bias_t = pltpu.VMEM((row_len, half), F32)
    rd_s = pltpu.VMEM((HEADS, 1, half), F32)

    def raw(*arrays):
        return [Raw(a) for a in arrays]

    def fetch(*arrays):
        return [Fetch(a) for a in arrays]

    def late(*shapes):
        return [Late(a) for a in shapes]

    attn_zs = jnp.stack(attn_z)
    ffn_z = z_pieces(after(lax.dynamic_index_in_dim(ffn_local, me, 0, False), attn_zs))
    attn_ys, info, gains, shifts = together(swap_dp(attn_zs, 2), info, gains, shifts)
    gain1, gain3 = gains[0:1], gains[1:2]
    shift1, shift3 = shifts[0:1], shifts[1:2]
    attn_ws = raw(attn_local, attn_zs, swap_dp(attn_zs, 1), attn_ys, swap_dp(attn_ys, 1))
    mates = [swap_dp(x, 1) for x in got]
    mid, mid_low, n1, inv1, q1, k1, v1, att1, lse1 = call(
        self_forward_kernel,
        [(rows, F32), (rows, BF), *late((rows, F32)), (column, F32), (rows, BF), (full, BF), (full, BF), (rows, BF),
         ((HEADS, 1, half), F32)],
        [info, *fetch(after(got[0], cross_piece), got[1], *mates), gain1, shift1, *attn_ws], [wall, bias_n], 17,
    )
    ffn_zs = jnp.stack(after(ffn_z, mid))
    ffn_ys = swap_dp(ffn_zs, 2)
    cross_z = z_pieces(after(cross_piece, mid))
    ffn_ys, *cross_z = together(ffn_ys, *cross_z)
    ffn_ws = raw(ffn_local, ffn_zs, swap_dp(ffn_zs, 1), ffn_ys, swap_dp(ffn_ys, 1))
    cross_zs = jnp.stack(cross_z)
    cross_ys = swap_dp(cross_zs, 2)
    mem_low, n3e, inv3e = call(
        ffn_forward_kernel, [(rows, BF), (rows, F32), (column, F32)], [info, after(mid, cross_zs), gain3, shift3, *ffn_ws], [units], 8,
    )
    cross_ys = after(cross_ys, mem_low)
    mem_own, cross_zm, cross_ym = together(to_decoder(mem_low), swap_dp(cross_zs, 1), swap_dp(cross_ys, 1))
    cross_ws = raw(cross_local, cross_zs, cross_zm, cross_ys, cross_ym)
    mem_mate = swap_dp(mem_own, 1)
    cots = [deal(after(lax.dynamic_index_in_dim(cotangent[0], (t + k) % 2, 0, False), mem_own), k) for k in range(2)]
    h2, n2, inv2, q2, k2, v2, att2, lse2 = call(
        cross_forward_kernel,
        [(rows, F32), (rows, F32), (column, F32), (rows, BF), (full, BF), (full, BF), (rows, BF), ((HEADS, 1, half), F32)],
        [info, *fetch(mem_own, mem_mate), mid_low, mid, cgain, cshift, *cross_ws], [wall, bias_n], 17,
    )
    cots = after(cots, h2)
    out0, out1, ffn_x, n3, inv3, dh1, dmem_own, dmem_mate, dbr2, dq2, dk2, dv2, dnorm2 = call(
        decoder_kernel,
        [((chunk, feat), BF), ((chunk, feat), BF), (rows, BF), (rows, F32), (column, F32), (rows, F32), (rows, BF), (rows, BF),
         (rows, BF), (rows, BF), (full, BF), (full, BF), ((8, feat), F32)],
        [info, h2, *fetch(*cots), n2, inv2, cgain, gain3, shift3, q2, k2, v2, att2, lse2, mid_low, mem_low, n3e, inv3e, *cross_ws, *ffn_ws],
        [wall, units, bias_t, rd_s, pltpu.VMEM(rows, BF), pltpu.VMEM((half, 4 * n_t * unit_quarter), F32)], 30,
    )
    dmem_got = swap_dp(dmem_mate, 1)
    pieces = [((2, n_t, feat, quarter), BF)] * 2
    cross_keep, cross_send = call(
        cross_weights_kernel, pieces, [info, mid_low, dq2, mem_own, mem_mate, dk2, dv2, dbr2, att2], vmem=8,
    )
    dmem = add_low(dmem_own, after(dmem_got, cross_keep))
    dmem_enc = to_encoder(dmem)
    cross_mate = swap_dp(after(cross_send, dmem), 1)
    cross_got = swap_dp(add_low(cross_keep[1], cross_mate[1]), 2)
    dmem_enc, cross_got = together(dmem_enc, cross_got)
    cross_quarter = add_low(cross_keep[0], cross_mate[0], cross_got)

    ffn_pieces = (2, n_t, 2, unit_quarter, feat)
    half_units = pltpu.VMEM((2 * n_t, 2, unit_quarter, feat), BF)
    ffn_send, acc, dbr3, dnorm3 = call(
        ffn_backward_mate_kernel, [(ffn_pieces, BF), (rows, F32), (rows, BF), ((8, feat), F32)],
        [info, ffn_x, n3, inv3, *fetch(*cots, dmem_enc), gain3, *ffn_ws], [half_units], 10,
    )
    ffn_mate = swap_dp(ffn_send, 1)
    out_back = [deal_back(after(out, ffn_send), k) for k, out in enumerate((out0, out1))]
    do1, ffn_keep, dr1, dbr1, dnorm1 = call(
        ffn_backward_own_kernel, [(rows, BF), (ffn_pieces, BF), (rows, F32), (rows, BF), ((8, feat), F32)],
        [info, ffn_x, dbr3, acc, *fetch(n1), inv1, gain1, dh1, *ffn_ws, *attn_ws], [half_units, wall], 11,
    )
    ffn_mate = after(ffn_mate, do1)
    ffn_got = swap_dp(add_low(ffn_keep[1], ffn_mate[1]), 2)

    def self_backward(first, n_pairs, do):
        width = n_pairs * PAIR
        half_grad = ((2, half, width), BF)
        return call(
            functools.partial(self_backward_kernel, first), [((half, width), BF), half_grad, half_grad],
            [info, *raw(q1, k1, v1, att1), do, lse1],
            [bias_t, pltpu.VMEM((half, width), BF), pltpu.VMEM((row_len, width), BF), pltpu.VMEM((row_len, width), BF),
             pltpu.VMEM((half, width), BF), pltpu.VMEM((half, width), BF), rd_s,
             pltpu.VMEM((row_len, width), BF), pltpu.VMEM((row_len, width), BF)], 11,
        )

    cross_enc = cross_to_owner(after(cross_quarter, do1))
    dq_a, own_a, mate_a = self_backward(0, 2, do1)
    got_a = swap_dp(mate_a, 1)
    dq_b, own_b, mate_b = self_backward(2, 2, after(do1, dq_a, cross_enc, *out_back))
    got_b = swap_dp(mate_b, 1)
    ffn_quarter = add_low(ffn_keep[0], ffn_mate[0], after(ffn_got, dq_b))
    ffn_parts = z_parts(ffn_quarter)
    self_pieces = [((2, n_t, feat + 32, quarter), BF)] * 2
    self_keep, self_send, dk1, dv1 = call(
        self_weights_kernel, [*self_pieces, (rows, BF), (rows, BF)],
        [info, *fetch(*got), dq_a, dq_b, own_a, own_b, *fetch(after(got_a, ffn_quarter), got_b, att1), dbr1, dnorm1, dnorm2, dnorm3], vmem=10,
    )
    dx0, dx1 = call(
        input_backward_kernel, [((chunk, feat), BF), ((chunk, feat), BF)],
        [info, dq_a, dq_b, dk1, dv1, dr1, *attn_ws], [wall], 60,
    )
    self_send, dx0, dx1, *ffn_parts = together(self_send, dx0, dx1, *ffn_parts)
    ffn_back = z_sum(ffn_parts)
    self_mate = swap_dp(self_send, 1)
    dx_back = [deal_back(dx, k) for k, dx in enumerate((dx0, dx1))]
    self_got = swap_dp(add_low(self_keep[1], self_mate[1]), 2)
    ffn_y = swap_dp(after(ffn_back, self_mate), 2)
    cross_parts = cross_z_parts(after(jnp.where(is_dec, cross_quarter, cross_enc), ffn_parts[1]))
    self_got, ffn_y, *rest = together(self_got, ffn_y, *dx_back, *cross_parts)
    dx_back, cross_parts = rest[:2], rest[2:]
    cross_back = other_groups(add_low(*cross_parts))
    ffn_two = jnp.stack([ffn_back, ffn_y])
    self_parts = z_parts(add_low(self_keep[0], self_mate[0], self_got))
    cross_y, ffn_core, *self_parts = together(swap_dp(cross_back, 2), swap_dp(ffn_two, 1), *self_parts)
    self_piece = z_sum(self_parts)
    self_back = self_piece[:feat]
    norms = self_piece[feat:].astype(F32).reshape(n_t, 8, PAIR).transpose(1, 0, 2).reshape(8, feat)
    other = lax.ppermute(norms, "section", [(0, 1), (1, 0)])
    cross_two = jnp.stack([cross_back, cross_y])
    self_y, cross_core, other = together(swap_dp(self_back, 2), swap_dp(cross_two, 1), other)
    self_two = jnp.stack([self_back, self_y])
    self_core = swap_dp(self_two, 1)

    def four(two, mate):
        return jnp.stack([two[0], mate[0], two[1], mate[1]])

    ffn_sum = four(ffn_two, ffn_core)
    self_sum = four(self_two, self_core)
    cross_sum = four(cross_two, cross_core)

    def matrix(stacked, which):
        return lax.dynamic_index_in_dim(stacked, me ^ which, 0, False).astype(F32)

    qkv_grad = jnp.stack([matrix(self_sum, m) for m in range(3)])
    out_grad = matrix(self_sum, 3).T
    cross_grad = jnp.stack([
        matrix(cross_sum, jnp.where(is_dec, 0, 1)), matrix(cross_sum, jnp.where(is_dec, 3, 2))
    ])
    ffn_true = [matrix(ffn_sum, m) for m in range(4)]
    up_grad = jnp.concatenate([f[0].T for f in ffn_true], axis=1)
    down_grad = jnp.concatenate([f[1] for f in ffn_true], axis=0)

    enc = jnp.where(is_dec, other, norms)
    dec = jnp.where(is_dec, norms, other)
    full_gain = jnp.stack([enc[0:2], dec[0:2]])
    full_bias = jnp.stack([enc[2:4], dec[2:4]])

    def in_order(back):
        even = t % 2 == 0
        return jnp.stack([jnp.where(even, back[0], back[1]), jnp.where(even, back[1], back[0])])

    out_rows = in_order(out_back)
    grad_rows = in_order(dx_back).astype(F32)
    return (
        out_rows[None],
        grad_rows[None],
        qkv_grad[None],
        out_grad[None],
        cross_grad[None],
        up_grad[None],
        down_grad[None],
        full_gain,
        full_bias,
        dec[4],
        dec[5],
    )


def solution(mesh):
    return jax.shard_map(
        body,
        mesh=mesh,
        in_specs=(
            P("section", "dp", "tensor", None),
            P("section", "dp", "tensor", None),
            P(None, "dp", None),
            P("dp"),
            P("section", None, None, "tensor"),
            P("section", "tensor", None),
            P("section", None, None, "tensor"),
            P("section", None, "tensor"),
            P("section", "tensor", None),
            P(),
            P(),
            P(),
            P(),
        ),
        out_specs=(
            P("section", "dp", "tensor", None),
            P("section", "dp", "tensor", None),
            P("section", None, None, "tensor"),
            P("section", "tensor", None),
            P("section", None, None, "tensor"),
            P("section", None, "tensor"),
            P("section", "tensor", None),
            P(),
            P(),
            P(),
            P(),
        ),
        check_vma=False,
    )
```

```python
import functools

import jax
import jax.numpy as jnp
from jax import lax
from jax.experimental import pallas as pl
from jax.experimental.pallas import tpu as pltpu
from jax.sharding import PartitionSpec as P

HEADS = 8
HD = 64
PAIR = 2 * HD
SLOT_BITS = 7
SLOTS = 8
NEG = -1e30
EPS = 1e-05
SCALE = HD ** -0.5
BF = jnp.bfloat16
F32 = jnp.float32
MIB = 1024 * 1024


def swap_dp(x, bit):
    n = lax.axis_size("dp")
    return lax.ppermute(x, "dp", [(i, i ^ bit) for i in range(n)])


def shift_tensor(x, step):
    n = lax.axis_size("tensor")
    return lax.ppermute(x, "tensor", [(i, (i + step) % n) for i in range(n)])


def swap_tensor(x, bit):
    n = lax.axis_size("tensor")
    return lax.ppermute(x, "tensor", [(i, i ^ bit) for i in range(n)])


def to_decoder(x):
    return lax.ppermute(x, "section", [(0, 1)])


def to_encoder(x):
    return lax.ppermute(x, "section", [(1, 0)])


def deal_route(k):
    n_t = lax.axis_size("tensor")
    route = []
    for d in range(lax.axis_size("dp")):
        group, core = divmod(d, 2)
        for t in range(n_t):
            plane = 2 * core + (t + k) % 2
            route.append((d * n_t + t, (2 * group + t // 2) * n_t + plane))
    return route


def deal(x, k):
    return lax.ppermute(x, ("dp", "tensor"), deal_route(k))


def deal_back(x, k):
    return lax.ppermute(x, ("dp", "tensor"), [(b, a) for a, b in deal_route(k)])


def together(*xs):
    return lax.optimization_barrier(xs)


def after(x, *events):
    return lax.optimization_barrier((x, *events))[0]


def z_pieces(piece):
    return [shift_tensor(piece, r) for r in range(1, 4)]


def add_low(*parts):
    return sum(p.astype(F32) for p in parts).astype(BF)


def other_groups(total):
    bit = 4
    while bit < lax.axis_size("dp"):
        total = add_low(total, swap_dp(total, bit))
        bit *= 2
    return total


def z_parts(quarter):
    return [quarter[0]] + [shift_tensor(quarter[r], -r) for r in range(1, 4)]


def z_sum(parts):
    return other_groups(add_low(*parts))


def dg(a, b, ca, cb):
    return lax.dot_general(a, b, (((ca,), (cb,)), ((), ())), preferred_element_type=F32)


def norm_fwd(r):
    off = r - jnp.mean(r, axis=-1, keepdims=True)
    inv = lax.rsqrt(jnp.mean(off * off, axis=-1, keepdims=True) + EPS)
    return off * inv, inv


def norm_bwd(dy, n, inv, gain):
    sc = dy * gain
    dr = inv * (
        sc
        - jnp.mean(sc, axis=-1, keepdims=True)
        - n * jnp.mean(sc * n, axis=-1, keepdims=True)
    )
    return dr, jnp.sum(dy * n, axis=0, keepdims=True), jnp.sum(dy, axis=0, keepdims=True)


def head_lanes(h):
    return (lax.broadcasted_iota(jnp.int32, (1, PAIR), 1) // HD) == h


def mask_bias(info, row, n_q, n_k, q_axis):
    flip = info[row, 9]
    q_shape = (n_q, 1) if q_axis == 0 else (1, n_q)
    full = (n_q, n_k) if q_axis == 0 else (n_k, n_q)
    q_pos = lax.broadcasted_iota(jnp.int32, q_shape, q_axis) ^ flip
    seg = jnp.where(info[row, 8] == 1, 0, q_pos >> SLOT_BITS)
    size = jnp.zeros(q_shape, jnp.int32)
    for j in range(SLOTS):
        size = size + jnp.where(seg == j, info[row, j], 0)
    first = seg << SLOT_BITS
    end = first + size
    end = jnp.where(info[row, 10] == 1, jnp.minimum(end, q_pos + 1), end)
    k_pos = lax.broadcasted_iota(jnp.int32, full, 1 - q_axis) ^ flip
    return jnp.where((k_pos >= first) & (k_pos < end), 0.0, NEG)


class Copies:
    def __init__(self, sems):
        self.sems = sems
        self.count = 0

    def start(self, src, dst):
        copy = pltpu.make_async_copy(src, dst, self.sems.at[self.count])
        self.count += 1
        copy.start()
        return copy


class Raw:
    def __init__(self, value):
        self.value = value


class Fetch(Raw):
    pass


class Late(Raw):
    pass


class Fetched:
    def __init__(self, copy, ref):
        self.copy = copy
        self.ref = ref
        self.shape = ref.shape

    def ready(self):
        if self.copy is not None:
            self.copy.wait()
            self.copy = None
        return self.ref

    def __getitem__(self, at):
        return self.ready()[at]


class Result:
    def __init__(self, copies, ref, dst):
        self.copies = copies
        self.ref = ref
        self.dst = dst
        self.shape = ref.shape
        self.copy = None

    def __setitem__(self, at, value):
        self.ref[at] = value

    def __getitem__(self, at):
        return self.ref[at]

    def flush(self):
        if self.copy is None:
            self.copy = self.copies.start(self.ref, self.dst)


def load_wall(copies, me, refs, wall):
    local, *pieces = refs
    started = []
    for rel, ref in enumerate(pieces):
        started.append(copies.start(local.at[me ^ rel], wall.at[rel, :, pl.ds(0, PAIR)]))
        for z in range(1, 4):
            started.append(copies.start(ref.at[z - 1], wall.at[rel, :, pl.ds(z * PAIR, PAIR)]))
    return started


def load_units(copies, me, refs, units, rels=range(4)):
    local, *pieces = refs
    started = []
    for i, rel in enumerate(rels):
        started.append(copies.start(local.at[me ^ rel], units.at[4 * i]))
        started.append(copies.start(pieces[rel], units.at[pl.ds(4 * i + 1, 3)]))
    return started


def wait_all(started):
    for copy in started:
        copy.wait()


def unit_block(units, which, i):
    return jnp.concatenate([units[2 * i, which], units[2 * i + 1, which]], axis=0)


def mask_columns(info, row, n, of_queries):
    pos = lax.broadcasted_iota(jnp.int32, (n, 1), 0) ^ info[row, 9]
    seg = jnp.where(info[row, 8] == 1, 0, pos >> SLOT_BITS)
    lane = lax.broadcasted_iota(jnp.int32, (1, PAIR), 1) % HD
    if of_queries:
        return jnp.where(lane == seg, 1.0, 0.0).astype(BF)
    size = jnp.zeros((n, 1), jnp.int32)
    for j in range(SLOTS):
        size = size + jnp.where(seg == j, info[row, j], 0)
    counts = (lane == seg) & (pos - (seg << SLOT_BITS) < size)
    return jnp.where(lane < SLOTS, jnp.where(counts, 0.0, NEG), 0.0).astype(BF)


def attend_forward(info, row, q_ref, k_ref, v_ref, att_ref, lse_ref, qm_ref, km_ref, bias_ref=None):
    n_q = q_ref.shape[0]
    lane = lax.broadcasted_iota(jnp.int32, (1, PAIR), 1)

    def heads(causal):
        qm_ref[...] = mask_columns(info, row, n_q, True)
        km_ref[...] = mask_columns(info, row, k_ref.shape[0], False)
        if causal:
            bias_ref[...] = mask_bias(info, row, n_q, k_ref.shape[0], 0)
        lse = jnp.zeros((n_q, PAIR), F32)
        for hp in range(HEADS // 2):
            sl = slice(hp * PAIR, (hp + 1) * PAIR)
            qp, kp, vp = q_ref[:, sl], k_ref[:, sl], v_ref[:, sl]
            outs = []
            for h in range(2):
                own = head_lanes(h)
                s = dg(jnp.where(own, qp, qm_ref[...]), jnp.where(own, kp, km_ref[...]), 1, 1)
                if causal:
                    s = s + bias_ref[...]
                top = jnp.max(s, axis=1, keepdims=True)
                e = jnp.exp(s - top).astype(BF)
                o = dg(e, jnp.where(own, vp, jnp.ones_like(vp)), 1, 0)
                at = (1 - h) * HD
                total = o[:, at : at + 1]
                outs.append(o * (1.0 / total))
                lse = jnp.where(lane == 2 * hp + h, top + jnp.log(total), lse)
            att_ref[:, sl] = jnp.where(head_lanes(0), outs[0], outs[1]).astype(BF)
        rows = jnp.transpose(lse)
        for h in range(HEADS):
            lse_ref[h] = rows[h : h + 1]

    if bias_ref is None:
        heads(False)
    else:
        pl.when(info[row, 10] == 1)(lambda: heads(True))
        pl.when(info[row, 10] != 1)(lambda: heads(False))


def attend_backward(info, row, n_pairs, q_ref, k_ref, v_ref, do_ref, att_ref, lse_ref, bias_ref, rd_ref, dq_ref, dk_ref, dv_ref):
    n_q = q_ref.shape[0]
    block = 256
    empty = info[row, 0]
    for j in range(1, SLOTS):
        empty = empty + info[row, j]
    empty = empty == 0
    p_fix = jnp.where(empty, 1.0 / k_ref.shape[0], 1.0)
    s_fix = jnp.where(empty, 0.0, 1.0)
    width = n_pairs * PAIR
    prod = do_ref[...].astype(F32) * att_ref[...].astype(F32)
    high = prod.astype(BF)
    low = (prod - high.astype(F32)).astype(BF)
    heads = lax.broadcasted_iota(jnp.int32, (HEADS, width), 0)
    lanes_of = lax.broadcasted_iota(jnp.int32, (HEADS, width), 1) // HD
    ones = jnp.where(heads == lanes_of, 1.0, 0.0).astype(BF)
    rd = dg(ones, high, 1, 1) + dg(ones, low, 1, 1)
    for h in range(2 * n_pairs):
        rd_ref[h] = rd[h : h + 1]

    def pair(hp, _):
        sl = pl.ds(pl.multiple_of(hp * PAIR, PAIR), PAIR)
        kp = k_ref[:, sl]
        vp = v_ref[:, sl]
        k_t = jnp.transpose(kp)
        dk = dv = None
        for qi in range(n_q // block):
            qs = slice(qi * block, (qi + 1) * block)
            qp = q_ref[qs, sl]
            dop = do_ref[qs, sl]
            dqs = []
            for h in range(2):
                lanes = head_lanes(h)
                qm = jnp.where(lanes, qp, jnp.zeros_like(qp))
                dom = jnp.where(lanes, dop, jnp.zeros_like(dop))
                s = dg(kp, qm, 1, 1) + bias_ref[:, qs]
                p = jnp.exp(s - lse_ref[hp * 2 + h, :, qs])
                dp = dg(vp, dom, 1, 1)
                ds = (p * (dp - rd_ref[hp * 2 + h, :, qs])).astype(BF)
                a = dg(p.astype(BF), dom, 1, 0)
                dv = a if dv is None else dv + a
                a = dg(ds, qm, 1, 0)
                dk = a if dk is None else dk + a
                dqs.append(dg(k_t[h * HD : (h + 1) * HD], ds, 1, 0))
            dq = jnp.transpose(jnp.concatenate(dqs, axis=0))
            dq_ref[qs, sl] = (dq * (SCALE * s_fix)).astype(BF)
        dk_ref[:, sl] = (dk * s_fix).astype(BF)
        dv_ref[:, sl] = (dv * p_fix).astype(BF)
        return 0

    lax.fori_loop(0, n_pairs, pair, 0)


def self_forward_kernel(copies, info, x0, x1, x2, x3, gain, shift, *refs):
    w_refs = refs[:5]
    y_out, low_out, n_out, inv_out, q_out, k_out, v_out, att_out, lse_out, wall, qm_ref, km_ref, bias_ref = refs[5:]
    me = info[0, 11]
    started = load_wall(copies, me, w_refs, wall)
    wait_all(started)
    rows_low = jnp.concatenate([x0[...], x1[...]], axis=0)
    q_out[...] = dg(rows_low, wall[me], 1, 0).astype(BF) * jnp.asarray(SCALE, BF)
    wk = wall[me ^ 1]
    wv = wall[me ^ 2]
    at = 0
    for ref in (x0, x1, x2, x3):
        part = ref[...]
        k_out[at : at + ref.shape[0]] = dg(part, wk, 1, 0).astype(BF)
        v_out[at : at + ref.shape[0]] = dg(part, wv, 1, 0).astype(BF)
        at += ref.shape[0]
    attend_forward(info, 0, q_out, k_out, v_out, att_out, lse_out, qm_ref, km_ref, bias_ref)
    n, inv = norm_fwd(rows_low.astype(F32) + dg(att_out[...], wall[me ^ 3], 1, 1))
    n_out[...] = n
    inv_out[...] = jnp.broadcast_to(inv, inv_out.shape)
    y = n * gain[...] + shift[...]
    y_out[...] = y
    low_out[...] = y.astype(BF)


def silu_parts(u):
    sg = jax.nn.sigmoid(u)
    return u * sg, sg


def ffn_forward_kernel(copies, info, x_ref, gain, shift, *refs):
    low_out, n_out, inv_out, units = refs[5:]
    started = load_units(copies, info[0, 11], refs[:5], units)
    x = x_ref[...]
    low = x.astype(BF)
    acc = x
    wait_all(started)
    for i in range(units.shape[0] // 2):
        u = dg(low, unit_block(units, 0, i), 1, 1)
        act = silu_parts(u)[0].astype(BF)
        acc = acc + dg(act, unit_block(units, 1, i), 1, 0)
    n, inv = norm_fwd(acc)
    low_out[...] = (n * gain[...] + shift[...]).astype(BF)
    n_out[...] = n
    inv_out[...] = jnp.broadcast_to(inv, inv_out.shape)


def cross_forward_kernel(copies, info, mem_own, mem_mate, h_low, h_ref, cgain, cshift, *refs):
    y_out, n_out, inv_out, q_out, k_out, v_out, att_out, lse_out, wall, qm_ref, km_ref = refs[5:]
    me = info[1, 11]
    started = load_wall(copies, me, refs[:5], wall)
    wait_all(started)
    q_out[...] = dg(h_low[...], wall[me], 1, 0).astype(BF) * jnp.asarray(SCALE, BF)
    half = mem_own.shape[0]
    for ref, at in ((mem_own, 0), (mem_mate, half)):
        k_out[at : at + half] = dg(ref[...], wall[me ^ 1], 1, 0).astype(BF)
        v_out[at : at + half] = dg(ref[...], wall[me ^ 2], 1, 0).astype(BF)
    attend_forward(info, 1, q_out, k_out, v_out, att_out, lse_out, qm_ref, km_ref)
    n, inv = norm_fwd(h_ref[...] + dg(att_out[...], wall[me ^ 3], 1, 1))
    n_out[...] = n
    inv_out[...] = jnp.broadcast_to(inv, inv_out.shape)
    y_out[...] = n * cgain[...] + cshift[...]


def decoder_kernel(copies, info, h_ref, cot0, cot1, n2_ref, inv2_ref, cgain, gain3, shift3, q_ref, k_ref, v_ref, att_ref, lse_ref,
                   h_low, mem_low, n3e, inv3e, *refs):
    w_refs, unit_refs = refs[:5], refs[5:10]
    (out0, out1, x_ref, n3_ref, inv3_ref, dh_out, dmem_own_out, dmem_mate_out, dbr_out, dq_out, dk_out, dv_out, dnorm_out,
     wall, units, bias_ref, rd_ref, do_ref, u_ref) = refs[10:]
    me = info[1, 11]
    dec = info[1, 12] == 1
    started = load_units(copies, me, unit_refs, units)
    wall_started = load_wall(copies, me, w_refs, wall)
    bias_ref[...] = mask_bias(info, 1, q_ref.shape[0], k_ref.shape[0], 1)
    acc = h_ref[...]
    low = acc.astype(BF)
    x_ref[...] = low
    wait_all(started)
    width = 2 * PAIR
    blocks = units.shape[0] // 2
    for i in range(blocks):
        u = dg(low, unit_block(units, 0, i), 1, 1)
        u_ref[:, i * width : (i + 1) * width] = u
        act = silu_parts(u)[0].astype(BF)
        acc = acc + dg(act, unit_block(units, 1, i), 1, 0)
    n, inv = norm_fwd(acc)
    y = (n * gain3[...] + shift3[...]).astype(BF)
    half = out0.shape[0]
    out0[...] = y[:half]
    out1[...] = y[half:]
    n3_ref[...] = n
    inv3_ref[...] = jnp.broadcast_to(inv, inv3_ref.shape)
    passed = ((out0, mem_low[:half]), (out1, mem_low[half:]), (x_ref, h_low[...]), (n3_ref, n3e[...]), (inv3_ref, inv3e[...]))
    for ref, src in passed:
        ref[...] = jnp.where(dec, ref[...], src)
    cot = jnp.concatenate([cot0[...], cot1[...]], axis=0).astype(F32)
    dr, _, _ = norm_bwd(cot, n, inv, gain3[...])
    dbr = dr.astype(BF)
    acc = dr
    for i in range(blocks):
        u = u_ref[:, i * width : (i + 1) * width]
        sg = jax.nn.sigmoid(u)
        dact = dg(dbr, unit_block(units, 1, i), 1, 1)
        du = (dact * sg * (1.0 + u * (1.0 - sg))).astype(BF)
        acc = acc + dg(du, unit_block(units, 0, i), 1, 0)
    dr, dg_sum, db_sum = norm_bwd(acc, n2_ref[...], inv2_ref[:, 0:1], cgain[...])
    dnorm_out[0:1] = dg_sum
    dnorm_out[1:2] = db_sum
    dh_out[...] = dr
    dbr = dr.astype(BF)
    dbr_out[...] = dbr
    wait_all(wall_started)
    do_ref[...] = dg(dbr, wall[me ^ 3], 1, 0).astype(BF)
    attend_backward(info, 1, HEADS // 2, q_ref, k_ref, v_ref, do_ref, att_ref, lse_ref, bias_ref, rd_ref, dq_out, dk_out, dv_out)
    half = dmem_own_out.shape[0]
    wk = wall[me ^ 1]
    wv = wall[me ^ 2]
    for out, at in ((dmem_mate_out, half), (dmem_own_out, 0)):
        part = dg(dk_out[at : at + half], wk, 1, 1) + dg(dv_out[at : at + half], wv, 1, 1)
        out[...] = part.astype(BF)
    dh_out[...] = dh_out[...] + dg(dq_out[...], wall[me], 1, 1)


def put_matrix(keep_ref, send_ref, me, which, value):
    slot = me ^ which
    y = slot >> 1

    def put(ref):
        for z in range(4):
            ref[y, z, : value.shape[0]] = value[:, z * PAIR : (z + 1) * PAIR]

    @pl.when(slot % 2 == 0)
    def _():
        put(keep_ref)

    @pl.when(slot % 2 == 1)
    def _():
        put(send_ref)


def cross_weights_kernel(copies, info, h_low, dq_ref, mem_own, mem_mate, dk_ref, dv_ref, dbr_ref, att_ref, keep, send):
    me = info[1, 11]
    half = mem_own.shape[0]


    put_matrix(keep, send, me, 0, dg(h_low[...], dq_ref[...], 0, 0).astype(BF))
    for which, ref in ((1, dk_ref), (2, dv_ref)):
        value = dg(mem_own[...], ref[:half], 0, 0) + dg(mem_mate[...], ref[half:], 0, 0)
        put_matrix(keep, send, me, which, value.astype(BF))
    put_matrix(keep, send, me, 3, dg(dbr_ref[...], att_ref[...], 0, 0).astype(BF))


def ffn_backward_part(low, dbr, acc, units, up_grad, down_grad):
    for i in range(units.shape[0] // 2):
        y, z = i // 2, i % 2
        wu = unit_block(units, 0, i)
        wd = unit_block(units, 1, i)
        u_t = dg(wu, low, 1, 1)
        act_t, sg = silu_parts(u_t)
        act_t = act_t.astype(BF)
        dact_t = dg(wd, dbr, 1, 1)
        du_t = (dact_t * sg * (1.0 + u_t * (1.0 - sg))).astype(BF)
        acc = acc + dg(du_t, wu, 0, 0)
        dup = dg(du_t, low, 1, 0).astype(BF)
        ddown = dg(act_t, dbr, 1, 0).astype(BF)
        for j in range(2):
            up_grad[y, 2 * z + j] = dup[j * PAIR : (j + 1) * PAIR]
            down_grad[y, 2 * z + j] = ddown[j * PAIR : (j + 1) * PAIR]
    return acc


def ffn_backward_mate_kernel(copies, info, x_ref, n3_ref, inv3_ref, cot0, cot1, dmem_ref, gain3, *refs):
    up_send, down_send, acc_out, dbr_out, dnorm_out, units = refs[5:]
    started = load_units(copies, info[0, 11], refs[:5], units, (1, 3))
    dy = jnp.concatenate([cot0[...], cot1[...]], axis=0).astype(F32) + dmem_ref[...].astype(F32)
    dr3, dg3, db3 = norm_bwd(dy, n3_ref[...], inv3_ref[:, 0:1], gain3[...])
    dnorm_out[0:1] = dg3
    dnorm_out[1:2] = db3
    dbr = dr3.astype(BF)
    dbr_out[...] = dbr
    wait_all(started)
    acc_out[...] = ffn_backward_part(x_ref[...], dbr, dr3, units, up_send, down_send)


def ffn_backward_own_kernel(copies, info, x_ref, dbr_ref, acc_ref, n1_ref, inv1_ref, gain1, dmid_ref, *refs):
    do_out, up_keep, down_keep, dr1_out, dbr1_out, dnorm_out, units, wall = refs[10:]
    me = info[0, 11]
    started = load_units(copies, me, refs[:5], units, (0, 2))
    wall_started = load_wall(copies, me, refs[5:10], wall)
    wait_all(started)
    acc = ffn_backward_part(x_ref[...], dbr_ref[...], acc_ref[...], units, up_keep, down_keep)
    dmid = jnp.where(info[0, 12] == 1, dmid_ref[...], acc)
    dr1, dg1, db1 = norm_bwd(dmid, n1_ref[...], inv1_ref[:, 0:1], gain1[...])
    dr1_out[...] = dr1
    dbr1 = dr1.astype(BF)
    dbr1_out[...] = dbr1
    dnorm_out[0:1] = dg1
    dnorm_out[1:2] = db1
    wait_all(wall_started)
    do_out[...] = dg(dbr1, wall[me ^ 3], 1, 0).astype(BF)


def self_backward_kernel(copies, info, q_ref, k_ref, v_ref, att_ref, do_ref, lse_ref, dq_out, own, mate, bias_ref, rd_ref, dk_ref, dv_ref):
    bias_ref[...] = mask_bias(info, 0, q_ref.shape[0], k_ref.shape[0], 1)
    q, k, v, att = q_ref.ready(), k_ref.ready(), v_ref.ready(), att_ref.ready()
    attend_backward(info, 0, HEADS // 2, q, k, v, do_ref, att, lse_ref, bias_ref, rd_ref, dq_out, dk_ref, dv_ref)
    half = q_ref.shape[0]
    for dst, at in ((mate, half), (own, 0)):
        dst[0] = dk_ref[at : at + half]
        dst[1] = dv_ref[at : at + half]


def self_weights_kernel(copies, info, x0, x1, dq_ref, own, got, att_ref, dbr_ref, dnorm1, dnorm2, dnorm3, keep, send, dk_out, dv_out):
    me = info[0, 11]
    dq = dq_ref[...]
    dk = (own[0].astype(F32) + got[0].astype(F32)).astype(BF)
    dv = (own[1].astype(F32) + got[1].astype(F32)).astype(BF)
    dk_out[...] = dk
    dv_out[...] = dv
    x = jnp.concatenate([x0[...], x1[...]], axis=0)
    for which, value in ((0, dq), (1, dk), (2, dv)):
        put_matrix(keep, send, me, which, dg(x, value, 0, 0).astype(BF))
    put_matrix(keep, send, me, 3, dg(dbr_ref[...], att_ref[...], 0, 0).astype(BF))
    feat = dq.shape[1]
    norms = jnp.concatenate([dnorm1[0:1], dnorm3[0:1], dnorm1[1:2], dnorm3[1:2], dnorm2[0:2], jnp.zeros((2, feat), F32)], axis=0)
    rows = jnp.concatenate([norms[:, i * PAIR : (i + 1) * PAIR] for i in range(feat // PAIR)], axis=0).astype(BF)
    for out in (keep, send):
        for y in range(2):
            for z in range(4):
                out[y, z, feat:] = rows


def input_backward_kernel(copies, info, dq_ref, dk_ref, dv_ref, dr_ref, *refs):
    dx0, dx1, wall = refs[5:]
    me = info[0, 11]
    started = load_wall(copies, me, refs[:5], wall)
    wait_all(started)
    dx = dr_ref[...] + dg(dq_ref[...], wall[me], 1, 1) + dg(dk_ref[...], wall[me ^ 1], 1, 1) + dg(dv_ref[...], wall[me ^ 2], 1, 1)
    half = dx0.shape[0]
    dx0[...] = dx[:half].astype(BF)
    dx1[...] = dx[half:].astype(BF)


US = {
    "self_forward_kernel": 13.5, "ffn_forward_kernel": 4.5, "cross_forward_kernel": 13.5, "decoder_kernel": 23.0,
    "cross_weights_kernel": 3.7, "ffn_backward_mate_kernel": 6.0, "ffn_backward_own_kernel": 6.7,
    "self_backward_kernel": 7.5, "self_weights_kernel": 3.5, "input_backward_kernel": 2.0,
}


def call(kernel, outs, args, scratch=(), vmem=60):
    in_hbm = pl.BlockSpec(memory_space=pltpu.HBM)
    in_vmem = pl.BlockSpec(memory_space=pltpu.VMEM)
    in_smem = pl.BlockSpec(memory_space=pltpu.SMEM)
    us = 0.01 * US[getattr(kernel, "func", kernel).__name__]
    arrays = [a.value if isinstance(a, Raw) else a for a in args]
    shapes = [o.value if isinstance(o, Raw) else o for o in outs]
    moved = [pltpu.VMEM(a.value.shape, a.value.dtype) for a in args if isinstance(a, Fetch)]
    moved += [pltpu.VMEM(*o.value) for o in outs if isinstance(o, Late)]

    def wrapped(*refs):
        ins, refs = refs[: len(arrays)], refs[len(arrays) :]
        results, refs = refs[: len(shapes)], refs[len(shapes) :]
        buffers, rest, sems = list(refs[: len(moved)]), refs[len(moved) : -1], refs[-1]
        copies = Copies(sems)
        given = []
        for ref, arg in zip(ins, args):
            if isinstance(arg, Fetch):
                buffer = buffers.pop(0)
                ref = Fetched(copies.start(ref, buffer), buffer)
            given.append(ref)
        produced = []
        for ref, out in zip(results, outs):
            produced.append(Result(copies, buffers.pop(0), ref) if isinstance(out, Late) else ref)
        kernel(copies, *given, *produced, *rest)
        for ref in given:
            if isinstance(ref, Fetched):
                ref.ready()
        for out in produced:
            if isinstance(out, Result):
                out.flush()
        for out in produced:
            if isinstance(out, Result):
                out.copy.wait()

    return pl.pallas_call(
        wrapped,
        out_shape=tuple(jax.ShapeDtypeStruct(*o) for o in shapes),
        in_specs=[
            in_hbm if isinstance(a, Raw) else in_smem if a.dtype == jnp.int32 else in_vmem for a in args
        ],
        out_specs=tuple(in_hbm if isinstance(o, Raw) else in_vmem for o in outs),
        scratch_shapes=[*moved, *scratch, pltpu.SemaphoreType.DMA((64,))],
        compiler_params=pltpu.CompilerParams(vmem_limit_bytes=vmem * MIB),
        cost_estimate=pl.CostEstimate(flops=int(us * 1e9), bytes_accessed=int(us * 2e6), transcendentals=0),
    )(*arrays)


def body(
    inputs,
    cotangent,
    lengths,
    row_flags,
    qkv_w,
    out_w,
    cross_w,
    up_w,
    down_w,
    norm_gain,
    norm_bias,
    cross_gain,
    cross_bias,
):
    section = lax.axis_index("section")
    is_dec = section == 1
    d = lax.axis_index("dp")
    t = lax.axis_index("tensor")
    core = d % 2
    me = d % 4
    feat = inputs.shape[3]
    chunk = inputs.shape[2]
    half = 2 * chunk
    row_len = 2 * half
    quarter = qkv_w.shape[3]
    n_t = 4

    attn_local = jnp.concatenate([qkv_w[0], out_w[0].T[None]], axis=0)
    piece = jnp.where(me == 3, out_w[0].T, lax.dynamic_index_in_dim(qkv_w[0], jnp.minimum(me, 2), 0, False))
    attn_z = z_pieces(piece)
    got = [deal(lax.dynamic_index_in_dim(inputs[0], (t + k) % 2, 0, False), k) for k in range(2)]
    unit_quarter = up_w.shape[2] // 4
    ffn_local = jnp.stack([up_w[0].T.reshape(4, unit_quarter, feat), down_w[0].reshape(4, unit_quarter, feat)], axis=1)
    cross_other = to_decoder(after(cross_w[0], attn_z))
    cross_local = jnp.stack([cross_w[0, 0], cross_other[0], cross_other[1], cross_w[0, 1]])
    cross_piece = lax.dynamic_index_in_dim(cross_local, me, 0, False)

    own_info = jnp.concatenate(
        [lengths[0], lengths[1], row_flags[:, None], jnp.zeros((2, 7), jnp.int32)], axis=1
    ).astype(F32)
    mate_info = swap_dp(own_info, 1)
    row_info = jnp.where(t // 2 == core, own_info, mate_info)
    row_info = lax.dynamic_index_in_dim(row_info, t % 2, 0, False).astype(jnp.int32)
    flip = core * half + (t % 2) * chunk
    src_lens = row_info[0:8]
    dec_int = is_dec.astype(jnp.int32)

    def tail(causal):
        return jnp.stack([row_info[16], flip, causal, me, dec_int, t, 0, 0]).astype(jnp.int32)

    info = jnp.stack([
        jnp.concatenate([jnp.where(is_dec, row_info[8:16], src_lens), tail(dec_int)]),
        jnp.concatenate([src_lens, tail(0)]),
    ])

    gains = jnp.where(is_dec, norm_gain[1], norm_gain[0])
    shifts = jnp.where(is_dec, norm_bias[1], norm_bias[0])
    cgain, cshift = cross_gain[None], cross_bias[None]

    rows = (half, feat)
    full = (row_len, feat)
    column = (half, PAIR)
    wall = pltpu.VMEM((4, feat, feat), BF)
    units = pltpu.VMEM((4 * n_t, 2, unit_quarter, feat), BF)
    bias_n = pltpu.VMEM((half, row_len), F32)
    masks = [pltpu.VMEM((half, PAIR), BF), pltpu.VMEM((row_len, PAIR), BF)]
    bias_t = pltpu.VMEM((row_len, half), F32)
    rd_s = pltpu.VMEM((HEADS, 1, half), F32)

    def raw(*arrays):
        return [Raw(a) for a in arrays]

    def fetch(*arrays):
        return [Fetch(a) for a in arrays]

    def late(*shapes):
        return [Late(a) for a in shapes]

    attn_zs = jnp.stack(attn_z)
    ffn_z = z_pieces(after(lax.dynamic_index_in_dim(ffn_local, me, 0, False), attn_zs))
    attn_ys, info, gains, shifts = together(swap_dp(attn_zs, 2), info, gains, shifts)
    gain1, gain3 = gains[0:1], gains[1:2]
    shift1, shift3 = shifts[0:1], shifts[1:2]
    attn_ws = raw(attn_local, attn_zs, swap_dp(attn_zs, 1), attn_ys, swap_dp(attn_ys, 1))
    mates = [swap_dp(x, 1) for x in got]
    mid, mid_low, n1, inv1, q1, k1, v1, att1, lse1 = call(
        self_forward_kernel,
        [(rows, F32), (rows, BF), *late((rows, F32)), (column, F32), (rows, BF), (full, BF), (full, BF), (rows, BF),
         ((HEADS, 1, half), F32)],
        [info, *fetch(after(got[0], cross_piece), got[1], *mates), gain1, shift1, *attn_ws], [wall, *masks, bias_n], 20,
    )
    ffn_zs = jnp.stack(after(ffn_z, mid))
    ffn_ys = swap_dp(ffn_zs, 2)
    cross_z = z_pieces(after(cross_piece, mid))
    ffn_ys, *cross_z = together(ffn_ys, *cross_z)
    ffn_ws = raw(ffn_local, ffn_zs, swap_dp(ffn_zs, 1), ffn_ys, swap_dp(ffn_ys, 1))
    cross_zs = jnp.stack(cross_z)
    cross_ys = swap_dp(cross_zs, 2)
    mem_low, n3e, inv3e = call(
        ffn_forward_kernel, [(rows, BF), (rows, F32), (column, F32)], [info, after(mid, cross_zs), gain3, shift3, *ffn_ws], [units], 8,
    )
    cross_ys = after(cross_ys, mem_low)
    mem_own, cross_zm, cross_ym = together(to_decoder(mem_low), swap_dp(cross_zs, 1), swap_dp(cross_ys, 1))
    cross_ws = raw(cross_local, cross_zs, cross_zm, cross_ys, cross_ym)
    mem_mate = swap_dp(mem_own, 1)
    cots = [deal(after(lax.dynamic_index_in_dim(cotangent[0], (t + k) % 2, 0, False), mem_own), k) for k in range(2)]
    h2, n2, inv2, q2, k2, v2, att2, lse2 = call(
        cross_forward_kernel,
        [(rows, F32), (rows, F32), (column, F32), (rows, BF), (full, BF), (full, BF), (rows, BF), ((HEADS, 1, half), F32)],
        [info, *fetch(mem_own, mem_mate), mid_low, mid, cgain, cshift, *cross_ws], [wall, *masks], 20,
    )
    cots = after(cots, h2)
    out0, out1, ffn_x, n3, inv3, dh1, dmem_own, dmem_mate, dbr2, dq2, dk2, dv2, dnorm2 = call(
        decoder_kernel,
        [((chunk, feat), BF), ((chunk, feat), BF), (rows, BF), (rows, F32), (column, F32), (rows, F32), (rows, BF), (rows, BF),
         (rows, BF), (rows, BF), (full, BF), (full, BF), ((8, feat), F32)],
        [info, h2, *fetch(*cots), n2, inv2, cgain, gain3, shift3, q2, k2, v2, att2, lse2, mid_low, mem_low, n3e, inv3e, *cross_ws, *ffn_ws],
        [wall, units, bias_t, rd_s, pltpu.VMEM(rows, BF), pltpu.VMEM((half, 4 * n_t * unit_quarter), F32)], 30,
    )
    dmem_got = swap_dp(dmem_mate, 1)
    pieces = [((2, n_t, feat, quarter), BF)] * 2
    cross_keep, cross_send = call(
        cross_weights_kernel, pieces, [info, mid_low, dq2, mem_own, mem_mate, dk2, dv2, dbr2, att2], vmem=8,
    )
    dmem = add_low(dmem_own, after(dmem_got, cross_keep))
    dmem_enc = to_encoder(dmem)
    cross_mate = swap_dp(after(cross_send, dmem), 1)
    cross_got = swap_dp(add_low(cross_keep[1], cross_mate[1]), 2)
    out_back = [deal_back(after(out, dmem), k) for k, out in enumerate((out0, out1))]
    dmem_enc, cross_got, *out_back = together(dmem_enc, cross_got, *out_back)
    cross_quarter = add_low(cross_keep[0], cross_mate[0], cross_got)

    ffn_pieces = ((2, n_t, unit_quarter, feat), BF)
    half_units = pltpu.VMEM((2 * n_t, 2, unit_quarter, feat), BF)
    up_send, down_send, acc, dbr3, dnorm3 = call(
        ffn_backward_mate_kernel, [ffn_pieces, ffn_pieces, (rows, F32), (rows, BF), ((8, feat), F32)],
        [info, ffn_x, n3, inv3, *fetch(*cots, dmem_enc), gain3, *ffn_ws], [half_units], 10,
    )
    up_mate, down_mate = swap_dp(up_send, 1), swap_dp(down_send, 1)
    do1, up_keep, down_keep, dr1, dbr1, dnorm1 = call(
        ffn_backward_own_kernel, [(rows, BF), ffn_pieces, ffn_pieces, (rows, F32), (rows, BF), ((8, feat), F32)],
        [info, ffn_x, dbr3, acc, *fetch(n1), inv1, gain1, dh1, *ffn_ws, *attn_ws], [half_units, wall], 11,
    )
    up_mate, down_mate = after(up_mate, do1), after(down_mate, do1)
    up_got = swap_dp(add_low(up_keep[1], up_mate[1]), 2)
    down_got = swap_dp(add_low(down_keep[1], down_mate[1]), 2)

    def self_backward(first, n_pairs, do):
        width = n_pairs * PAIR
        half_grad = ((2, half, width), BF)
        return call(
            functools.partial(self_backward_kernel, first), [((half, width), BF), half_grad, half_grad],
            [info, *raw(q1, k1, v1, att1), do, lse1],
            [bias_t, pltpu.VMEM((half, width), BF), pltpu.VMEM((row_len, width), BF), pltpu.VMEM((row_len, width), BF),
             pltpu.VMEM((half, width), BF), pltpu.VMEM((half, width), BF), rd_s,
             pltpu.VMEM((row_len, width), BF), pltpu.VMEM((row_len, width), BF)], 11,
        )

    cross_parts = z_parts(after(cross_quarter, do1))
    dq1, dkv_own, dkv_mate = call(
        self_backward_kernel, [(rows, BF), ((2, half, feat), BF), ((2, half, feat), BF)],
        [info, *fetch(q1, k1, v1, att1), do1, lse1], [bias_t, rd_s, pltpu.VMEM(full, BF), pltpu.VMEM(full, BF)], 18,
    )
    dkv_mate, up_got, *cross_parts = together(dkv_mate, up_got, *cross_parts)
    dkv_got = swap_dp(dkv_mate, 1)
    up_parts = z_parts(add_low(up_keep[0], up_mate[0], up_got))
    self_pieces = [((2, n_t, feat + 32, quarter), BF)] * 2
    self_keep, self_send, dk1, dv1 = call(
        self_weights_kernel, [*self_pieces, (rows, BF), (rows, BF)],
        [info, *fetch(*got), dq1, dkv_own, *fetch(dkv_got, att1), dbr1, dnorm1, dnorm2, dnorm3], vmem=10,
    )
    self_send, down_got, *up_parts = together(self_send, down_got, *up_parts)
    self_mate = swap_dp(self_send, 1)
    down_parts = z_parts(add_low(down_keep[0], down_mate[0], down_got))
    dx0, dx1 = call(
        input_backward_kernel, [((chunk, feat), BF), ((chunk, feat), BF)],
        [info, dq1, after(dk1, self_mate), dv1, dr1, *attn_ws], [wall], 60,
    )
    self_got = swap_dp(add_low(self_keep[1], self_mate[1]), 2)
    self_got, dx0, dx1, *down_parts = together(self_got, dx0, dx1, *down_parts)
    ffn_back = jnp.stack([z_sum(up_parts), z_sum(down_parts)])
    self_parts = z_parts(add_low(self_keep[0], self_mate[0], self_got))
    cross_back = z_sum(after(cross_parts, self_got))
    cross_enc = to_encoder(cross_back)
    ffn_y, cross_enc, *self_parts = together(swap_dp(ffn_back, 2), cross_enc, *self_parts)
    cross_back = jnp.where(is_dec, cross_back, cross_enc)
    self_piece = z_sum(self_parts)
    self_back = self_piece[:feat]
    norms = self_piece[feat:].astype(F32).reshape(n_t, 8, PAIR).transpose(1, 0, 2).reshape(8, feat)
    other = lax.ppermute(norms, "section", [(0, 1), (1, 0)])
    ffn_two = jnp.stack([ffn_back, ffn_y])
    dx_back = [deal_back(after(dx, self_parts[0]), k) for k, dx in enumerate((dx0, dx1))]
    self_y, ffn_core, cross_y, other, *dx_back = together(
        swap_dp(self_back, 2), swap_dp(ffn_two, 1), swap_dp(cross_back, 2), other, *dx_back
    )
    self_two = jnp.stack([self_back, self_y])
    cross_two = jnp.stack([cross_back, cross_y])
    self_core, cross_core = swap_dp(self_two, 1), swap_dp(cross_two, 1)

    def four(two, mate):
        return jnp.stack([two[0], mate[0], two[1], mate[1]])

    ffn_sum = four(ffn_two, ffn_core)
    self_sum = four(self_two, self_core)
    cross_sum = four(cross_two, cross_core)

    def matrix(stacked, which):
        return lax.dynamic_index_in_dim(stacked, me ^ which, 0, False).astype(F32)

    qkv_grad = jnp.stack([matrix(self_sum, m) for m in range(3)])
    out_grad = matrix(self_sum, 3).T
    cross_grad = jnp.stack([
        matrix(cross_sum, jnp.where(is_dec, 0, 1)), matrix(cross_sum, jnp.where(is_dec, 3, 2))
    ])
    ffn_true = [matrix(ffn_sum, m) for m in range(4)]
    up_grad = jnp.concatenate([f[0].T for f in ffn_true], axis=1)
    down_grad = jnp.concatenate([f[1] for f in ffn_true], axis=0)

    enc = jnp.where(is_dec, other, norms)
    dec = jnp.where(is_dec, norms, other)
    full_gain = jnp.stack([enc[0:2], dec[0:2]])
    full_bias = jnp.stack([enc[2:4], dec[2:4]])

    def in_order(back):
        even = t % 2 == 0
        return jnp.stack([jnp.where(even, back[0], back[1]), jnp.where(even, back[1], back[0])])

    out_rows = in_order(out_back)
    grad_rows = in_order(dx_back).astype(F32)
    return (
        out_rows[None],
        grad_rows[None],
        qkv_grad[None],
        out_grad[None],
        cross_grad[None],
        up_grad[None],
        down_grad[None],
        full_gain,
        full_bias,
        dec[4],
        dec[5],
    )


def solution(mesh):
    return jax.shard_map(
        body,
        mesh=mesh,
        in_specs=(
            P("section", "dp", "tensor", None),
            P("section", "dp", "tensor", None),
            P(None, "dp", None),
            P("dp"),
            P("section", None, None, "tensor"),
            P("section", "tensor", None),
            P("section", None, None, "tensor"),
            P("section", None, "tensor"),
            P("section", "tensor", None),
            P(),
            P(),
            P(),
            P(),
        ),
        out_specs=(
            P("section", "dp", "tensor", None),
            P("section", "dp", "tensor", None),
            P("section", None, None, "tensor"),
            P("section", "tensor", None),
            P("section", None, None, "tensor"),
            P("section", None, "tensor"),
            P("section", "tensor", None),
            P(),
            P(),
            P(),
            P(),
        ),
        check_vma=False,
    )
```

```python
import functools

import jax
import jax.numpy as jnp
from jax import lax
from jax.experimental import pallas as pl
from jax.experimental.pallas import tpu as pltpu
from jax.sharding import PartitionSpec as P

HEADS = 8
HD = 64
PAIR = 2 * HD
SLOT_BITS = 7
SLOTS = 8
NEG = -1e30
EPS = 1e-05
SCALE = HD ** -0.5
BF = jnp.bfloat16
F32 = jnp.float32
MIB = 1024 * 1024


def swap_dp(x, bit):
    n = lax.axis_size("dp")
    return lax.ppermute(x, "dp", [(i, i ^ bit) for i in range(n)])


def shift_tensor(x, step):
    n = lax.axis_size("tensor")
    return lax.ppermute(x, "tensor", [(i, (i + step) % n) for i in range(n)])


def swap_tensor(x, bit):
    n = lax.axis_size("tensor")
    return lax.ppermute(x, "tensor", [(i, i ^ bit) for i in range(n)])


def to_decoder(x):
    return lax.ppermute(x, "section", [(0, 1)])


def to_encoder(x):
    return lax.ppermute(x, "section", [(1, 0)])


def deal_route(k):
    n_t = lax.axis_size("tensor")
    route = []
    for d in range(lax.axis_size("dp")):
        group, core = divmod(d, 2)
        for t in range(n_t):
            plane = 2 * core + (t + k) % 2
            route.append((d * n_t + t, (2 * group + t // 2) * n_t + plane))
    return route


def deal(x, k):
    return lax.ppermute(x, ("dp", "tensor"), deal_route(k))


def deal_back(x, k):
    return lax.ppermute(x, ("dp", "tensor"), [(b, a) for a, b in deal_route(k)])


def together(*xs):
    return lax.optimization_barrier(xs)


def after(x, *events):
    return lax.optimization_barrier((x, *events))[0]


def z_pieces(piece):
    return [shift_tensor(piece, r) for r in range(1, 4)]


def add_low(*parts):
    return sum(p.astype(F32) for p in parts).astype(BF)


def other_groups(total):
    bit = 4
    while bit < lax.axis_size("dp"):
        total = add_low(total, swap_dp(total, bit))
        bit *= 2
    return total


def z_parts(quarter):
    return [quarter[0]] + [shift_tensor(quarter[r], -r) for r in range(1, 4)]


def z_sum(parts):
    return other_groups(add_low(*parts))


def dg(a, b, ca, cb):
    return lax.dot_general(a, b, (((ca,), (cb,)), ((), ())), preferred_element_type=F32)


def norm_fwd(r):
    off = r - jnp.mean(r, axis=-1, keepdims=True)
    inv = lax.rsqrt(jnp.mean(off * off, axis=-1, keepdims=True) + EPS)
    return off * inv, inv


def norm_bwd(dy, n, inv, gain):
    sc = dy * gain
    dr = inv * (
        sc
        - jnp.mean(sc, axis=-1, keepdims=True)
        - n * jnp.mean(sc * n, axis=-1, keepdims=True)
    )
    return dr, jnp.sum(dy * n, axis=0, keepdims=True), jnp.sum(dy, axis=0, keepdims=True)


def head_lanes(h):
    return (lax.broadcasted_iota(jnp.int32, (1, PAIR), 1) // HD) == h


def mask_bias(info, row, n_q, n_k, q_axis):
    flip = info[row, 9]
    q_shape = (n_q, 1) if q_axis == 0 else (1, n_q)
    full = (n_q, n_k) if q_axis == 0 else (n_k, n_q)
    q_pos = lax.broadcasted_iota(jnp.int32, q_shape, q_axis) ^ flip
    seg = jnp.where(info[row, 8] == 1, 0, q_pos >> SLOT_BITS)
    size = jnp.zeros(q_shape, jnp.int32)
    for j in range(SLOTS):
        size = size + jnp.where(seg == j, info[row, j], 0)
    first = seg << SLOT_BITS
    end = first + size
    end = jnp.where(info[row, 10] == 1, jnp.minimum(end, q_pos + 1), end)
    k_pos = lax.broadcasted_iota(jnp.int32, full, 1 - q_axis) ^ flip
    return jnp.where((k_pos >= first) & (k_pos < end), 0.0, NEG)


class Copies:
    def __init__(self, sems):
        self.sems = sems
        self.count = 0

    def start(self, src, dst):
        copy = pltpu.make_async_copy(src, dst, self.sems.at[self.count])
        self.count += 1
        copy.start()
        return copy


class Raw:
    def __init__(self, value):
        self.value = value


class Fetch(Raw):
    pass


class Late(Raw):
    pass


class Fetched:
    def __init__(self, copy, ref):
        self.copy = copy
        self.ref = ref
        self.shape = ref.shape

    def ready(self):
        if self.copy is not None:
            self.copy.wait()
            self.copy = None
        return self.ref

    def __getitem__(self, at):
        return self.ready()[at]


class Result:
    def __init__(self, copies, ref, dst):
        self.copies = copies
        self.ref = ref
        self.dst = dst
        self.shape = ref.shape
        self.copy = None

    def __setitem__(self, at, value):
        self.ref[at] = value

    def __getitem__(self, at):
        return self.ref[at]

    def flush(self):
        if self.copy is None:
            self.copy = self.copies.start(self.ref, self.dst)


def load_wall(copies, me, refs, wall):
    local, *pieces = refs
    started = []
    for rel, ref in enumerate(pieces):
        started.append(copies.start(local.at[me ^ rel], wall.at[rel, :, pl.ds(0, PAIR)]))
        for z in range(1, 4):
            started.append(copies.start(ref.at[z - 1], wall.at[rel, :, pl.ds(z * PAIR, PAIR)]))
    return started


def load_units(copies, me, refs, units, rels=range(4)):
    local, *pieces = refs
    started = []
    for i, rel in enumerate(rels):
        started.append(copies.start(local.at[me ^ rel], units.at[4 * i]))
        started.append(copies.start(pieces[rel], units.at[pl.ds(4 * i + 1, 3)]))
    return started


def wait_all(started):
    for copy in started:
        copy.wait()


def unit_block(units, which, i):
    return jnp.concatenate([units[2 * i, which], units[2 * i + 1, which]], axis=0)


def mask_columns(info, row, n, of_queries):
    pos = lax.broadcasted_iota(jnp.int32, (n, 1), 0) ^ info[row, 9]
    seg = jnp.where(info[row, 8] == 1, 0, pos >> SLOT_BITS)
    lane = lax.broadcasted_iota(jnp.int32, (1, PAIR), 1) % HD
    if of_queries:
        return jnp.where(lane == seg, 1.0, 0.0).astype(BF)
    size = jnp.zeros((n, 1), jnp.int32)
    for j in range(SLOTS):
        size = size + jnp.where(seg == j, info[row, j], 0)
    counts = (lane == seg) & (pos - (seg << SLOT_BITS) < size)
    return jnp.where(lane < SLOTS, jnp.where(counts, 0.0, NEG), 0.0).astype(BF)


def attend_forward(info, row, q_ref, k_ref, v_ref, att_ref, lse_ref, qm_ref, km_ref, bias_ref=None):
    n_q = q_ref.shape[0]
    lane = lax.broadcasted_iota(jnp.int32, (1, PAIR), 1)

    def heads(causal):
        qm_ref[...] = mask_columns(info, row, n_q, True)
        km_ref[...] = mask_columns(info, row, k_ref.shape[0], False)
        if causal:
            bias_ref[...] = mask_bias(info, row, n_q, k_ref.shape[0], 0)
        lse = jnp.zeros((n_q, PAIR), F32)
        for hp in range(HEADS // 2):
            sl = slice(hp * PAIR, (hp + 1) * PAIR)
            qp, kp, vp = q_ref[:, sl], k_ref[:, sl], v_ref[:, sl]
            outs = []
            for h in range(2):
                own = head_lanes(h)
                s = dg(jnp.where(own, qp, qm_ref[...]), jnp.where(own, kp, km_ref[...]), 1, 1)
                if causal:
                    s = s + bias_ref[...]
                top = jnp.max(s, axis=1, keepdims=True)
                e = jnp.exp(s - top).astype(BF)
                o = dg(e, jnp.where(own, vp, jnp.ones_like(vp)), 1, 0)
                at = (1 - h) * HD
                total = o[:, at : at + 1]
                outs.append(o * (1.0 / total))
                lse = jnp.where(lane == 2 * hp + h, top + jnp.log(total), lse)
            att_ref[:, sl] = jnp.where(head_lanes(0), outs[0], outs[1]).astype(BF)
        rows = jnp.transpose(lse)
        for h in range(HEADS):
            lse_ref[h] = rows[h : h + 1]

    if bias_ref is None:
        heads(False)
    else:
        pl.when(info[row, 10] == 1)(lambda: heads(True))
        pl.when(info[row, 10] != 1)(lambda: heads(False))


def attend_backward(info, row, n_pairs, q_ref, k_ref, v_ref, do_ref, att_ref, lse_ref, bias_ref, rd_ref, dq_ref, dk_ref, dv_ref):
    n_q = q_ref.shape[0]
    block = 256
    empty = info[row, 0]
    for j in range(1, SLOTS):
        empty = empty + info[row, j]
    empty = empty == 0
    p_fix = jnp.where(empty, 1.0 / k_ref.shape[0], 1.0)
    s_fix = jnp.where(empty, 0.0, 1.0)
    width = n_pairs * PAIR
    prod = do_ref[...].astype(F32) * att_ref[...].astype(F32)
    high = prod.astype(BF)
    low = (prod - high.astype(F32)).astype(BF)
    heads = lax.broadcasted_iota(jnp.int32, (HEADS, width), 0)
    lanes_of = lax.broadcasted_iota(jnp.int32, (HEADS, width), 1) // HD
    ones = jnp.where(heads == lanes_of, 1.0, 0.0).astype(BF)
    rd = dg(ones, high, 1, 1) + dg(ones, low, 1, 1)
    for h in range(2 * n_pairs):
        rd_ref[h] = rd[h : h + 1]

    def pair(hp, _):
        sl = pl.ds(pl.multiple_of(hp * PAIR, PAIR), PAIR)
        kp = k_ref[:, sl]
        vp = v_ref[:, sl]
        k_t = jnp.transpose(kp)
        dk = dv = None
        for qi in range(n_q // block):
            qs = slice(qi * block, (qi + 1) * block)
            qp = q_ref[qs, sl]
            dop = do_ref[qs, sl]
            dqs = []
            for h in range(2):
                lanes = head_lanes(h)
                qm = jnp.where(lanes, qp, jnp.zeros_like(qp))
                dom = jnp.where(lanes, dop, jnp.zeros_like(dop))
                s = dg(kp, qm, 1, 1) + bias_ref[:, qs]
                p = jnp.exp(s - lse_ref[hp * 2 + h, :, qs])
                dp = dg(vp, dom, 1, 1)
                ds = (p * (dp - rd_ref[hp * 2 + h, :, qs])).astype(BF)
                a = dg(p.astype(BF), dom, 1, 0)
                dv = a if dv is None else dv + a
                a = dg(ds, qm, 1, 0)
                dk = a if dk is None else dk + a
                dqs.append(dg(k_t[h * HD : (h + 1) * HD], ds, 1, 0))
            dq = jnp.transpose(jnp.concatenate(dqs, axis=0))
            dq_ref[qs, sl] = (dq * (SCALE * s_fix)).astype(BF)
        dk_ref[:, sl] = (dk * s_fix).astype(BF)
        dv_ref[:, sl] = (dv * p_fix).astype(BF)
        return 0

    lax.fori_loop(0, n_pairs, pair, 0)


def self_forward_kernel(copies, info, x0, x1, x2, x3, gain, shift, *refs):
    w_refs = refs[:5]
    y_out, low_out, n_out, inv_out, q_out, k_out, v_out, att_out, lse_out, wall, qm_ref, km_ref, bias_ref = refs[5:]
    me = info[0, 11]
    started = load_wall(copies, me, w_refs, wall)
    wait_all(started)
    rows_low = jnp.concatenate([x0[...], x1[...]], axis=0)
    q_out[...] = dg(rows_low, wall[me], 1, 0).astype(BF) * jnp.asarray(SCALE, BF)
    wk = wall[me ^ 1]
    wv = wall[me ^ 2]
    at = 0
    for ref in (x0, x1, x2, x3):
        part = ref[...]
        k_out[at : at + ref.shape[0]] = dg(part, wk, 1, 0).astype(BF)
        v_out[at : at + ref.shape[0]] = dg(part, wv, 1, 0).astype(BF)
        at += ref.shape[0]
    attend_forward(info, 0, q_out, k_out, v_out, att_out, lse_out, qm_ref, km_ref, bias_ref)
    n, inv = norm_fwd(rows_low.astype(F32) + dg(att_out[...], wall[me ^ 3], 1, 1))
    n_out[...] = n
    inv_out[...] = jnp.broadcast_to(inv, inv_out.shape)
    y = n * gain[...] + shift[...]
    y_out[...] = y
    low_out[...] = y.astype(BF)


def silu_parts(u):
    sg = jax.nn.sigmoid(u)
    return u * sg, sg


def ffn_forward_kernel(copies, info, x_ref, gain, shift, *refs):
    low0, low1, n_out, inv_out, units = refs[5:]
    started = load_units(copies, info[0, 11], refs[:5], units)
    x = x_ref[...]
    low = x.astype(BF)
    acc = x
    wait_all(started)
    for i in range(units.shape[0] // 2):
        u = dg(low, unit_block(units, 0, i), 1, 1)
        act = silu_parts(u)[0].astype(BF)
        acc = acc + dg(act, unit_block(units, 1, i), 1, 0)
    n, inv = norm_fwd(acc)
    y = (n * gain[...] + shift[...]).astype(BF)
    low0[...] = y[: low0.shape[0]]
    low1[...] = y[low0.shape[0] :]
    n_out[...] = n
    inv_out[...] = jnp.broadcast_to(inv, inv_out.shape)


def cross_forward_kernel(copies, info, own0, own1, mate0, mate1, h_low, h_ref, cgain, cshift, *refs):
    y_out, n_out, inv_out, q_out, k_out, v_out, att_out, lse_out, wall, qm_ref, km_ref = refs[5:]
    me = info[1, 11]
    started = load_wall(copies, me, refs[:5], wall)
    wait_all(started)
    q_out[...] = dg(h_low[...], wall[me], 1, 0).astype(BF) * jnp.asarray(SCALE, BF)
    half = own0.shape[0]
    for ref, at in ((own0, 0), (own1, half), (mate0, 2 * half), (mate1, 3 * half)):
        k_out[at : at + half] = dg(ref[...], wall[me ^ 1], 1, 0).astype(BF)
        v_out[at : at + half] = dg(ref[...], wall[me ^ 2], 1, 0).astype(BF)
    attend_forward(info, 1, q_out, k_out, v_out, att_out, lse_out, qm_ref, km_ref)
    n, inv = norm_fwd(h_ref[...] + dg(att_out[...], wall[me ^ 3], 1, 1))
    n_out[...] = n
    inv_out[...] = jnp.broadcast_to(inv, inv_out.shape)
    y_out[...] = n * cgain[...] + cshift[...]


def decoder_kernel(copies, info, h_ref, cot0, cot1, n2_ref, inv2_ref, cgain, gain3, shift3, q_ref, k_ref, v_ref, att_ref, lse_ref,
                   h_low, mem_low0, mem_low1, n3e, inv3e, *refs):
    w_refs, unit_refs = refs[:5], refs[5:10]
    (out0, out1, x_ref, n3_ref, inv3_ref, dh_out, dmem_own_out, dmem_mate_out, dbr_out, dq_out, dk_out, dv_out, dnorm_out,
     wall, units, bias_ref, rd_ref, do_ref, u_ref) = refs[10:]
    me = info[1, 11]
    dec = info[1, 12] == 1
    started = load_units(copies, me, unit_refs, units)
    wall_started = load_wall(copies, me, w_refs, wall)
    bias_ref[...] = mask_bias(info, 1, q_ref.shape[0], k_ref.shape[0], 1)
    acc = h_ref[...]
    low = acc.astype(BF)
    x_ref[...] = low
    wait_all(started)
    width = 2 * PAIR
    blocks = units.shape[0] // 2
    for i in range(blocks):
        u = dg(low, unit_block(units, 0, i), 1, 1)
        u_ref[:, i * width : (i + 1) * width] = u
        act = silu_parts(u)[0].astype(BF)
        acc = acc + dg(act, unit_block(units, 1, i), 1, 0)
    n, inv = norm_fwd(acc)
    y = (n * gain3[...] + shift3[...]).astype(BF)
    half = out0.shape[0]
    out0[...] = y[:half]
    out1[...] = y[half:]
    n3_ref[...] = n
    inv3_ref[...] = jnp.broadcast_to(inv, inv3_ref.shape)
    passed = ((out0, mem_low0[...]), (out1, mem_low1[...]), (x_ref, h_low[...]), (n3_ref, n3e[...]), (inv3_ref, inv3e[...]))
    for ref, src in passed:
        ref[...] = jnp.where(dec, ref[...], src)
    cot = jnp.concatenate([cot0[...], cot1[...]], axis=0).astype(F32)
    dr, _, _ = norm_bwd(cot, n, inv, gain3[...])
    dbr = dr.astype(BF)
    acc = dr
    for i in range(blocks):
        u = u_ref[:, i * width : (i + 1) * width]
        sg = jax.nn.sigmoid(u)
        dact = dg(dbr, unit_block(units, 1, i), 1, 1)
        du = (dact * sg * (1.0 + u * (1.0 - sg))).astype(BF)
        acc = acc + dg(du, unit_block(units, 0, i), 1, 0)
    dr, dg_sum, db_sum = norm_bwd(acc, n2_ref[...], inv2_ref[:, 0:1], cgain[...])
    dnorm_out[0:1] = dg_sum
    dnorm_out[1:2] = db_sum
    dh_out[...] = dr
    dbr = dr.astype(BF)
    dbr_out[...] = dbr
    wait_all(wall_started)
    do_ref[...] = dg(dbr, wall[me ^ 3], 1, 0).astype(BF)
    attend_backward(info, 1, HEADS // 2, q_ref, k_ref, v_ref, do_ref, att_ref, lse_ref, bias_ref, rd_ref, dq_out, dk_out, dv_out)
    half = dmem_own_out.shape[0]
    wk = wall[me ^ 1]
    wv = wall[me ^ 2]
    for out, at in ((dmem_mate_out, half), (dmem_own_out, 0)):
        part = dg(dk_out[at : at + half], wk, 1, 1) + dg(dv_out[at : at + half], wv, 1, 1)
        out[...] = part.astype(BF)
    dh_out[...] = dh_out[...] + dg(dq_out[...], wall[me], 1, 1)


def put_matrix(keep_ref, send_ref, me, which, value):
    slot = me ^ which
    y = slot >> 1

    def put(ref):
        for z in range(4):
            ref[y, z, : value.shape[0]] = value[:, z * PAIR : (z + 1) * PAIR]

    @pl.when(slot % 2 == 0)
    def _():
        put(keep_ref)

    @pl.when(slot % 2 == 1)
    def _():
        put(send_ref)


def cross_weights_kernel(copies, info, h_low, dq_ref, own0, own1, mate0, mate1, dk_ref, dv_ref, dbr_ref, att_ref, keep, send):
    me = info[1, 11]
    mem = jnp.concatenate([own0[...], own1[...], mate0[...], mate1[...]], axis=0)


    put_matrix(keep, send, me, 0, dg(h_low[...], dq_ref[...], 0, 0).astype(BF))
    for which, ref in ((1, dk_ref), (2, dv_ref)):
        value = dg(mem, ref[...], 0, 0)
        put_matrix(keep, send, me, which, value.astype(BF))
    put_matrix(keep, send, me, 3, dg(dbr_ref[...], att_ref[...], 0, 0).astype(BF))


def ffn_backward_part(low, dbr, acc, units, up_grad, down_grad):
    for i in range(units.shape[0] // 2):
        y, z = i // 2, i % 2
        wu = unit_block(units, 0, i)
        wd = unit_block(units, 1, i)
        u_t = dg(wu, low, 1, 1)
        act_t, sg = silu_parts(u_t)
        act_t = act_t.astype(BF)
        dact_t = dg(wd, dbr, 1, 1)
        du_t = (dact_t * sg * (1.0 + u_t * (1.0 - sg))).astype(BF)
        acc = acc + dg(du_t, wu, 0, 0)
        dup = dg(du_t, low, 1, 0).astype(BF)
        ddown = dg(act_t, dbr, 1, 0).astype(BF)
        for j in range(2):
            up_grad[y, 2 * z + j] = dup[j * PAIR : (j + 1) * PAIR]
            down_grad[y, 2 * z + j] = ddown[j * PAIR : (j + 1) * PAIR]
    return acc


def ffn_backward_mate_kernel(copies, info, x_ref, n3_ref, inv3_ref, cot0, cot1, dmem_ref, gain3, *refs):
    up_send, down_send, acc_out, dbr_out, dnorm_out, units = refs[5:]
    started = load_units(copies, info[0, 11], refs[:5], units, (1, 3))
    dy = jnp.concatenate([cot0[...], cot1[...]], axis=0).astype(F32) + dmem_ref[...].astype(F32)
    dr3, dg3, db3 = norm_bwd(dy, n3_ref[...], inv3_ref[:, 0:1], gain3[...])
    dnorm_out[0:1] = dg3
    dnorm_out[1:2] = db3
    dbr = dr3.astype(BF)
    dbr_out[...] = dbr
    wait_all(started)
    acc_out[...] = ffn_backward_part(x_ref[...], dbr, dr3, units, up_send, down_send)


def ffn_backward_own_kernel(copies, info, x_ref, dbr_ref, acc_ref, n1_ref, inv1_ref, gain1, dmid_ref, *refs):
    do_out, up_keep, down_keep, dr1_out, dbr1_out, dnorm_out, units, wall = refs[10:]
    me = info[0, 11]
    started = load_units(copies, me, refs[:5], units, (0, 2))
    wall_started = load_wall(copies, me, refs[5:10], wall)
    wait_all(started)
    acc = ffn_backward_part(x_ref[...], dbr_ref[...], acc_ref[...], units, up_keep, down_keep)
    dmid = jnp.where(info[0, 12] == 1, dmid_ref[...], acc)
    dr1, dg1, db1 = norm_bwd(dmid, n1_ref[...], inv1_ref[:, 0:1], gain1[...])
    dr1_out[...] = dr1
    dbr1 = dr1.astype(BF)
    dbr1_out[...] = dbr1
    dnorm_out[0:1] = dg1
    dnorm_out[1:2] = db1
    wait_all(wall_started)
    do_out[...] = dg(dbr1, wall[me ^ 3], 1, 0).astype(BF)


def self_backward_kernel(copies, info, q_ref, k_ref, v_ref, att_ref, do_ref, lse_ref, dq_out, own, mate, bias_ref, rd_ref, dk_ref, dv_ref):
    bias_ref[...] = mask_bias(info, 0, q_ref.shape[0], k_ref.shape[0], 1)
    q, k, v, att = q_ref.ready(), k_ref.ready(), v_ref.ready(), att_ref.ready()
    attend_backward(info, 0, HEADS // 2, q, k, v, do_ref, att, lse_ref, bias_ref, rd_ref, dq_out, dk_ref, dv_ref)
    half = q_ref.shape[0]
    for dst, at in ((mate, half), (own, 0)):
        dst[0] = dk_ref[at : at + half]
        dst[1] = dv_ref[at : at + half]


def self_weights_kernel(copies, info, x0, x1, dq_ref, own, got, att_ref, dbr_ref, dnorm1, dnorm2, dnorm3, keep, send, dk_out, dv_out):
    me = info[0, 11]
    dq = dq_ref[...]
    dk = (own[0].astype(F32) + got[0].astype(F32)).astype(BF)
    dv = (own[1].astype(F32) + got[1].astype(F32)).astype(BF)
    dk_out[...] = dk
    dv_out[...] = dv
    x = jnp.concatenate([x0[...], x1[...]], axis=0)
    for which, value in ((0, dq), (1, dk), (2, dv)):
        put_matrix(keep, send, me, which, dg(x, value, 0, 0).astype(BF))
    put_matrix(keep, send, me, 3, dg(dbr_ref[...], att_ref[...], 0, 0).astype(BF))
    feat = dq.shape[1]
    norms = jnp.concatenate([dnorm1[0:1], dnorm3[0:1], dnorm1[1:2], dnorm3[1:2], dnorm2[0:2], jnp.zeros((2, feat), F32)], axis=0)
    rows = jnp.concatenate([norms[:, i * PAIR : (i + 1) * PAIR] for i in range(feat // PAIR)], axis=0).astype(BF)
    for out in (keep, send):
        for y in range(2):
            for z in range(4):
                out[y, z, feat:] = rows


def input_backward_kernel(copies, info, dq_ref, dk_ref, dv_ref, dr_ref, *refs):
    dx0, dx1, wall = refs[5:]
    me = info[0, 11]
    started = load_wall(copies, me, refs[:5], wall)
    wait_all(started)
    dx = dr_ref[...] + dg(dq_ref[...], wall[me], 1, 1) + dg(dk_ref[...], wall[me ^ 1], 1, 1) + dg(dv_ref[...], wall[me ^ 2], 1, 1)
    half = dx0.shape[0]
    dx0[...] = dx[:half].astype(BF)
    dx1[...] = dx[half:].astype(BF)


US = {
    "self_forward_kernel": 13.5, "ffn_forward_kernel": 4.5, "cross_forward_kernel": 13.5, "decoder_kernel": 23.0,
    "cross_weights_kernel": 3.7, "ffn_backward_mate_kernel": 6.0, "ffn_backward_own_kernel": 6.7,
    "self_backward_kernel": 7.5, "self_weights_kernel": 3.5, "input_backward_kernel": 2.0,
}


def call(kernel, outs, args, scratch=(), vmem=60):
    in_hbm = pl.BlockSpec(memory_space=pltpu.HBM)
    in_vmem = pl.BlockSpec(memory_space=pltpu.VMEM)
    in_smem = pl.BlockSpec(memory_space=pltpu.SMEM)
    us = 0.01 * US[getattr(kernel, "func", kernel).__name__]
    arrays = [a.value if isinstance(a, Raw) else a for a in args]
    shapes = [o.value if isinstance(o, Raw) else o for o in outs]
    moved = [pltpu.VMEM(a.value.shape, a.value.dtype) for a in args if isinstance(a, Fetch)]
    moved += [pltpu.VMEM(*o.value) for o in outs if isinstance(o, Late)]

    def wrapped(*refs):
        ins, refs = refs[: len(arrays)], refs[len(arrays) :]
        results, refs = refs[: len(shapes)], refs[len(shapes) :]
        buffers, rest, sems = list(refs[: len(moved)]), refs[len(moved) : -1], refs[-1]
        copies = Copies(sems)
        given = []
        for ref, arg in zip(ins, args):
            if isinstance(arg, Fetch):
                buffer = buffers.pop(0)
                ref = Fetched(copies.start(ref, buffer), buffer)
            given.append(ref)
        produced = []
        for ref, out in zip(results, outs):
            produced.append(Result(copies, buffers.pop(0), ref) if isinstance(out, Late) else ref)
        kernel(copies, *given, *produced, *rest)
        for ref in given:
            if isinstance(ref, Fetched):
                ref.ready()
        for out in produced:
            if isinstance(out, Result):
                out.flush()
        for out in produced:
            if isinstance(out, Result):
                out.copy.wait()

    return pl.pallas_call(
        wrapped,
        out_shape=tuple(jax.ShapeDtypeStruct(*o) for o in shapes),
        in_specs=[
            in_hbm if isinstance(a, Raw) else in_smem if a.dtype == jnp.int32 else in_vmem for a in args
        ],
        out_specs=tuple(in_hbm if isinstance(o, Raw) else in_vmem for o in outs),
        scratch_shapes=[*moved, *scratch, pltpu.SemaphoreType.DMA((64,))],
        compiler_params=pltpu.CompilerParams(vmem_limit_bytes=vmem * MIB),
        cost_estimate=pl.CostEstimate(flops=int(us * 1e9), bytes_accessed=int(us * 2e6), transcendentals=0),
    )(*arrays)


def body(
    inputs,
    cotangent,
    lengths,
    row_flags,
    qkv_w,
    out_w,
    cross_w,
    up_w,
    down_w,
    norm_gain,
    norm_bias,
    cross_gain,
    cross_bias,
):
    section = lax.axis_index("section")
    is_dec = section == 1
    d = lax.axis_index("dp")
    t = lax.axis_index("tensor")
    core = d % 2
    me = d % 4
    feat = inputs.shape[3]
    chunk = inputs.shape[2]
    half = 2 * chunk
    row_len = 2 * half
    quarter = qkv_w.shape[3]
    n_t = 4

    attn_local = jnp.concatenate([qkv_w[0], out_w[0].T[None]], axis=0)
    piece = jnp.where(me == 3, out_w[0].T, lax.dynamic_index_in_dim(qkv_w[0], jnp.minimum(me, 2), 0, False))
    attn_z = z_pieces(piece)
    got = [deal(lax.dynamic_index_in_dim(inputs[0], (t + k) % 2, 0, False), k) for k in range(2)]
    unit_quarter = up_w.shape[2] // 4
    ffn_local = jnp.stack([up_w[0].T.reshape(4, unit_quarter, feat), down_w[0].reshape(4, unit_quarter, feat)], axis=1)
    cross_other = to_decoder(after(cross_w[0], got[0]))
    cross_local = jnp.stack([cross_w[0, 0], cross_other[0], cross_other[1], cross_w[0, 1]])
    cross_piece = lax.dynamic_index_in_dim(cross_local, me, 0, False)

    own_info = jnp.concatenate(
        [lengths[0], lengths[1], row_flags[:, None], jnp.zeros((2, 7), jnp.int32)], axis=1
    ).astype(F32)
    mate_info = swap_dp(own_info, 1)
    row_info = jnp.where(t // 2 == core, own_info, mate_info)
    row_info = lax.dynamic_index_in_dim(row_info, t % 2, 0, False).astype(jnp.int32)
    flip = core * half + (t % 2) * chunk
    src_lens = row_info[0:8]
    dec_int = is_dec.astype(jnp.int32)

    def tail(causal):
        return jnp.stack([row_info[16], flip, causal, me, dec_int, t, 0, 0]).astype(jnp.int32)

    info = jnp.stack([
        jnp.concatenate([jnp.where(is_dec, row_info[8:16], src_lens), tail(dec_int)]),
        jnp.concatenate([src_lens, tail(0)]),
    ])

    gains = jnp.where(is_dec, norm_gain[1], norm_gain[0])
    shifts = jnp.where(is_dec, norm_bias[1], norm_bias[0])
    cgain, cshift = cross_gain[None], cross_bias[None]

    rows = (half, feat)
    full = (row_len, feat)
    column = (half, PAIR)
    wall = pltpu.VMEM((4, feat, feat), BF)
    units = pltpu.VMEM((4 * n_t, 2, unit_quarter, feat), BF)
    bias_n = pltpu.VMEM((half, row_len), F32)
    masks = [pltpu.VMEM((half, PAIR), BF), pltpu.VMEM((row_len, PAIR), BF)]
    bias_t = pltpu.VMEM((row_len, half), F32)
    rd_s = pltpu.VMEM((HEADS, 1, half), F32)

    def raw(*arrays):
        return [Raw(a) for a in arrays]

    def fetch(*arrays):
        return [Fetch(a) for a in arrays]

    def late(*shapes):
        return [Late(a) for a in shapes]

    attn_zs = jnp.stack(attn_z)
    ffn_z = z_pieces(after(lax.dynamic_index_in_dim(ffn_local, me, 0, False), attn_zs))
    attn_ys, info, gains, shifts = together(swap_dp(attn_zs, 2), info, gains, shifts)
    gain1, gain3 = gains[0:1], gains[1:2]
    shift1, shift3 = shifts[0:1], shifts[1:2]
    attn_ws = raw(attn_local, attn_zs, swap_dp(attn_zs, 1), attn_ys, swap_dp(attn_ys, 1))
    mates = [swap_dp(x, 1) for x in got]
    mid, mid_low, n1, inv1, q1, k1, v1, att1, lse1 = call(
        self_forward_kernel,
        [(rows, F32), (rows, BF), *late((rows, F32)), (column, F32), (rows, BF), (full, BF), (full, BF), (rows, BF),
         ((HEADS, 1, half), F32)],
        [info, *fetch(after(got[0], cross_piece), got[1], *mates), gain1, shift1, *attn_ws], [wall, *masks, bias_n], 20,
    )
    ffn_zs = jnp.stack(after(ffn_z, mid))
    ffn_ys = swap_dp(ffn_zs, 2)
    cross_z = z_pieces(after(cross_piece, mid))
    ffn_ys, *cross_z = together(ffn_ys, *cross_z)
    ffn_ws = raw(ffn_local, ffn_zs, swap_dp(ffn_zs, 1), ffn_ys, swap_dp(ffn_ys, 1))
    cross_zs = jnp.stack(cross_z)
    cross_ys = swap_dp(cross_zs, 2)
    mem0, mem1, n3e, inv3e = call(
        ffn_forward_kernel, [((chunk, feat), BF), ((chunk, feat), BF), (rows, F32), (column, F32)], [info, after(mid, cross_zs), gain3, shift3, *ffn_ws], [units], 8,
    )
    own1 = to_decoder(mem1)
    own0, cross_ys, cross_zm = together(to_decoder(mem0), cross_ys, swap_dp(cross_zs, 1))
    cross_ws = raw(cross_local, cross_zs, cross_zm, cross_ys, swap_dp(cross_ys, 1))
    cots = [deal(after(lax.dynamic_index_in_dim(cotangent[0], (t + k) % 2, 0, False), mem0), k) for k in range(2)]
    own1, cots[0] = together(own1, cots[0])
    mem = (own0, own1, swap_dp(own0, 1), swap_dp(own1, 1))

    h2, n2, inv2, q2, k2, v2, att2, lse2 = call(
        cross_forward_kernel,
        [(rows, F32), (rows, F32), (column, F32), (rows, BF), (full, BF), (full, BF), (rows, BF), ((HEADS, 1, half), F32)],
        [info, *fetch(*mem), mid_low, mid, cgain, cshift, *cross_ws], [wall, *masks], 20,
    )
    cots[1] = after(cots[1], h2)
    out0, out1, ffn_x, n3, inv3, dh1, dmem_own, dmem_mate, dbr2, dq2, dk2, dv2, dnorm2 = call(
        decoder_kernel,
        [((chunk, feat), BF), ((chunk, feat), BF), (rows, BF), (rows, F32), (column, F32), (rows, F32), (rows, BF), (rows, BF),
         (rows, BF), (rows, BF), (full, BF), (full, BF), ((8, feat), F32)],
        [info, h2, *fetch(*cots), n2, inv2, cgain, gain3, shift3, q2, k2, v2, att2, lse2, mid_low, mem0, mem1, n3e, inv3e, *cross_ws, *ffn_ws],
        [wall, units, bias_t, rd_s, pltpu.VMEM(rows, BF), pltpu.VMEM((half, 4 * n_t * unit_quarter), F32)], 30,
    )
    dmem_got = swap_dp(dmem_mate, 1)
    pieces = [((2, n_t, feat, quarter), BF)] * 2
    cross_keep, cross_send = call(
        cross_weights_kernel, pieces, [info, mid_low, dq2, *mem, dk2, dv2, dbr2, att2], vmem=8,
    )
    dmem = add_low(dmem_own, after(dmem_got, cross_keep))
    dmem_enc = to_encoder(dmem)
    cross_mate = swap_dp(after(cross_send, dmem), 1)
    cross_got = swap_dp(add_low(cross_keep[1], cross_mate[1]), 2)
    out_back = [deal_back(after(out, dmem), k) for k, out in enumerate((out0, out1))]
    dmem_enc, cross_got, *out_back = together(dmem_enc, cross_got, *out_back)
    cross_quarter = add_low(cross_keep[0], cross_mate[0], cross_got)

    ffn_pieces = ((2, n_t, unit_quarter, feat), BF)
    half_units = pltpu.VMEM((2 * n_t, 2, unit_quarter, feat), BF)
    up_send, down_send, acc, dbr3, dnorm3 = call(
        ffn_backward_mate_kernel, [ffn_pieces, ffn_pieces, (rows, F32), (rows, BF), ((8, feat), F32)],
        [info, ffn_x, n3, inv3, *fetch(*cots, dmem_enc), gain3, *ffn_ws], [half_units], 10,
    )
    up_mate, down_mate = swap_dp(up_send, 1), swap_dp(down_send, 1)
    do1, up_keep, down_keep, dr1, dbr1, dnorm1 = call(
        ffn_backward_own_kernel, [(rows, BF), ffn_pieces, ffn_pieces, (rows, F32), (rows, BF), ((8, feat), F32)],
        [info, ffn_x, dbr3, acc, *fetch(n1), inv1, gain1, dh1, *ffn_ws, *attn_ws], [half_units, wall], 11,
    )
    up_mate, down_mate = after(up_mate, do1), after(down_mate, do1)
    up_got = swap_dp(add_low(up_keep[1], up_mate[1]), 2)
    down_got = swap_dp(add_low(down_keep[1], down_mate[1]), 2)

    def self_backward(first, n_pairs, do):
        width = n_pairs * PAIR
        half_grad = ((2, half, width), BF)
        return call(
            functools.partial(self_backward_kernel, first), [((half, width), BF), half_grad, half_grad],
            [info, *raw(q1, k1, v1, att1), do, lse1],
            [bias_t, pltpu.VMEM((half, width), BF), pltpu.VMEM((row_len, width), BF), pltpu.VMEM((row_len, width), BF),
             pltpu.VMEM((half, width), BF), pltpu.VMEM((half, width), BF), rd_s,
             pltpu.VMEM((row_len, width), BF), pltpu.VMEM((row_len, width), BF)], 11,
        )

    cross_parts = z_parts(after(cross_quarter, do1))
    dq1, dkv_own, dkv_mate = call(
        self_backward_kernel, [(rows, BF), ((2, half, feat), BF), ((2, half, feat), BF)],
        [info, *fetch(q1, k1, v1, att1), do1, lse1], [bias_t, rd_s, pltpu.VMEM(full, BF), pltpu.VMEM(full, BF)], 18,
    )
    dkv_mate, up_got, *cross_parts = together(dkv_mate, up_got, *cross_parts)
    dkv_got = swap_dp(dkv_mate, 1)
    up_parts = z_parts(add_low(up_keep[0], up_mate[0], up_got))
    self_pieces = [((2, n_t, feat + 32, quarter), BF)] * 2
    self_keep, self_send, dk1, dv1 = call(
        self_weights_kernel, [*self_pieces, (rows, BF), (rows, BF)],
        [info, *fetch(*got), dq1, dkv_own, *fetch(dkv_got, att1), dbr1, dnorm1, dnorm2, dnorm3], vmem=10,
    )
    self_send, down_got, up_parts[1], up_parts[3] = together(self_send, down_got, up_parts[1], up_parts[3])
    self_mate = swap_dp(self_send, 1)
    down_parts = z_parts(add_low(down_keep[0], down_mate[0], down_got))
    dx0, dx1 = call(
        input_backward_kernel, [((chunk, feat), BF), ((chunk, feat), BF)],
        [info, dq1, after(dk1, self_mate), dv1, dr1, *attn_ws], [wall], 60,
    )
    self_got = swap_dp(add_low(self_keep[1], self_mate[1]), 2)
    self_got, dx0, dx1, up_parts[2], *down_parts = together(self_got, dx0, dx1, up_parts[2], *down_parts)
    ffn_back = jnp.stack([z_sum(up_parts), z_sum(down_parts)])
    self_parts = z_parts(add_low(self_keep[0], self_mate[0], self_got))
    cross_back = z_sum(after(cross_parts, self_got))
    cross_enc = to_encoder(cross_back)
    ffn_y, cross_enc, *self_parts = together(swap_dp(ffn_back, 2), cross_enc, *self_parts)
    cross_back = jnp.where(is_dec, cross_back, cross_enc)
    self_piece = z_sum(self_parts)
    self_back = self_piece[:feat]
    norms = self_piece[feat:].astype(F32).reshape(n_t, 8, PAIR).transpose(1, 0, 2).reshape(8, feat)
    other = lax.ppermute(norms, "section", [(0, 1), (1, 0)])
    ffn_two = jnp.stack([ffn_back, ffn_y])
    dx_back = [deal_back(after(dx, self_got), k) for k, dx in enumerate((dx0, dx1))]
    ffn_core = swap_dp(ffn_two, 1)

    def four(two, mate):
        return jnp.stack([two[0], mate[0], two[1], mate[1]])

    def matrix(stacked, which):
        return lax.dynamic_index_in_dim(stacked, me ^ which, 0, False).astype(F32)

    ffn_sum = four(ffn_two, ffn_core)
    ffn_true = [matrix(ffn_sum, m) for m in range(4)]
    up_grad = jnp.concatenate([f[0].T for f in ffn_true], axis=1)
    down_grad = jnp.concatenate([f[1] for f in ffn_true], axis=0)
    self_y, cross_y, other, up_grad, down_grad, *dx_back = together(
        swap_dp(self_back, 2), swap_dp(cross_back, 2), other, up_grad, down_grad, *dx_back
    )
    self_two = jnp.stack([self_back, self_y])
    cross_two = jnp.stack([cross_back, cross_y])
    self_core, cross_core = swap_dp(self_two, 1), swap_dp(cross_two, 1)
    self_sum = four(self_two, self_core)
    cross_sum = four(cross_two, cross_core)
    qkv_grad = jnp.stack([matrix(self_sum, m) for m in range(3)])
    out_grad = matrix(self_sum, 3).T
    cross_grad = jnp.stack([
        matrix(cross_sum, jnp.where(is_dec, 0, 1)), matrix(cross_sum, jnp.where(is_dec, 3, 2))
    ])

    enc = jnp.where(is_dec, other, norms)
    dec = jnp.where(is_dec, norms, other)
    full_gain = jnp.stack([enc[0:2], dec[0:2]])
    full_bias = jnp.stack([enc[2:4], dec[2:4]])

    def in_order(back):
        even = t % 2 == 0
        return jnp.stack([jnp.where(even, back[0], back[1]), jnp.where(even, back[1], back[0])])

    out_rows = in_order(out_back)
    grad_rows = in_order(dx_back).astype(F32)
    return (
        out_rows[None],
        grad_rows[None],
        qkv_grad[None],
        out_grad[None],
        cross_grad[None],
        up_grad[None],
        down_grad[None],
        full_gain,
        full_bias,
        dec[4],
        dec[5],
    )


def solution(mesh):
    return jax.shard_map(
        body,
        mesh=mesh,
        in_specs=(
            P("section", "dp", "tensor", None),
            P("section", "dp", "tensor", None),
            P(None, "dp", None),
            P("dp"),
            P("section", None, None, "tensor"),
            P("section", "tensor", None),
            P("section", None, None, "tensor"),
            P("section", None, "tensor"),
            P("section", "tensor", None),
            P(),
            P(),
            P(),
            P(),
        ),
        out_specs=(
            P("section", "dp", "tensor", None),
            P("section", "dp", "tensor", None),
            P("section", None, None, "tensor"),
            P("section", "tensor", None),
            P("section", None, None, "tensor"),
            P("section", None, "tensor"),
            P("section", "tensor", None),
            P(),
            P(),
            P(),
            P(),
        ),
        check_vma=False,
    )
```

```python
import functools

import jax
import jax.numpy as jnp
from jax import lax
from jax.experimental import pallas as pl
from jax.experimental.pallas import tpu as pltpu
from jax.sharding import PartitionSpec as P

HEADS = 8
HD = 64
PAIR = 2 * HD
SLOT_BITS = 7
SLOTS = 8
NEG = -(2.0 ** 100)
EPS = 1e-05
SCALE = HD ** -0.5
BF = jnp.bfloat16
F32 = jnp.float32
MIB = 1024 * 1024


def swap_dp(x, bit):
    n = lax.axis_size("dp")
    return lax.ppermute(x, "dp", [(i, i ^ bit) for i in range(n)])


def shift_tensor(x, step):
    n = lax.axis_size("tensor")
    return lax.ppermute(x, "tensor", [(i, (i + step) % n) for i in range(n)])


def swap_tensor(x, bit):
    n = lax.axis_size("tensor")
    return lax.ppermute(x, "tensor", [(i, i ^ bit) for i in range(n)])


def to_decoder(x):
    return lax.ppermute(x, "section", [(0, 1)])


def to_encoder(x):
    return lax.ppermute(x, "section", [(1, 0)])


def deal_route(k):
    n_t = lax.axis_size("tensor")
    route = []
    for d in range(lax.axis_size("dp")):
        group, core = divmod(d, 2)
        for t in range(n_t):
            plane = 2 * core + (t + k) % 2
            route.append((d * n_t + t, (2 * group + t // 2) * n_t + plane))
    return route


def deal(x, k):
    return lax.ppermute(x, ("dp", "tensor"), deal_route(k))


def deal_back(x, k):
    return lax.ppermute(x, ("dp", "tensor"), [(b, a) for a, b in deal_route(k)])


def together(*xs):
    return lax.optimization_barrier(xs)


def after(x, *events):
    return lax.optimization_barrier((x, *events))[0]


def z_pieces(piece):
    return [shift_tensor(piece, r) for r in range(1, 4)]


def add_low(*parts):
    return sum(p.astype(F32) for p in parts).astype(BF)


def other_groups(total):
    bit = 4
    while bit < lax.axis_size("dp"):
        total = add_low(total, swap_dp(total, bit))
        bit *= 2
    return total


def z_parts(quarter):
    return [quarter[0]] + [shift_tensor(quarter[r], -r) for r in range(1, 4)]


def z_sum(parts):
    return other_groups(add_low(*parts))


def dg(a, b, ca, cb):
    return lax.dot_general(a, b, (((ca,), (cb,)), ((), ())), preferred_element_type=F32)


def norm_fwd(r):
    off = r - jnp.mean(r, axis=-1, keepdims=True)
    inv = lax.rsqrt(jnp.mean(off * off, axis=-1, keepdims=True) + EPS)
    return off * inv, inv


def norm_bwd(dy, n, inv, gain):
    sc = dy * gain
    dr = inv * (
        sc
        - jnp.mean(sc, axis=-1, keepdims=True)
        - n * jnp.mean(sc * n, axis=-1, keepdims=True)
    )
    return dr, jnp.sum(dy * n, axis=0, keepdims=True), jnp.sum(dy, axis=0, keepdims=True)


def head_lanes(h):
    return (lax.broadcasted_iota(jnp.int32, (1, PAIR), 1) // HD) == h


def mask_bias(info, row, n_q, n_k, q_axis):
    flip = info[row, 9]
    q_shape = (n_q, 1) if q_axis == 0 else (1, n_q)
    full = (n_q, n_k) if q_axis == 0 else (n_k, n_q)
    q_pos = lax.broadcasted_iota(jnp.int32, q_shape, q_axis) ^ flip
    seg = jnp.where(info[row, 8] == 1, 0, q_pos >> SLOT_BITS)
    size = jnp.zeros(q_shape, jnp.int32)
    for j in range(SLOTS):
        size = size + jnp.where(seg == j, info[row, j], 0)
    first = seg << SLOT_BITS
    end = first + size
    end = jnp.where(info[row, 10] == 1, jnp.minimum(end, q_pos + 1), end)
    k_pos = lax.broadcasted_iota(jnp.int32, full, 1 - q_axis) ^ flip
    return jnp.where((k_pos >= first) & (k_pos < end), 0.0, NEG)


class Copies:
    def __init__(self, sems):
        self.sems = sems
        self.count = 0

    def start(self, src, dst):
        copy = pltpu.make_async_copy(src, dst, self.sems.at[self.count])
        self.count += 1
        copy.start()
        return copy


class Raw:
    def __init__(self, value):
        self.value = value


class Fetch(Raw):
    pass


class Late(Raw):
    pass


class Fetched:
    def __init__(self, copy, ref):
        self.copy = copy
        self.ref = ref
        self.shape = ref.shape

    def ready(self):
        if self.copy is not None:
            self.copy.wait()
            self.copy = None
        return self.ref

    def __getitem__(self, at):
        return self.ready()[at]


class Result:
    def __init__(self, copies, ref, dst):
        self.copies = copies
        self.ref = ref
        self.dst = dst
        self.shape = ref.shape
        self.copy = None

    def __setitem__(self, at, value):
        self.ref[at] = value

    def __getitem__(self, at):
        return self.ref[at]

    def flush(self):
        if self.copy is None:
            self.copy = self.copies.start(self.ref, self.dst)


def load_wall(copies, me, refs, wall):
    local, *pieces = refs
    started = []
    for rel, ref in enumerate(pieces):
        started.append(copies.start(local.at[me ^ rel], wall.at[rel, :, pl.ds(0, PAIR)]))
        for z in range(1, 4):
            started.append(copies.start(ref.at[z - 1], wall.at[rel, :, pl.ds(z * PAIR, PAIR)]))
    return started


def load_units(copies, me, refs, units, rels=range(4)):
    local, *pieces = refs
    started = []
    for i, rel in enumerate(rels):
        started.append(copies.start(local.at[me ^ rel], units.at[4 * i]))
        started.append(copies.start(pieces[rel], units.at[pl.ds(4 * i + 1, 3)]))
    return started


def wait_all(started):
    for copy in started:
        copy.wait()


def unit_block(units, which, i):
    return jnp.concatenate([units[2 * i, which], units[2 * i + 1, which]], axis=0)


def mask_columns(info, row, n, of_queries):
    pos = lax.broadcasted_iota(jnp.int32, (n, 1), 0) ^ info[row, 9]
    seg = jnp.where(info[row, 8] == 1, 0, pos >> SLOT_BITS)
    lane = lax.broadcasted_iota(jnp.int32, (1, PAIR), 1) % HD
    if of_queries:
        return jnp.where(lane == seg, 1.0, 0.0).astype(BF)
    size = jnp.zeros((n, 1), jnp.int32)
    for j in range(SLOTS):
        size = size + jnp.where(seg == j, info[row, j], 0)
    counts = (lane == seg) & (pos - (seg << SLOT_BITS) < size)
    return jnp.where(lane < SLOTS, jnp.where(counts, 0.0, NEG), 0.0).astype(BF)


def attend_forward(info, row, q_ref, k_ref, v_ref, att_ref, lse_ref, qm_ref, km_ref, bias_ref=None):
    n_q = q_ref.shape[0]
    lane = lax.broadcasted_iota(jnp.int32, (1, PAIR), 1)

    def heads(causal):
        qm_ref[...] = mask_columns(info, row, n_q, True)
        if causal:
            km_ref[...] = jnp.zeros_like(km_ref)
            bias_ref[...] = mask_bias(info, row, n_q, k_ref.shape[0], 0)
        else:
            km_ref[...] = mask_columns(info, row, k_ref.shape[0], False)
        lse = jnp.zeros((n_q, PAIR), F32)
        for hp in range(HEADS // 2):
            sl = slice(hp * PAIR, (hp + 1) * PAIR)
            qp, kp, vp = q_ref[:, sl], k_ref[:, sl], v_ref[:, sl]
            outs = []
            for h in range(2):
                own = head_lanes(h)
                s = dg(jnp.where(own, qp, qm_ref[...]), jnp.where(own, kp, km_ref[...]), 1, 1)
                if causal:
                    s = s + bias_ref[...]
                top = jnp.max(s, axis=1, keepdims=True)
                e = jnp.exp(s - top).astype(BF)
                o = dg(e, jnp.where(own, vp, jnp.ones_like(vp)), 1, 0)
                at = (1 - h) * HD
                total = o[:, at : at + 1]
                outs.append(o * (1.0 / total))
                lse = jnp.where(lane == 2 * hp + h, top + jnp.log(total), lse)
            att_ref[:, sl] = jnp.where(head_lanes(0), outs[0], outs[1]).astype(BF)
        rows = jnp.transpose(lse)
        for h in range(HEADS):
            lse_ref[h] = rows[h : h + 1]

    if bias_ref is None:
        heads(False)
    else:
        pl.when(info[row, 10] == 1)(lambda: heads(True))
        pl.when(info[row, 10] != 1)(lambda: heads(False))


def attend_backward(info, row, n_pairs, q_ref, k_ref, v_ref, do_ref, att_ref, lse_ref, bias_ref, rd_ref, dq_ref, dk_ref, dv_ref):
    n_q = q_ref.shape[0]
    block = 256
    empty = info[row, 0]
    for j in range(1, SLOTS):
        empty = empty + info[row, j]
    empty = empty == 0
    p_fix = jnp.where(empty, 1.0 / k_ref.shape[0], 1.0)
    s_fix = jnp.where(empty, 0.0, 1.0)
    width = n_pairs * PAIR
    prod = do_ref[...].astype(F32) * att_ref[...].astype(F32)
    high = prod.astype(BF)
    low = (prod - high.astype(F32)).astype(BF)
    heads = lax.broadcasted_iota(jnp.int32, (HEADS, width), 0)
    lanes_of = lax.broadcasted_iota(jnp.int32, (HEADS, width), 1) // HD
    ones = jnp.where(heads == lanes_of, 1.0, 0.0).astype(BF)
    rd = dg(ones, high, 1, 1) + dg(ones, low, 1, 1)
    for h in range(2 * n_pairs):
        rd_ref[h] = rd[h : h + 1]

    def pair(hp, _):
        sl = pl.ds(pl.multiple_of(hp * PAIR, PAIR), PAIR)
        kp = k_ref[:, sl]
        vp = v_ref[:, sl]
        k_t = jnp.transpose(kp)
        dk = dv = None
        for qi in range(n_q // block):
            qs = slice(qi * block, (qi + 1) * block)
            qp = q_ref[qs, sl]
            dop = do_ref[qs, sl]
            dqs = []
            for h in range(2):
                lanes = head_lanes(h)
                qm = jnp.where(lanes, qp, jnp.zeros_like(qp))
                dom = jnp.where(lanes, dop, jnp.zeros_like(dop))
                s = dg(kp, qm, 1, 1) + bias_ref[:, qs]
                p = jnp.exp(s - lse_ref[hp * 2 + h, :, qs])
                dp = dg(vp, dom, 1, 1)
                ds = (p * (dp - rd_ref[hp * 2 + h, :, qs])).astype(BF)
                a = dg(p.astype(BF), dom, 1, 0)
                dv = a if dv is None else dv + a
                a = dg(ds, qm, 1, 0)
                dk = a if dk is None else dk + a
                dqs.append(dg(k_t[h * HD : (h + 1) * HD], ds, 1, 0))
            dq = jnp.transpose(jnp.concatenate(dqs, axis=0))
            dq_ref[qs, sl] = (dq * (SCALE * s_fix)).astype(BF)
        dk_ref[:, sl] = (dk * s_fix).astype(BF)
        dv_ref[:, sl] = (dv * p_fix).astype(BF)
        return 0

    lax.fori_loop(0, n_pairs, pair, 0)


def self_forward_kernel(copies, info, x0, x1, x2, x3, gain, shift, *refs):
    w_refs = refs[:5]
    y_out, low_out, n_out, inv_out, q_out, k_out, v_out, att_out, lse_out, wall, qm_ref, km_ref, bias_ref = refs[5:]
    me = info[0, 11]
    started = load_wall(copies, me, w_refs, wall)
    wait_all(started)
    rows_low = jnp.concatenate([x0[...], x1[...]], axis=0)
    q_out[...] = dg(rows_low, wall[me], 1, 0).astype(BF) * jnp.asarray(SCALE, BF)
    wk = wall[me ^ 1]
    wv = wall[me ^ 2]
    at = 0
    for ref in (x0, x1, x2, x3):
        part = ref[...]
        k_out[at : at + ref.shape[0]] = dg(part, wk, 1, 0).astype(BF)
        v_out[at : at + ref.shape[0]] = dg(part, wv, 1, 0).astype(BF)
        at += ref.shape[0]
    attend_forward(info, 0, q_out, k_out, v_out, att_out, lse_out, qm_ref, km_ref, bias_ref)
    n, inv = norm_fwd(rows_low.astype(F32) + dg(att_out[...], wall[me ^ 3], 1, 1))
    n_out[...] = n
    inv_out[...] = jnp.broadcast_to(inv, inv_out.shape)
    y = n * gain[...] + shift[...]
    y_out[...] = y
    low_out[...] = y.astype(BF)


def silu_parts(u):
    sg = jax.nn.sigmoid(u)
    return u * sg, sg


def ffn_forward_kernel(copies, info, x_ref, gain, shift, *refs):
    low0, low1, n_out, inv_out, units = refs[5:]
    started = load_units(copies, info[0, 11], refs[:5], units)
    x = x_ref[...]
    low = x.astype(BF)
    acc = x
    wait_all(started)
    for i in range(units.shape[0] // 2):
        u = dg(low, unit_block(units, 0, i), 1, 1)
        act = silu_parts(u)[0].astype(BF)
        acc = acc + dg(act, unit_block(units, 1, i), 1, 0)
    n, inv = norm_fwd(acc)
    y = (n * gain[...] + shift[...]).astype(BF)
    low0[...] = y[: low0.shape[0]]
    low1[...] = y[low0.shape[0] :]
    n_out[...] = n
    inv_out[...] = jnp.broadcast_to(inv, inv_out.shape)


def cross_forward_kernel(copies, info, own0, own1, mate0, mate1, h_low, h_ref, cgain, cshift, *refs):
    y_out, n_out, inv_out, q_out, k_out, v_out, att_out, lse_out, wall, qm_ref, km_ref = refs[5:]
    me = info[1, 11]
    started = load_wall(copies, me, refs[:5], wall)
    wait_all(started)
    q_out[...] = dg(h_low[...], wall[me], 1, 0).astype(BF) * jnp.asarray(SCALE, BF)
    half = own0.shape[0]
    for ref, at in ((own0, 0), (own1, half), (mate0, 2 * half), (mate1, 3 * half)):
        k_out[at : at + half] = dg(ref[...], wall[me ^ 1], 1, 0).astype(BF)
        v_out[at : at + half] = dg(ref[...], wall[me ^ 2], 1, 0).astype(BF)
    attend_forward(info, 1, q_out, k_out, v_out, att_out, lse_out, qm_ref, km_ref)
    n, inv = norm_fwd(h_ref[...] + dg(att_out[...], wall[me ^ 3], 1, 1))
    n_out[...] = n
    inv_out[...] = jnp.broadcast_to(inv, inv_out.shape)
    y_out[...] = n * cgain[...] + cshift[...]


def decoder_kernel(copies, info, h_ref, cot0, cot1, n2_ref, inv2_ref, cgain, gain3, shift3, q_ref, k_ref, v_ref, att_ref, lse_ref,
                   h_low, mem_low0, mem_low1, n3e, inv3e, *refs):
    w_refs, unit_refs = refs[:5], refs[5:10]
    (out0, out1, x_ref, n3_ref, inv3_ref, dh_out, dmem_own_out, dmem_mate_out, dbr_out, dq_out, dk_out, dv_out, dnorm_out,
     wall, units, bias_ref, rd_ref, do_ref, u_ref) = refs[10:]
    me = info[1, 11]
    dec = info[1, 12] == 1
    started = load_units(copies, me, unit_refs, units)
    wall_started = load_wall(copies, me, w_refs, wall)
    bias_ref[...] = mask_bias(info, 1, q_ref.shape[0], k_ref.shape[0], 1)
    acc = h_ref[...]
    low = acc.astype(BF)
    x_ref[...] = low
    wait_all(started)
    width = 2 * PAIR
    blocks = units.shape[0] // 2
    for i in range(blocks):
        u = dg(low, unit_block(units, 0, i), 1, 1)
        u_ref[:, i * width : (i + 1) * width] = u
        act = silu_parts(u)[0].astype(BF)
        acc = acc + dg(act, unit_block(units, 1, i), 1, 0)
    n, inv = norm_fwd(acc)
    y = (n * gain3[...] + shift3[...]).astype(BF)
    half = out0.shape[0]
    out0[...] = y[:half]
    out1[...] = y[half:]
    n3_ref[...] = n
    inv3_ref[...] = jnp.broadcast_to(inv, inv3_ref.shape)
    passed = ((out0, mem_low0[...]), (out1, mem_low1[...]), (x_ref, h_low[...]), (n3_ref, n3e[...]), (inv3_ref, inv3e[...]))
    for ref, src in passed:
        ref[...] = jnp.where(dec, ref[...], src)
    cot = jnp.concatenate([cot0[...], cot1[...]], axis=0).astype(F32)
    dr, _, _ = norm_bwd(cot, n, inv, gain3[...])
    dbr = dr.astype(BF)
    acc = dr
    for i in range(blocks):
        u = u_ref[:, i * width : (i + 1) * width]
        sg = jax.nn.sigmoid(u)
        dact = dg(dbr, unit_block(units, 1, i), 1, 1)
        du = (dact * sg * (1.0 + u * (1.0 - sg))).astype(BF)
        acc = acc + dg(du, unit_block(units, 0, i), 1, 0)
    dr, dg_sum, db_sum = norm_bwd(acc, n2_ref[...], inv2_ref[:, 0:1], cgain[...])
    dnorm_out[0:1] = dg_sum
    dnorm_out[1:2] = db_sum
    dh_out[...] = dr
    dbr = dr.astype(BF)
    dbr_out[...] = dbr
    wait_all(wall_started)
    do_ref[...] = dg(dbr, wall[me ^ 3], 1, 0).astype(BF)
    attend_backward(info, 1, HEADS // 2, q_ref, k_ref, v_ref, do_ref, att_ref, lse_ref, bias_ref, rd_ref, dq_out, dk_out, dv_out)
    half = dmem_own_out.shape[0]
    wk = wall[me ^ 1]
    wv = wall[me ^ 2]
    for out, at in ((dmem_mate_out, half), (dmem_own_out, 0)):
        part = dg(dk_out[at : at + half], wk, 1, 1) + dg(dv_out[at : at + half], wv, 1, 1)
        out[...] = part.astype(BF)
    dh_out[...] = dh_out[...] + dg(dq_out[...], wall[me], 1, 1)


def put_matrix(keep_ref, send_ref, me, which, value):
    slot = me ^ which
    y = slot >> 1

    def put(ref):
        for z in range(4):
            ref[y, z, : value.shape[0]] = value[:, z * PAIR : (z + 1) * PAIR]

    @pl.when(slot % 2 == 0)
    def _():
        put(keep_ref)

    @pl.when(slot % 2 == 1)
    def _():
        put(send_ref)


def cross_weights_kernel(copies, info, h_low, dq_ref, own0, own1, mate0, mate1, dk_ref, dv_ref, dbr_ref, att_ref, keep, send):
    me = info[1, 11]
    mem = jnp.concatenate([own0[...], own1[...], mate0[...], mate1[...]], axis=0)


    put_matrix(keep, send, me, 0, dg(h_low[...], dq_ref[...], 0, 0).astype(BF))
    for which, ref in ((1, dk_ref), (2, dv_ref)):
        value = dg(mem, ref[...], 0, 0)
        put_matrix(keep, send, me, which, value.astype(BF))
    put_matrix(keep, send, me, 3, dg(dbr_ref[...], att_ref[...], 0, 0).astype(BF))


def ffn_backward_part(low, dbr, acc, units, up_grad, down_grad):
    for i in range(units.shape[0] // 2):
        y, z = i // 2, i % 2
        wu = unit_block(units, 0, i)
        wd = unit_block(units, 1, i)
        u_t = dg(wu, low, 1, 1)
        act_t, sg = silu_parts(u_t)
        act_t = act_t.astype(BF)
        dact_t = dg(wd, dbr, 1, 1)
        du_t = (dact_t * sg * (1.0 + u_t * (1.0 - sg))).astype(BF)
        acc = acc + dg(du_t, wu, 0, 0)
        dup = dg(du_t, low, 1, 0).astype(BF)
        ddown = dg(act_t, dbr, 1, 0).astype(BF)
        for j in range(2):
            up_grad[y, 2 * z + j] = dup[j * PAIR : (j + 1) * PAIR]
            down_grad[y, 2 * z + j] = ddown[j * PAIR : (j + 1) * PAIR]
    return acc


def ffn_backward_mate_kernel(copies, info, x_ref, n3_ref, inv3_ref, cot0, cot1, dmem_ref, gain3, *refs):
    up_send, down_send, acc_out, dbr_out, dnorm_out, units = refs[5:]
    started = load_units(copies, info[0, 11], refs[:5], units, (1, 3))
    dy = jnp.concatenate([cot0[...], cot1[...]], axis=0).astype(F32) + dmem_ref[...].astype(F32)
    dr3, dg3, db3 = norm_bwd(dy, n3_ref[...], inv3_ref[:, 0:1], gain3[...])
    dnorm_out[0:1] = dg3
    dnorm_out[1:2] = db3
    dbr = dr3.astype(BF)
    dbr_out[...] = dbr
    wait_all(started)
    acc_out[...] = ffn_backward_part(x_ref[...], dbr, dr3, units, up_send, down_send)


def ffn_backward_own_kernel(copies, info, x_ref, dbr_ref, acc_ref, n1_ref, inv1_ref, gain1, dmid_ref, *refs):
    do_out, up_keep, down_keep, dr1_out, dbr1_out, dnorm_out, units, wall = refs[10:]
    me = info[0, 11]
    started = load_units(copies, me, refs[:5], units, (0, 2))
    wall_started = load_wall(copies, me, refs[5:10], wall)
    wait_all(started)
    acc = ffn_backward_part(x_ref[...], dbr_ref[...], acc_ref[...], units, up_keep, down_keep)
    dmid = jnp.where(info[0, 12] == 1, dmid_ref[...], acc)
    dr1, dg1, db1 = norm_bwd(dmid, n1_ref[...], inv1_ref[:, 0:1], gain1[...])
    dr1_out[...] = dr1
    dbr1 = dr1.astype(BF)
    dbr1_out[...] = dbr1
    dnorm_out[0:1] = dg1
    dnorm_out[1:2] = db1
    wait_all(wall_started)
    do_out[...] = dg(dbr1, wall[me ^ 3], 1, 0).astype(BF)


def self_backward_kernel(copies, info, q_ref, k_ref, v_ref, att_ref, do_ref, lse_ref, dq_out, own, mate, bias_ref, rd_ref, dk_ref, dv_ref):
    bias_ref[...] = mask_bias(info, 0, q_ref.shape[0], k_ref.shape[0], 1)
    q, k, v, att = q_ref.ready(), k_ref.ready(), v_ref.ready(), att_ref.ready()
    attend_backward(info, 0, HEADS // 2, q, k, v, do_ref, att, lse_ref, bias_ref, rd_ref, dq_out, dk_ref, dv_ref)
    half = q_ref.shape[0]
    for dst, at in ((mate, half), (own, 0)):
        dst[0] = dk_ref[at : at + half]
        dst[1] = dv_ref[at : at + half]


def self_weights_kernel(copies, info, x0, x1, dq_ref, own, got, att_ref, dbr_ref, dnorm1, dnorm2, dnorm3, keep, send, dk_out, dv_out):
    me = info[0, 11]
    dq = dq_ref[...]
    dk = (own[0].astype(F32) + got[0].astype(F32)).astype(BF)
    dv = (own[1].astype(F32) + got[1].astype(F32)).astype(BF)
    dk_out[...] = dk
    dv_out[...] = dv
    x = jnp.concatenate([x0[...], x1[...]], axis=0)
    for which, value in ((0, dq), (1, dk), (2, dv)):
        put_matrix(keep, send, me, which, dg(x, value, 0, 0).astype(BF))
    put_matrix(keep, send, me, 3, dg(dbr_ref[...], att_ref[...], 0, 0).astype(BF))
    feat = dq.shape[1]
    norms = jnp.concatenate([dnorm1[0:1], dnorm3[0:1], dnorm1[1:2], dnorm3[1:2], dnorm2[0:2], jnp.zeros((2, feat), F32)], axis=0)
    rows = jnp.concatenate([norms[:, i * PAIR : (i + 1) * PAIR] for i in range(feat // PAIR)], axis=0).astype(BF)
    for out in (keep, send):
        for y in range(2):
            for z in range(4):
                out[y, z, feat:] = rows


def input_backward_kernel(copies, info, dq_ref, dk_ref, dv_ref, dr_ref, *refs):
    dx0, dx1, wall = refs[5:]
    me = info[0, 11]
    started = load_wall(copies, me, refs[:5], wall)
    wait_all(started)
    dx = dr_ref[...] + dg(dq_ref[...], wall[me], 1, 1) + dg(dk_ref[...], wall[me ^ 1], 1, 1) + dg(dv_ref[...], wall[me ^ 2], 1, 1)
    half = dx0.shape[0]
    dx0[...] = dx[:half].astype(BF)
    dx1[...] = dx[half:].astype(BF)


US = {
    "self_forward_kernel": 13.5, "ffn_forward_kernel": 4.5, "cross_forward_kernel": 13.5, "decoder_kernel": 23.0,
    "cross_weights_kernel": 3.7, "ffn_backward_mate_kernel": 6.0, "ffn_backward_own_kernel": 6.7,
    "self_backward_kernel": 7.5, "self_weights_kernel": 3.5, "input_backward_kernel": 2.0,
}


def call(kernel, outs, args, scratch=(), vmem=60):
    in_hbm = pl.BlockSpec(memory_space=pltpu.HBM)
    in_vmem = pl.BlockSpec(memory_space=pltpu.VMEM)
    in_smem = pl.BlockSpec(memory_space=pltpu.SMEM)
    us = 0.01 * US[getattr(kernel, "func", kernel).__name__]
    arrays = [a.value if isinstance(a, Raw) else a for a in args]
    shapes = [o.value if isinstance(o, Raw) else o for o in outs]
    moved = [pltpu.VMEM(a.value.shape, a.value.dtype) for a in args if isinstance(a, Fetch)]
    moved += [pltpu.VMEM(*o.value) for o in outs if isinstance(o, Late)]

    def wrapped(*refs):
        ins, refs = refs[: len(arrays)], refs[len(arrays) :]
        results, refs = refs[: len(shapes)], refs[len(shapes) :]
        buffers, rest, sems = list(refs[: len(moved)]), refs[len(moved) : -1], refs[-1]
        copies = Copies(sems)
        given = []
        for ref, arg in zip(ins, args):
            if isinstance(arg, Fetch):
                buffer = buffers.pop(0)
                ref = Fetched(copies.start(ref, buffer), buffer)
            given.append(ref)
        produced = []
        for ref, out in zip(results, outs):
            produced.append(Result(copies, buffers.pop(0), ref) if isinstance(out, Late) else ref)
        kernel(copies, *given, *produced, *rest)
        for ref in given:
            if isinstance(ref, Fetched):
                ref.ready()
        for out in produced:
            if isinstance(out, Result):
                out.flush()
        for out in produced:
            if isinstance(out, Result):
                out.copy.wait()

    return pl.pallas_call(
        wrapped,
        out_shape=tuple(jax.ShapeDtypeStruct(*o) for o in shapes),
        in_specs=[
            in_hbm if isinstance(a, Raw) else in_smem if a.dtype == jnp.int32 else in_vmem for a in args
        ],
        out_specs=tuple(in_hbm if isinstance(o, Raw) else in_vmem for o in outs),
        scratch_shapes=[*moved, *scratch, pltpu.SemaphoreType.DMA((64,))],
        compiler_params=pltpu.CompilerParams(vmem_limit_bytes=vmem * MIB),
        cost_estimate=pl.CostEstimate(flops=int(us * 1e9), bytes_accessed=int(us * 2e6), transcendentals=0),
    )(*arrays)


def body(
    inputs,
    cotangent,
    lengths,
    row_flags,
    qkv_w,
    out_w,
    cross_w,
    up_w,
    down_w,
    norm_gain,
    norm_bias,
    cross_gain,
    cross_bias,
):
    section = lax.axis_index("section")
    is_dec = section == 1
    d = lax.axis_index("dp")
    t = lax.axis_index("tensor")
    core = d % 2
    me = d % 4
    feat = inputs.shape[3]
    chunk = inputs.shape[2]
    half = 2 * chunk
    row_len = 2 * half
    quarter = qkv_w.shape[3]
    n_t = 4

    attn_local = jnp.concatenate([qkv_w[0], out_w[0].T[None]], axis=0)
    piece = jnp.where(me == 3, out_w[0].T, lax.dynamic_index_in_dim(qkv_w[0], jnp.minimum(me, 2), 0, False))
    attn_z = z_pieces(piece)
    got = [deal(lax.dynamic_index_in_dim(inputs[0], (t + k) % 2, 0, False), k) for k in range(2)]
    unit_quarter = up_w.shape[2] // 4
    ffn_local = jnp.stack([up_w[0].T.reshape(4, unit_quarter, feat), down_w[0].reshape(4, unit_quarter, feat)], axis=1)
    cross_other = to_decoder(after(cross_w[0], got[0]))
    cross_local = jnp.stack([cross_w[0, 0], cross_other[0], cross_other[1], cross_w[0, 1]])
    cross_piece = lax.dynamic_index_in_dim(cross_local, me, 0, False)

    own_info = jnp.concatenate(
        [lengths[0], lengths[1], row_flags[:, None], jnp.zeros((2, 7), jnp.int32)], axis=1
    ).astype(F32)
    mate_info = swap_dp(own_info, 1)
    row_info = jnp.where(t // 2 == core, own_info, mate_info)
    row_info = lax.dynamic_index_in_dim(row_info, t % 2, 0, False).astype(jnp.int32)
    flip = core * half + (t % 2) * chunk
    src_lens = row_info[0:8]
    dec_int = is_dec.astype(jnp.int32)

    def tail(causal):
        return jnp.stack([row_info[16], flip, causal, me, dec_int, t, 0, 0]).astype(jnp.int32)

    info = jnp.stack([
        jnp.concatenate([jnp.where(is_dec, row_info[8:16], src_lens), tail(dec_int)]),
        jnp.concatenate([src_lens, tail(0)]),
    ])

    gains = jnp.where(is_dec, norm_gain[1], norm_gain[0])
    shifts = jnp.where(is_dec, norm_bias[1], norm_bias[0])
    cgain, cshift = cross_gain[None], cross_bias[None]

    rows = (half, feat)
    full = (row_len, feat)
    column = (half, PAIR)
    wall = pltpu.VMEM((4, feat, feat), BF)
    units = pltpu.VMEM((4 * n_t, 2, unit_quarter, feat), BF)
    bias_n = pltpu.VMEM((half, row_len), F32)
    masks = [pltpu.VMEM((half, PAIR), BF), pltpu.VMEM((row_len, PAIR), BF)]
    bias_t = pltpu.VMEM((row_len, half), F32)
    rd_s = pltpu.VMEM((HEADS, 1, half), F32)

    def raw(*arrays):
        return [Raw(a) for a in arrays]

    def fetch(*arrays):
        return [Fetch(a) for a in arrays]

    def late(*shapes):
        return [Late(a) for a in shapes]

    attn_zs = jnp.stack(attn_z)
    ffn_z = z_pieces(after(lax.dynamic_index_in_dim(ffn_local, me, 0, False), attn_zs))
    attn_ys, info, gains, shifts = together(swap_dp(attn_zs, 2), info, gains, shifts)
    gain1, gain3 = gains[0:1], gains[1:2]
    shift1, shift3 = shifts[0:1], shifts[1:2]
    attn_ws = raw(attn_local, attn_zs, swap_dp(attn_zs, 1), attn_ys, swap_dp(attn_ys, 1))
    mates = [swap_dp(x, 1) for x in got]
    mid, mid_low, n1, inv1, q1, k1, v1, att1, lse1 = call(
        self_forward_kernel,
        [(rows, F32), (rows, BF), *late((rows, F32)), (column, F32), (rows, BF), (full, BF), (full, BF), (rows, BF),
         ((HEADS, 1, half), F32)],
        [info, *fetch(after(got[0], cross_piece), got[1], *mates), gain1, shift1, *attn_ws], [wall, *masks, bias_n], 20,
    )
    ffn_zs = jnp.stack(after(ffn_z, mid))
    ffn_ys = swap_dp(ffn_zs, 2)
    cross_z = z_pieces(after(cross_piece, mid))
    ffn_ys, *cross_z = together(ffn_ys, *cross_z)
    ffn_ws = raw(ffn_local, ffn_zs, swap_dp(ffn_zs, 1), ffn_ys, swap_dp(ffn_ys, 1))
    cross_zs = jnp.stack(cross_z)
    cross_ys = swap_dp(cross_zs, 2)
    mem0, mem1, n3e, inv3e = call(
        ffn_forward_kernel, [((chunk, feat), BF), ((chunk, feat), BF), (rows, F32), (column, F32)], [info, after(mid, cross_zs), gain3, shift3, *ffn_ws], [units], 8,
    )
    own1 = to_decoder(mem1)
    own0, cross_ys, cross_zm = together(to_decoder(mem0), cross_ys, swap_dp(cross_zs, 1))
    cross_ws = raw(cross_local, cross_zs, cross_zm, cross_ys, swap_dp(cross_ys, 1))
    cots = [deal(after(lax.dynamic_index_in_dim(cotangent[0], (t + k) % 2, 0, False), mem0), k) for k in range(2)]
    own1, cots[0] = together(own1, cots[0])
    mem = (own0, own1, swap_dp(own0, 1), swap_dp(own1, 1))

    h2, n2, inv2, q2, k2, v2, att2, lse2 = call(
        cross_forward_kernel,
        [(rows, F32), (rows, F32), (column, F32), (rows, BF), (full, BF), (full, BF), (rows, BF), ((HEADS, 1, half), F32)],
        [info, *fetch(*mem), mid_low, mid, cgain, cshift, *cross_ws], [wall, *masks], 20,
    )
    cots[1] = after(cots[1], h2)
    out0, out1, ffn_x, n3, inv3, dh1, dmem_own, dmem_mate, dbr2, dq2, dk2, dv2, dnorm2 = call(
        decoder_kernel,
        [((chunk, feat), BF), ((chunk, feat), BF), (rows, BF), (rows, F32), (column, F32), (rows, F32), (rows, BF), (rows, BF),
         (rows, BF), (rows, BF), (full, BF), (full, BF), ((8, feat), F32)],
        [info, h2, *fetch(*cots), n2, inv2, cgain, gain3, shift3, q2, k2, v2, att2, lse2, mid_low, mem0, mem1, n3e, inv3e, *cross_ws, *ffn_ws],
        [wall, units, bias_t, rd_s, pltpu.VMEM(rows, BF), pltpu.VMEM((half, 4 * n_t * unit_quarter), F32)], 30,
    )
    dmem_got = swap_dp(dmem_mate, 1)
    pieces = [((2, n_t, feat, quarter), BF)] * 2
    cross_keep, cross_send = call(
        cross_weights_kernel, pieces, [info, mid_low, dq2, *mem, dk2, dv2, dbr2, att2], vmem=8,
    )
    dmem = add_low(dmem_own, after(dmem_got, cross_keep))
    dmem_enc = to_encoder(dmem)
    cross_mate = swap_dp(after(cross_send, dmem), 1)
    cross_got = swap_dp(add_low(cross_keep[1], cross_mate[1]), 2)
    out_back = [deal_back(after(out, dmem), k) for k, out in enumerate((out0, out1))]
    dmem_enc, cross_got, *out_back = together(dmem_enc, cross_got, *out_back)
    cross_quarter = add_low(cross_keep[0], cross_mate[0], cross_got)

    ffn_pieces = ((2, n_t, unit_quarter, feat), BF)
    half_units = pltpu.VMEM((2 * n_t, 2, unit_quarter, feat), BF)
    up_send, down_send, acc, dbr3, dnorm3 = call(
        ffn_backward_mate_kernel, [ffn_pieces, ffn_pieces, (rows, F32), (rows, BF), ((8, feat), F32)],
        [info, ffn_x, n3, inv3, *fetch(*cots, dmem_enc), gain3, *ffn_ws], [half_units], 10,
    )
    up_mate, down_mate = swap_dp(up_send, 1), swap_dp(down_send, 1)
    do1, up_keep, down_keep, dr1, dbr1, dnorm1 = call(
        ffn_backward_own_kernel, [(rows, BF), ffn_pieces, ffn_pieces, (rows, F32), (rows, BF), ((8, feat), F32)],
        [info, ffn_x, dbr3, acc, *fetch(n1), inv1, gain1, dh1, *ffn_ws, *attn_ws], [half_units, wall], 11,
    )
    up_mate, down_mate = after(up_mate, do1), after(down_mate, do1)
    up_got = swap_dp(add_low(up_keep[1], up_mate[1]), 2)
    down_got = swap_dp(add_low(down_keep[1], down_mate[1]), 2)

    def self_backward(first, n_pairs, do):
        width = n_pairs * PAIR
        half_grad = ((2, half, width), BF)
        return call(
            functools.partial(self_backward_kernel, first), [((half, width), BF), half_grad, half_grad],
            [info, *raw(q1, k1, v1, att1), do, lse1],
            [bias_t, pltpu.VMEM((half, width), BF), pltpu.VMEM((row_len, width), BF), pltpu.VMEM((row_len, width), BF),
             pltpu.VMEM((half, width), BF), pltpu.VMEM((half, width), BF), rd_s,
             pltpu.VMEM((row_len, width), BF), pltpu.VMEM((row_len, width), BF)], 11,
        )

    cross_parts = z_parts(after(cross_quarter, do1))
    dq1, dkv_own, dkv_mate = call(
        self_backward_kernel, [(rows, BF), ((2, half, feat), BF), ((2, half, feat), BF)],
        [info, *fetch(q1, k1, v1, att1), do1, lse1], [bias_t, rd_s, pltpu.VMEM(full, BF), pltpu.VMEM(full, BF)], 18,
    )
    dkv_mate, up_got, *cross_parts = together(dkv_mate, up_got, *cross_parts)
    dkv_got = swap_dp(dkv_mate, 1)
    up_parts = z_parts(add_low(up_keep[0], up_mate[0], up_got))
    self_pieces = [((2, n_t, feat + 32, quarter), BF)] * 2
    self_keep, self_send, dk1, dv1 = call(
        self_weights_kernel, [*self_pieces, (rows, BF), (rows, BF)],
        [info, *fetch(*got), dq1, dkv_own, *fetch(dkv_got, att1), dbr1, dnorm1, dnorm2, dnorm3], vmem=10,
    )
    self_send, down_got, up_parts[1], up_parts[3] = together(self_send, down_got, up_parts[1], up_parts[3])
    self_mate = swap_dp(self_send, 1)
    down_parts = z_parts(add_low(down_keep[0], down_mate[0], down_got))
    dx0, dx1 = call(
        input_backward_kernel, [((chunk, feat), BF), ((chunk, feat), BF)],
        [info, dq1, after(dk1, self_mate), dv1, dr1, *attn_ws], [wall], 60,
    )
    self_got = swap_dp(add_low(self_keep[1], self_mate[1]), 2)
    self_got, dx0, dx1, up_parts[2], *down_parts = together(self_got, dx0, dx1, up_parts[2], *down_parts)
    ffn_back = jnp.stack([z_sum(up_parts), z_sum(down_parts)])
    self_parts = z_parts(add_low(self_keep[0], self_mate[0], self_got))
    cross_back = z_sum(after(cross_parts, self_got))
    cross_enc = to_encoder(cross_back)
    ffn_y, cross_enc, *self_parts = together(swap_dp(ffn_back, 2), cross_enc, *self_parts)
    cross_back = jnp.where(is_dec, cross_back, cross_enc)
    self_piece = z_sum(self_parts)
    self_back = self_piece[:feat]
    norms = self_piece[feat:].astype(F32).reshape(n_t, 8, PAIR).transpose(1, 0, 2).reshape(8, feat)
    other = lax.ppermute(norms, "section", [(0, 1), (1, 0)])
    ffn_two = jnp.stack([ffn_back, ffn_y])
    dx_back = [deal_back(after(dx, self_got), k) for k, dx in enumerate((dx0, dx1))]
    ffn_core = swap_dp(ffn_two, 1)

    def four(two, mate):
        return jnp.stack([two[0], mate[0], two[1], mate[1]])

    def matrix(stacked, which):
        return lax.dynamic_index_in_dim(stacked, me ^ which, 0, False).astype(F32)

    ffn_sum = four(ffn_two, ffn_core)
    ffn_true = [matrix(ffn_sum, m) for m in range(4)]
    up_grad = jnp.concatenate([f[0].T for f in ffn_true], axis=1)
    down_grad = jnp.concatenate([f[1] for f in ffn_true], axis=0)
    self_y, cross_y, other, up_grad, down_grad, *dx_back = together(
        swap_dp(self_back, 2), swap_dp(cross_back, 2), other, up_grad, down_grad, *dx_back
    )
    self_two = jnp.stack([self_back, self_y])
    cross_two = jnp.stack([cross_back, cross_y])
    self_core, cross_core = swap_dp(self_two, 1), swap_dp(cross_two, 1)
    self_sum = four(self_two, self_core)
    cross_sum = four(cross_two, cross_core)
    qkv_grad = jnp.stack([matrix(self_sum, m) for m in range(3)])
    out_grad = matrix(self_sum, 3).T
    cross_grad = jnp.stack([
        matrix(cross_sum, jnp.where(is_dec, 0, 1)), matrix(cross_sum, jnp.where(is_dec, 3, 2))
    ])

    enc = jnp.where(is_dec, other, norms)
    dec = jnp.where(is_dec, norms, other)
    full_gain = jnp.stack([enc[0:2], dec[0:2]])
    full_bias = jnp.stack([enc[2:4], dec[2:4]])

    def in_order(back):
        even = t % 2 == 0
        return jnp.stack([jnp.where(even, back[0], back[1]), jnp.where(even, back[1], back[0])])

    out_rows = in_order(out_back)
    grad_rows = in_order(dx_back).astype(F32)
    return (
        out_rows[None],
        grad_rows[None],
        qkv_grad[None],
        out_grad[None],
        cross_grad[None],
        up_grad[None],
        down_grad[None],
        full_gain,
        full_bias,
        dec[4],
        dec[5],
    )


def solution(mesh):
    return jax.shard_map(
        body,
        mesh=mesh,
        in_specs=(
            P("section", "dp", "tensor", None),
            P("section", "dp", "tensor", None),
            P(None, "dp", None),
            P("dp"),
            P("section", None, None, "tensor"),
            P("section", "tensor", None),
            P("section", None, None, "tensor"),
            P("section", None, "tensor"),
            P("section", "tensor", None),
            P(),
            P(),
            P(),
            P(),
        ),
        out_specs=(
            P("section", "dp", "tensor", None),
            P("section", "dp", "tensor", None),
            P("section", None, None, "tensor"),
            P("section", "tensor", None),
            P("section", None, None, "tensor"),
            P("section", None, "tensor"),
            P("section", "tensor", None),
            P(),
            P(),
            P(),
            P(),
        ),
        check_vma=False,
    )
```
